256 devices in a mesh: group: 4 (over y), ep: 64 (over z, x, core).
Axes of the slice: x: 4, y: 4, z: 8, core: 2. Of those that a mesh axis runs over, the one named last changes fastest.
Arguments:
- hidden_in: bfloat16 [2, 512, 7168], P(None, 'ep'), may hold values from -6 to 6
- queries: bfloat16 [2, 512, 64, 576], P(None, 'ep', 'group'), may hold values from -60 to 60
- latent_cache: bfloat16 [2, 512, 256, 576], P(None, 'ep'), may hold values from -8 to 8
- cache_lengths: int32 [2, 512], P(None, 'ep'), may hold values from 1 to 256, as said below
- expert_ids: int32 [2, 512, 8], P(None, 'ep'), may hold values from 0 to 31, all different within a row; in each aligned block of 8 rows (0 to 7, 8 to 15, ..., all dimensions but the last counted through in order) at most 4 rows name the same one
- gate_values: float32 [2, 512, 8], P(None, 'ep'), may hold values from 0.1 to 1
- norm_gain: float32 [7168], replicated, may hold values from 0.1 to 1.9
- value_up: bfloat16 [64, 512, 128], P('group'), may hold values from -0.25 to 0.25
- out_proj: bfloat16 [8192, 7168], P('group', 'ep'), may hold values from -0.0625 to 0.0625
- gate_up: bfloat16 [64, 7168, 2, 512], P('ep', 'group'), may hold values from -0.0625 to 0.0625
- down_proj: bfloat16 [64, 512, 7168], P('ep', 'group'), may hold values from -0.1875 to 0.1875
Outputs:
- layer_out: bfloat16 [2, 512, 7168], P(None, 'ep')
The draws below stay inside these ranges and needn't reach their ends.
Inputs may be any that keep to these rules, and one draw needn't show every extreme that they name: `expert_ids`: in each micro-batch no expert is named by more than 4 of the 8 rows of one ep index, a bound that some block reaches; a row names 8 different experts. `cache_lengths`: some row of every ep index holds 256 valid positions in each micro-batch.
All inputs are finite; a program needn't handle non-finite values.
Results may differ from the reference program's by a relative error of at most 0.015.
Values may be sent and summed in bfloat16 or wider, within the bound.
No kernel may reach another device: no remote copies, remote signals or barrier semaphores. Data moves between devices by JAX's collectives and lax.ppermute only.
A program may use at most 128 MiB of HBM per device.

```python
import math
import jax
import jax.numpy as jnp
import numpy as np
from jax import lax

D = 7168
EXP_UNITS = 1024
HEADS = 64
LATENT = 512
ROPE = 64
NOPE = 128
VDIM = 128
ROWS_DEV = 8
CACHE_LEN = 256
MB = 2
HALF = 512
KDIM = 576
NEXP = 32
TOPK = 8
ROWS = 512
CAP = 4
N_EP = 64


def cache_field(key):
    field = jax.random.normal(jax.random.fold_in(key, 101), (MB, ROWS, CACHE_LEN, KDIM), jnp.float32)
    return jnp.clip(field, -8.0, 8.0)


def draw_latent_cache(key, part):
    field = cache_field(key)
    return field.astype(jnp.bfloat16)


def draw_queries(key, part):
    key = jax.random.fold_in(key, 2)
    noise = jax.random.normal(key, (MB, ROWS, HEADS, KDIM), jnp.float32)
    return jnp.clip(noise, -60.0, 60.0).astype(jnp.bfloat16)


def draw_cache_lengths(key, part):
    key = jax.random.fold_in(key, 5)
    drawn = jax.random.randint(key, (MB, ROWS), 1, CACHE_LEN + 1, dtype=jnp.int32)
    leading = (jnp.arange(ROWS, dtype=jnp.int32) % ROWS_DEV == 0)[None, :]
    return jnp.where(leading, CACHE_LEN, drawn).astype(jnp.int32)


def block_scale(stream_key, shape, cuts, smallest, largest):
    def one(position, shards_of):
        steps = jax.random.uniform(jax.random.fold_in(jax.random.fold_in(stream_key, 6), position), (shards_of,), jnp.float32, smallest / len(cuts), largest / len(cuts))
        return jnp.repeat(jnp.exp(steps), shape[position] // shards_of).reshape((-1,) + (1,) * (len(shape) - position - 1))

    gain = one(*cuts[0])
    for cut in cuts[1:]:
        gain = gain * one(*cut)
    return gain


def assign_block(stream_key, own, number, rows, number_of, top, most, lean):
    ranking = jax.random.permutation(stream_key, number_of)
    crowded, ordinary = shares(number_of, rows * top, most, lean, True), shares(number_of, rows * top, most, lean, False)
    places = jnp.arange(number_of)

    def named(sizes, rotation):
        used = int((sizes > 0).sum())
        fixed = max(1, used // 4)
        shifted = fixed + (places - fixed + rotation * (used - fixed)) % max(1, number_of - fixed)
        return jnp.zeros((number_of,), jnp.int32).at[ranking[jnp.where(places < fixed, places, shifted)]].set(jnp.asarray(sizes, jnp.int32))

    sizes = jnp.where(number % 4 == 0, named(crowded, number // 4), named(ordinary, number - number // 4 - 1))
    mixed = jax.random.permutation(jax.random.fold_in(own, 3), number_of)
    donor, receiver = mixed[0:number_of // 2 * 2:2], mixed[1:number_of // 2 * 2:2]
    margin = jnp.minimum(sizes[donor] - 1, most - sizes[receiver]) // 2
    margin = jnp.where((donor == ranking[0]) | (receiver == ranking[0]) | (sizes[receiver] == 0), 0, jnp.maximum(margin, 0))
    shifted = jax.random.randint(jax.random.fold_in(own, 4), (number_of // 2,), 0, 1 << 20) % (margin + 1)
    sizes = sizes.at[donor].add(-shifted).at[receiver].add(shifted)
    items = jnp.searchsorted(jnp.cumsum(sizes), jnp.arange(rows * top), side="right").astype(jnp.int32)
    grid = items.reshape(top, rows).T
    grid = grid[jax.random.permutation(jax.random.fold_in(own, 1), rows)]
    rotation = jax.random.randint(jax.random.fold_in(own, 2), (rows, 1), 0, top)
    return jnp.take_along_axis(grid, (jnp.arange(top)[None, :] + rotation) % top, axis=1)


def shares(amount, total, limit, skew, full):
    loads = [(1 << 20) // math.isqrt(grade ** skew) + 1 for grade in range(1, amount + 1)]
    largest = limit if full else min(limit, max(-(-total // amount), total * loads[0] // sum(loads)))
    least = 1 if total - largest >= amount - 1 else 0
    counts, surplus = [largest] + [least] * (amount - 1), total - largest - least * (amount - 1)
    while surplus > 0:
        movable = [i for i in range(1, amount) if counts[i] < largest] or [i for i in range(1, amount) if counts[i] < limit]
        pool, budget = sum([loads[i] for i in movable]), surplus
        for i in movable:
            extra = min(limit - counts[i], max(1, budget * loads[i] // pool), surplus)
            counts[i] = counts[i] + extra
            surplus = surplus - extra
    return np.array(counts)


def normal_values(rng, extent, scale, reach, pieces=(), kind=jnp.bfloat16):
    result = scale * jax.random.normal(rng, extent, jnp.float32)
    if pieces:
        result = result * block_scale(rng, extent, pieces, -0.22, 0.18)
    return jnp.clip(result, -reach, reach).astype(kind)


def setup_inputs(seed: int = 0) -> dict:
    arg_keys = jax.random.split(jax.random.key(seed), 12)
    hidden_in = normal_values(arg_keys[0], (MB, ROWS, D), 1.0, 6.0, ((1, 64),))
    queries = draw_queries(jax.random.fold_in(arg_keys[11], 71), 0)
    latent_cache = draw_latent_cache(jax.random.fold_in(arg_keys[11], 71), 0)
    cache_lengths = draw_cache_lengths(jax.random.fold_in(arg_keys[11], 71), 0)
    expert_ids_keys = jax.random.split(jax.random.fold_in(arg_keys[4], 1), MB * ROWS // ROWS_DEV)
    expert_ids_turns = jax.random.permutation(jax.random.fold_in(arg_keys[4], 3), MB * ROWS // ROWS_DEV)
    expert_ids = jax.vmap(lambda own, number: assign_block(jax.random.fold_in(arg_keys[4], 2), own, number, ROWS_DEV, NEXP, TOPK, CAP, 2))(expert_ids_keys, expert_ids_turns).reshape((MB, ROWS, TOPK))
    gate_values = jnp.clip(0.1 + 0.9 * jax.random.uniform(arg_keys[5], (MB, ROWS, TOPK), jnp.float32) ** block_scale(arg_keys[5], (MB, ROWS, TOPK), ((1, 64),), -0.2, 0.2), 0.1, 1.0)
    norm_gain = jnp.clip(1.0 + 0.18 * jax.random.normal(arg_keys[6], (D,), jnp.float32), 0.1, 1.9)
    value_up = normal_values(arg_keys[7], (HEADS, LATENT, VDIM), LATENT ** -0.5, 0.25, ((0, 4),))
    out_proj = normal_values(arg_keys[8], (HEADS * VDIM, D), (HEADS * VDIM) ** -0.5, 0.0625, ((0, 4), (1, 64)))
    gate_up = normal_values(arg_keys[9], (2 * NEXP, D, 2, HALF), D ** -0.5, 0.0625, ((0, 64), (1, 4)))
    down_proj = normal_values(arg_keys[10], (2 * NEXP, HALF, D), EXP_UNITS ** -0.5, 0.1875, ((0, 64), (1, 4)))
    return dict(hidden_in=hidden_in, queries=queries, latent_cache=latent_cache, cache_lengths=cache_lengths, expert_ids=expert_ids, gate_values=gate_values, norm_gain=norm_gain, value_up=value_up, out_proj=out_proj, gate_up=gate_up, down_proj=down_proj)


def attend(queries, cache, lengths, value_up):
    row_count, head_count, key_width = queries.shape
    latent_width = value_up.shape[1]
    score_scale = 1.0 / math.sqrt(NOPE + ROPE)
    scores = jnp.einsum('rhk,rlk->rhl', queries.astype(jnp.float32), cache.astype(jnp.float32)) * score_scale
    in_range = jnp.arange(cache.shape[1], dtype=jnp.int32)[None, None, :] < lengths[:, None, None]
    masked = jnp.where(in_range, scores, -1e+30)
    peak_score = lax.optimization_barrier(jnp.max(masked, axis=2, keepdims=True))
    exponent = jnp.where(in_range, jnp.exp(masked - peak_score), 0.0)
    weights = (exponent / lax.optimization_barrier(jnp.sum(exponent, axis=2, keepdims=True))).astype(jnp.bfloat16)
    latent = jnp.einsum('rhl,rlc->rhc', weights.astype(jnp.float32), cache[:, :, :latent_width].astype(jnp.float32)).astype(jnp.bfloat16)
    head_out = jnp.einsum('rhc,hcv->rhv', latent.astype(jnp.float32), value_up.astype(jnp.float32)).astype(jnp.bfloat16)
    return head_out.reshape(row_count, head_count * value_up.shape[2])

def rms_scale(residual, norm_gain):
    mean_square = lax.optimization_barrier(jnp.mean(residual * residual, axis=1, keepdims=True))
    return (residual * lax.rsqrt(mean_square + 1e-06) * norm_gain[None, :]).astype(jnp.bfloat16)

def expert_layer(normed, expert_ids, gate_values, gate_up, down_proj):
    row_count = normed.shape[0]
    bound = N_EP * CAP

    def one_expert(carry, expert):
        chosen = expert_ids == expert
        coefficient = lax.optimization_barrier(jnp.sum(jnp.where(chosen, gate_values, 0.0), axis=1))
        routed = jnp.any(chosen, axis=1)
        index = jnp.nonzero(routed, size=bound, fill_value=0)[0].astype(jnp.int32)
        live = jnp.arange(bound, dtype=jnp.int32) < jnp.sum(routed.astype(jnp.int32))
        rows_in = normed[index]
        first_half = (expert * 2).astype(jnp.int32)
        pair = lax.dynamic_slice_in_dim(gate_up, first_half, 2, 0)
        gate_matrix = jnp.concatenate([pair[0, :, 0, :], pair[1, :, 0, :]], axis=1)
        up_matrix = jnp.concatenate([pair[0, :, 1, :], pair[1, :, 1, :]], axis=1)
        down_matrix = lax.dynamic_slice_in_dim(down_proj, first_half, 2, 0).reshape(EXP_UNITS, D)
        pre_gate = jnp.dot(rows_in, gate_matrix, preferred_element_type=jnp.float32)
        pre_up = jnp.dot(rows_in, up_matrix, preferred_element_type=jnp.float32)
        activation = (jax.nn.silu(pre_gate) * pre_up).astype(jnp.bfloat16)
        expert_part = jnp.dot(activation, down_matrix, preferred_element_type=jnp.float32)
        factor = jnp.where(live, coefficient[index], 0.0)
        return (carry.at[index].add(expert_part * factor[:, None]), None)
    final_mix, unused = lax.scan(one_expert, jnp.zeros((row_count, D), jnp.float32), jnp.arange(NEXP, dtype=jnp.int32))
    return final_mix

def reference(hidden_in, queries, latent_cache, cache_lengths, expert_ids, gate_values, norm_gain, value_up, out_proj, gate_up, down_proj):
    results = []
    for micro in range(MB):
        head_values = attend(queries[micro], latent_cache[micro], cache_lengths[micro], value_up)
        attended = jnp.dot(head_values, out_proj, preferred_element_type=jnp.float32)
        residual = hidden_in[micro].astype(jnp.float32) + attended
        normed = rms_scale(residual, norm_gain)
        expert_out = expert_layer(normed, expert_ids[micro], gate_values[micro], gate_up, down_proj)
        results.append((residual + expert_out).astype(jnp.bfloat16))
    return jnp.stack(results)
```

```python
import math

import jax
import jax.numpy as jnp
from jax import lax
from jax.sharding import Mesh
from jax.sharding import PartitionSpec as P

ROPE = 64
NOPE = 128
NY, NZ, NX, NC = 4, 8, 4, 2
BF = jnp.bfloat16
F32 = jnp.float32


def attend(queries, cache, lengths, value_up):
    row_count, head_count, key_width = queries.shape
    latent_width = value_up.shape[1]
    score_scale = 1.0 / math.sqrt(NOPE + ROPE)
    scores = (
        jnp.einsum("rhk,rlk->rhl", queries, cache, preferred_element_type=F32) * score_scale
    )
    in_range = jnp.arange(cache.shape[1], dtype=jnp.int32)[None, None, :] < lengths[:, None, None]
    masked = jnp.where(in_range, scores, -1e30)
    peak_score = jnp.max(masked, axis=2, keepdims=True)
    exponent = jnp.where(in_range, jnp.exp(masked - peak_score), 0.0)
    weights = (exponent / jnp.sum(exponent, axis=2, keepdims=True)).astype(BF)
    latent = jnp.einsum(
        "rhl,rlc->rhc", weights, cache[:, :, :latent_width], preferred_element_type=F32
    ).astype(BF)
    head_out = jnp.einsum("rhc,hcv->rhv", latent, value_up, preferred_element_type=F32).astype(BF)
    return head_out.reshape(row_count, head_count * value_up.shape[2])


def swap_core(a):
    return lax.ppermute(a, "c", [(0, 1), (1, 0)])


def shift_y(a, d):
    return lax.ppermute(a, "y", [(i, (i + d) % NY) for i in range(NY)])


def exchange_y(a, g):
    out = [lax.dynamic_index_in_dim(a, g, 0, keepdims=False)]
    for d in range(1, NY):
        out.append(shift_y(lax.dynamic_index_in_dim(a, (g + d) % NY, 0, keepdims=False), d))
    return out


def gather_y(a):
    return [a] + [shift_y(a, d) for d in range(1, NY)]


def absolute(items, g):
    back = [items[(-j) % NY] for j in range(NY)]
    return lax.dynamic_slice_in_dim(jnp.stack(back + back[: NY - 1]), (NY - g) % NY, NY, 0)


def routing(ids, gates, expert_count, capacity):
    blocks, rows, top = ids.shape
    hot = ids[..., None] == jnp.arange(expert_count, dtype=jnp.int32)
    chosen = jnp.any(hot, axis=2)
    weight = jnp.sum(jnp.where(hot, gates[..., None], 0.0), axis=2)
    counts = chosen.astype(jnp.int32)
    place = jnp.cumsum(counts, axis=1) - counts
    slot = (
        chosen[:, :, :, None]
        & (place[:, :, :, None] == jnp.arange(capacity, dtype=jnp.int32))
    )
    same = jnp.arange(blocks)[:, None] == jnp.arange(blocks)[None, :]
    pick = slot.transpose(2, 0, 3, 1)[:, :, :, None, :] & same[None, :, None, :, None]
    weights = jnp.where(pick, weight.transpose(2, 0, 1)[:, None, None, :, :], 0.0)
    flat = (expert_count * blocks * capacity, blocks * rows)
    return pick.reshape(flat).astype(BF), weights.reshape(flat)


def local(
    hidden_in,
    queries,
    latent_cache,
    cache_lengths,
    expert_ids,
    gate_values,
    norm_gain,
    value_up,
    out_proj,
    gate_up,
    down_proj,
):
    g, c = lax.axis_index("y"), lax.axis_index("c")
    first = c == 0
    micro, row_local, width = hidden_in.shape
    rows = micro * row_local
    part = rows // NY
    quarter, slim = width // NY, width // (NY * NC)
    k_dim, n_dim = out_proj.shape
    k_slice = k_dim // NX
    expert_count = NZ * NX
    top = expert_ids.shape[2]
    capacity = min(row_local, 4)

    wt = out_proj.T.reshape(n_dim, NX, k_slice).transpose(1, 0, 2)
    wx = lax.all_to_all(wt, "x", 0, 0, tiled=True)
    wy = lax.all_gather(wx.reshape(NX * n_dim, k_slice), "y", axis=0, tiled=True)
    wo = swap_core(wy)
    w0 = jnp.where(first, wy, wo).reshape(NY, NX, n_dim, k_slice)
    w1 = jnp.where(first, wo, wy).reshape(NY, NX, n_dim, k_slice)
    w_full = jnp.stack([w0, w1], axis=2).transpose(1, 2, 3, 0, 4)
    w_full = w_full.reshape(NX * NC * n_dim, NY * k_slice)

    down = lax.all_to_all(
        down_proj[0].reshape(-1, NY, quarter).transpose(1, 0, 2), "y", 0, 0, tiled=True
    )
    down = down.reshape(-1, quarter)
    gu = gate_up[0].reshape(quarter, -1)

    ids_o, gates_o = swap_core(expert_ids), swap_core(gate_values)
    ids = jnp.concatenate(
        [jnp.where(first, expert_ids, ids_o), jnp.where(first, ids_o, expert_ids)]
    )
    gates = jnp.concatenate(
        [jnp.where(first, gate_values, gates_o), jnp.where(first, gates_o, gate_values)]
    )
    pick, weights = routing(ids, gates, expert_count, capacity)

    head = attend(
        queries.reshape((rows,) + queries.shape[2:]),
        latent_cache.reshape((rows,) + latent_cache.shape[2:]),
        cache_lengths.reshape(rows),
        value_up,
    )
    mine = absolute(exchange_y(head.reshape(NY, part, k_dim), g), g)
    mine = mine.reshape(NY, part, NX, k_slice).transpose(2, 1, 0, 3)
    send = jnp.broadcast_to(
        mine.reshape(1, NX, part, NY * k_slice), (NZ, NX, part, NY * k_slice)
    ).reshape(NZ * NX, part, NY * k_slice)
    got = lax.all_to_all(send, ("z", "x"), 0, 0, tiled=True)
    spread = lax.dot_general(
        got.reshape(NZ * NX * part, NY * k_slice),
        w_full,
        (((1,), (1,)), ((), ())),
        preferred_element_type=F32,
    ).astype(BF)
    back = lax.all_to_all(
        spread.reshape(NZ * NX, part, NX * NC * n_dim), ("z", "x"), 0, 0, tiled=True
    )
    attended = jnp.sum(back.reshape(NZ, NX, part, -1).astype(F32), axis=1)
    attended = attended.transpose(1, 0, 2).reshape(part, width)
    own_hidden = lax.dynamic_slice_in_dim(hidden_in.reshape(rows, width), g * part, part, 0)
    residual = own_hidden.astype(F32) + attended
    mean_square = jnp.mean(residual * residual, axis=1, keepdims=True)
    normed = (residual * lax.rsqrt(mean_square + 1e-06) * norm_gain[None, :]).astype(BF)

    def to_quarters(a):
        a = a.reshape(part, NY, quarter).transpose(1, 0, 2)
        return absolute(exchange_y(a, g), g).reshape(rows, quarter)

    normed_q = to_quarters(normed)
    residual_q = to_quarters(residual)
    keep = jnp.where(first, normed_q[:, :slim], normed_q[:, slim:])
    give = jnp.where(first, normed_q[:, slim:], normed_q[:, :slim])
    took = swap_core(give)
    chip_rows = jnp.concatenate([jnp.where(first, keep, took), jnp.where(first, took, keep)])
    outgoing = jnp.dot(pick, chip_rows, preferred_element_type=F32).astype(BF)
    slots = NC * micro * capacity
    received = lax.all_to_all(
        outgoing.reshape(expert_count, slots, slim), ("z", "x"), 0, 0, tiled=True
    ).reshape(expert_count * slots, slim)
    other = swap_core(received)
    left, right = jnp.where(first, received, other), jnp.where(first, other, received)
    pre = (
        jnp.dot(left, gu[:slim], preferred_element_type=F32)
        + jnp.dot(right, gu[slim:], preferred_element_type=F32)
    ).astype(BF)
    units = pre.shape[1] // (2 * NY)
    pre = pre.reshape(-1, 2, NY, units).transpose(2, 0, 1, 3).reshape(NY, -1, 2 * units)
    parts = exchange_y(pre, g)
    total = sum(p.astype(F32) for p in parts)
    act = (jax.nn.silu(total[:, :units]) * total[:, units:]).astype(BF)
    act_all = absolute(gather_y(act), g)
    act_all = act_all.transpose(1, 0, 2).reshape(-1, NY * units)
    result = jnp.dot(act_all, down, preferred_element_type=F32)
    keep_r = jnp.where(first, result[:, :slim], result[:, slim:])
    give_r = jnp.where(first, result[:, slim:], result[:, :slim]).astype(BF)
    whole = (keep_r + swap_core(give_r).astype(F32)).astype(BF)
    returned = lax.all_to_all(
        whole.reshape(expert_count, slots, slim), ("z", "x"), 0, 0, tiled=True
    ).reshape(expert_count * slots, slim)
    high = weights.astype(BF)
    low = (weights - high.astype(F32)).astype(BF)
    both = lax.dot_general(
        jnp.concatenate([high, low], axis=1),
        returned,
        (((0,), (0,)), ((), ())),
        preferred_element_type=F32,
    )
    mix = both[: NC * rows] + both[NC * rows :]
    mix_keep = jnp.where(first, mix[:rows], mix[rows:])
    mix_give = jnp.where(first, mix[rows:], mix[:rows])
    mix_took = swap_core(mix_give)
    mix_q = jnp.concatenate(
        [jnp.where(first, mix_keep, mix_took), jnp.where(first, mix_took, mix_keep)], axis=1
    )
    out_q = (residual_q + mix_q).astype(BF)
    out = absolute(gather_y(out_q), g).transpose(1, 0, 2)
    return out.reshape(micro, row_local, width)


def solution(mesh):
    fine = Mesh(mesh.devices.reshape(NY, NZ, NX, NC), ("y", "z", "x", "c"))
    ep = ("z", "x", "c")
    return jax.shard_map(
        local,
        mesh=fine,
        in_specs=(
            P(None, ep, None),
            P(None, ep, "y", None),
            P(None, ep, None, None),
            P(None, ep),
            P(None, ep, None),
            P(None, ep, None),
            P(),
            P("y", None, None),
            P("y", ep),
            P(ep, "y", None, None),
            P(ep, "y", None),
        ),
        out_specs=P(None, ep, None),
        check_vma=False,
    )
```

```python
import functools
import math

import jax
import jax.numpy as jnp
from jax import lax
from jax.experimental import pallas as pl
from jax.experimental.pallas import tpu as pltpu
from jax.sharding import Mesh
from jax.sharding import PartitionSpec as P

ROPE = 64
NOPE = 128
NY, NZ, NX, NC = 4, 8, 4, 2
BF = jnp.bfloat16
F32 = jnp.float32


def attend_kernel(rows, heads, latent, info_ref, q_ref, cache_ref, up_ref, *refs):
    outs, held = refs[:NY], refs[NY]
    step = pl.program_id(0)
    scale = 1.0 / math.sqrt(ROPE + NOPE)
    base = lax.rem(step + info_ref[0], NY) * rows
    for r in range(rows):
        cache = cache_ref[r]
        scores = jnp.dot(q_ref[r], cache, preferred_element_type=F32) * scale
        at = lax.broadcasted_iota(jnp.int32, scores.shape, 1)
        in_range = at < info_ref[1 + base + r]
        masked = jnp.where(in_range, scores, -1e30)
        peak = jnp.max(masked, axis=1, keepdims=True)
        exponent = jnp.where(in_range, jnp.exp(masked - peak), 0.0)
        weights = (exponent / jnp.sum(exponent, axis=1, keepdims=True)).astype(BF)
        held[step * rows + r] = lax.dot_general(
            weights, cache[:latent], (((1,), (1,)), ((), ())), preferred_element_type=F32
        )

    @pl.when(step == NY - 1)
    def _():
        for h in range(heads):
            value = jnp.dot(
                held[:, h, :].astype(BF), up_ref[h], preferred_element_type=F32
            ).astype(BF)
            for d in range(NY):
                outs[d][:, h * up_ref.shape[2] : (h + 1) * up_ref.shape[2]] = value[
                    d * rows : (d + 1) * rows
                ]


def attend(info, queries, cache_t, value_up):
    all_rows, heads, key = queries.shape
    rows = all_rows // NY
    latent, vdim = value_up.shape[1:]
    length = cache_t.shape[2]
    turn = lambda i, info: (lax.rem(i + info[0], NY), 0, 0)
    return pl.pallas_call(
        functools.partial(attend_kernel, rows, heads, latent),
        grid_spec=pltpu.PrefetchScalarGridSpec(
            num_scalar_prefetch=1,
            grid=(NY,),
            in_specs=[
                pl.BlockSpec((rows, heads, key), turn),
                pl.BlockSpec((rows, key, length), turn),
                pl.BlockSpec(value_up.shape, lambda i, info: (0, 0, 0)),
            ],
            out_specs=[pl.BlockSpec((rows, heads * vdim), lambda i, info: (0, 0))] * NY,
            scratch_shapes=[pltpu.VMEM((all_rows, heads, latent), F32)],
        ),
        out_shape=[jax.ShapeDtypeStruct((rows, heads * vdim), BF)] * NY,
        compiler_params=pltpu.CompilerParams(vmem_limit_bytes=60 << 20),
        name="attend",
    )(info, queries, cache_t, value_up)


def project_kernel(n_dim, place_ref, h_ref, *refs):
    own, other, out_ref, w_ref, acc_ref = refs[:NY], refs[NY : 2 * NY], *refs[2 * NY :]
    depth = own[0].shape[1]
    for d in range(NY):
        for core in range(NC):

            @pl.when(place_ref[1] == core)
            def _():
                for x in range(NX):

                    @pl.when(place_ref[0] == x)
                    def _():
                        for dx in range(NX):
                            rows = slice(dx * n_dim, (dx + 1) * n_dim)
                            at = NC * ((x - dx) % NX)
                            w_ref[at + core] = own[d][rows, :]
                            w_ref[at + 1 - core] = other[d][rows, :]

        term = lax.dot_general(
            h_ref[:, d * depth : (d + 1) * depth],
            w_ref[...].reshape(NX * NC * n_dim, depth),
            (((1,), (1,)), ((), ())),
            preferred_element_type=F32,
        )
        if d == 0:
            acc_ref[...] = term
        else:
            acc_ref[...] += term
    out_ref[...] = acc_ref[...].astype(BF)


def project(place, rows_in, own, other, n_dim):
    pieces = NX * NC
    count, depth = rows_in.shape[0], own[0].shape[1]
    vmem = pl.BlockSpec(memory_space=pltpu.VMEM)
    return pl.pallas_call(
        functools.partial(project_kernel, n_dim),
        in_specs=[pl.BlockSpec(memory_space=pltpu.SMEM)] + [vmem] * (1 + 2 * NY),
        out_specs=vmem,
        out_shape=jax.ShapeDtypeStruct((count, pieces * n_dim), BF),
        scratch_shapes=[
            pltpu.VMEM((pieces, n_dim, depth), BF),
            pltpu.VMEM((count, pieces * n_dim), F32),
        ],
        compiler_params=pltpu.CompilerParams(vmem_limit_bytes=32 << 20),
        name="project",
    )(place, rows_in, *own, *other)


def fan_out_kernel(depth, *refs):
    pieces, out_ref = refs[:NY], refs[NY]
    for x in range(NX):
        chunk = jnp.concatenate([p[:, x * depth : (x + 1) * depth] for p in pieces], axis=1)
        for z in range(NZ):
            out_ref[z * NX + x] = chunk


def fan_out(pieces):
    rows, k_dim = pieces[0].shape
    vmem = pl.BlockSpec(memory_space=pltpu.VMEM)
    return pl.pallas_call(
        functools.partial(fan_out_kernel, k_dim // NX),
        in_specs=[vmem] * NY,
        out_specs=vmem,
        out_shape=jax.ShapeDtypeStruct((NZ * NX, rows, NY * k_dim // NX), BF),
        name="fan_out",
    )(*pieces)


def norm_kernel(place_ref, back_ref, hidden_ref, gain_ref, *refs):
    normed, residual, held_ref = refs[:NY], refs[NY : 2 * NY], refs[2 * NY]
    g = place_ref[0]
    rows, width = held_ref.shape
    segment = back_ref.shape[2]
    quarter = width // NY
    squares = jnp.zeros((rows, 1), F32)
    lower = lax.rem(g, 2) == 0
    for z in range(NZ):
        at = slice(z * segment, (z + 1) * segment)
        total = back_ref[z * NX].astype(F32)
        for x in range(1, NX):
            total += back_ref[z * NX + x].astype(F32)
        hidden = hidden_ref[lax.div(g, 2), :, at].astype(F32)
        total += jnp.where(lower, hidden[:rows], hidden[rows:])
        held_ref[:, at] = total
        squares += jnp.sum(total * total, axis=1, keepdims=True)
    scale = lax.rsqrt(squares / width + 1e-06)
    for d in range(NY):
        at = pl.ds(pl.multiple_of(lax.rem(g + d, NY) * quarter, quarter), quarter)
        part = held_ref[:, at]
        residual[d][...] = part
        normed[d][...] = (part * scale * gain_ref[:, at]).astype(BF)


def norm(place, back, hidden, gain):
    micro, row_local, width = hidden.shape
    rows = micro * row_local // NY
    vmem = pl.BlockSpec(memory_space=pltpu.VMEM)
    outs = [jax.ShapeDtypeStruct((rows, width // NY), t) for t in (BF,) * NY + (F32,) * NY]
    got = pl.pallas_call(
        norm_kernel,
        in_specs=[pl.BlockSpec(memory_space=pltpu.SMEM), vmem, vmem, vmem],
        out_specs=[vmem] * (2 * NY),
        out_shape=outs,
        scratch_shapes=[pltpu.VMEM((rows, width), F32)],
        name="norm",
    )(place, back, hidden, gain)
    return got[:NY], got[NY:]


def join_kernel(place_ref, *refs):
    pieces, out_ref = refs[:NY], refs[NY]
    quarter = pieces[0].shape[1]
    micro, rows = out_ref.shape[:2]
    for d in range(NY):
        at = lax.rem(place_ref[0] - d + NY, NY) * quarter
        for m in range(micro):
            out_ref[m, :, pl.ds(pl.multiple_of(at, quarter), quarter)] = pieces[d][
                m * rows : (m + 1) * rows, :
            ]


def join(place, pieces, shape):
    vmem = pl.BlockSpec(memory_space=pltpu.VMEM)
    return pl.pallas_call(
        join_kernel,
        in_specs=[pl.BlockSpec(memory_space=pltpu.SMEM)] + [vmem] * NY,
        out_specs=vmem,
        out_shape=jax.ShapeDtypeStruct(shape, BF),
        name="join",
    )(place, *pieces)


def gate_up_kernel(place_ref, x_ref, w_ref, *refs):
    del place_ref
    refs[-1][...] = jnp.dot(x_ref[...], w_ref[...], preferred_element_type=F32)


def gate_up_last_kernel(units, place_ref, x_ref, w_ref, sum_ref, *refs):
    outs, acc_ref = refs[:NY], refs[NY]
    acc_ref[...] = sum_ref[...] + jnp.dot(x_ref[...], w_ref[...], preferred_element_type=F32)
    for d in range(NY):
        to = lax.rem(place_ref[0] + d, NY)
        for k in range(2):
            start = pl.multiple_of((k * NY + to) * units, units)
            outs[d][:, k * units : (k + 1) * units] = acc_ref[:, pl.ds(start, units)].astype(BF)


def gate_up_dot(place, half, x, w, before=None):
    count, depth = x.shape
    width = w.shape[1]
    units = width // (2 * NY)
    in_specs = [
        pl.BlockSpec((count, depth), lambda i, p: (0, 0)),
        pl.BlockSpec((depth, width), lambda i, p: (lax.rem(p[1] + half, NC), 0)),
    ]
    if before is None:
        body, operands, scratch = gate_up_kernel, (x, w), []
        out_specs = pl.BlockSpec((count, width), lambda i, p: (0, 0))
        out_shape = jax.ShapeDtypeStruct((count, width), F32)
    else:
        body, operands = functools.partial(gate_up_last_kernel, units), (x, w, before)
        scratch = [pltpu.VMEM((count, width), F32)]
        in_specs.append(pl.BlockSpec((count, width), lambda i, p: (0, 0)))
        out_specs = [pl.BlockSpec((count, 2 * units), lambda i, p: (0, 0))] * NY
        out_shape = [jax.ShapeDtypeStruct((count, 2 * units), BF)] * NY
    return pl.pallas_call(
        body,
        grid_spec=pltpu.PrefetchScalarGridSpec(
            num_scalar_prefetch=1,
            grid=(1,),
            in_specs=in_specs,
            out_specs=out_specs,
            scratch_shapes=scratch,
        ),
        out_shape=out_shape,
        compiler_params=pltpu.CompilerParams(vmem_limit_bytes=32 << 20),
        cost_estimate=pl.CostEstimate(
            flops=2 * count * depth * width, bytes_accessed=6 << 20, transcendentals=0
        ),
        name="gate_up",
    )(place, *operands)


def down_kernel(place_ref, *refs):
    del place_ref
    acts, downs, out_ref = refs[:NY], refs[NY : 2 * NY], refs[2 * NY]
    act = jnp.concatenate([a[...] for a in acts], axis=1)
    down = jnp.concatenate([w[...] for w in downs], axis=0)
    out_ref[...] = jnp.dot(act, down, preferred_element_type=F32).astype(out_ref.dtype)


def down_dot(place, half, acts, downs, dtype):
    count, units = acts[0].shape
    width = downs[0].shape[1] // NC
    return pl.pallas_call(
        down_kernel,
        grid_spec=pltpu.PrefetchScalarGridSpec(
            num_scalar_prefetch=1,
            grid=(1,),
            in_specs=[pl.BlockSpec((count, units), lambda i, p: (0, 0))] * NY
            + [pl.BlockSpec((units, width), lambda i, p: (0, lax.rem(p[1] + half, NC)))] * NY,
            out_specs=pl.BlockSpec((count, width), lambda i, p: (0, 0)),
        ),
        out_shape=jax.ShapeDtypeStruct((count, width), dtype),
        compiler_params=pltpu.CompilerParams(vmem_limit_bytes=32 << 20),
        cost_estimate=pl.CostEstimate(
            flops=2 * count * units * NY * width, bytes_accessed=3 << 20, transcendentals=0
        ),
        name="down",
    )(place, *acts, *downs)


def swap_core(a):
    return lax.ppermute(a, "c", [(0, 1), (1, 0)])


def shift_y(a, d):
    return lax.ppermute(a, "y", [(i, (i + d) % NY) for i in range(NY)])


def shift_x(a, d):
    return lax.ppermute(a, "x", [(i, (i + d) % NX) for i in range(NX)])


def lane_part(a, index, size):
    return lax.dynamic_slice_in_dim(a, index * size, size, 1)


def gather_y(a):
    return [a] + [shift_y(a, d) for d in range(1, NY)]


def absolute(items, g):
    back = [items[(-j) % NY] for j in range(NY)]
    return lax.dynamic_slice_in_dim(jnp.stack(back + back[: NY - 1]), (NY - g) % NY, NY, 0)


def routing(ids, gates, expert_count, capacity, g):
    blocks, rows, top = ids.shape
    hot = ids[..., None] == jnp.arange(expert_count, dtype=jnp.int32)
    chosen = jnp.any(hot, axis=2)
    weight = jnp.sum(jnp.where(hot, gates[..., None], 0.0), axis=2)
    counts = chosen.astype(jnp.int32)
    place = jnp.cumsum(counts, axis=1) - counts
    block = jnp.broadcast_to(jnp.arange(blocks, dtype=jnp.int32)[:, None, None], place.shape)
    slot = jnp.where(chosen, block * capacity + place, -1).reshape(blocks * rows, expert_count)
    slots = jnp.arange(blocks * capacity, dtype=jnp.int32)[None, :, None]
    flat = (expert_count * blocks * capacity, blocks * rows)
    weight = weight.reshape(blocks * rows, expert_count).T[:, None, :]
    weights = jnp.where(slot.T[:, None, :] == slots, weight, 0.0).reshape(flat)
    turned = slot.reshape(NC, NY, -1)
    turned = jnp.stack(
        [lax.dynamic_index_in_dim(turned, (g - d) % NY, 1, keepdims=False) for d in range(NY)],
        axis=1,
    )
    turned = turned.reshape(blocks * rows, expert_count)
    pick = (turned.T[:, None, :] == slots).reshape(flat).astype(BF)
    return pick, weights


def local(
    hidden_in,
    queries,
    latent_cache,
    cache_lengths,
    expert_ids,
    gate_values,
    norm_gain,
    value_up,
    out_proj,
    gate_up,
    down_proj,
):
    g, c = lax.axis_index("y"), lax.axis_index("c")
    first = c == 0
    micro, row_local, width = hidden_in.shape
    rows = micro * row_local
    part = rows // NY
    quarter, slim = width // NY, width // (NY * NC)
    k_dim, n_dim = out_proj.shape
    k_slice = k_dim // NX
    expert_count = NZ * NX
    top = expert_ids.shape[2]
    capacity = min(row_local, 4)

    x = lax.axis_index("x")
    place = jnp.stack([g, c, x]).astype(jnp.int32)
    wt = out_proj.T
    wx = [lane_part(wt, x, k_slice)]
    wx += [shift_x(lane_part(wt, (x + d) % NX, k_slice), d) for d in range(1, NX)]
    wx = jnp.concatenate(wx)
    info = jnp.concatenate([g.astype(jnp.int32)[None], cache_lengths.reshape(rows)])
    wx, info = lax.optimization_barrier((wx, info))
    w_own = gather_y(wx)

    ids_o, gates_o = swap_core(expert_ids), swap_core(gate_values)
    ids = jnp.concatenate(
        [jnp.where(first, expert_ids, ids_o), jnp.where(first, ids_o, expert_ids)]
    )
    gates = jnp.concatenate(
        [jnp.where(first, gate_values, gates_o), jnp.where(first, gates_o, gate_values)]
    )
    pick, weights = routing(ids, gates, expert_count, capacity, g)

    head = attend(
        info,
        queries.reshape((rows,) + queries.shape[2:]),
        latent_cache.transpose(0, 1, 3, 2).reshape((rows,) + latent_cache.shape[:1:-1]),
        value_up,
    )
    send = fan_out([head[0]] + [shift_y(head[d], d) for d in range(1, NY)])
    send, w_own[1], w_own[3] = lax.optimization_barrier((send, w_own[1], w_own[3]))
    w_other = [swap_core(w) for w in w_own]
    gate_up, send = lax.optimization_barrier((gate_up, send))
    gu = gate_up[0].reshape(quarter, -1)
    got = lax.all_to_all(send, ("z", "x"), 0, 0, tiled=True)
    got, gu = lax.optimization_barrier((got, gu))
    spread = project(
        jnp.stack([x, c]).astype(jnp.int32),
        got.reshape(NZ * NX * part, NY * k_slice),
        w_own,
        w_other,
        n_dim,
    )
    back = lax.all_to_all(
        spread.reshape(NZ * NX, part, NX * NC * n_dim), ("z", "x"), 0, 0, tiled=True
    )
    normed, residual = norm(place, back, hidden_in, norm_gain[None, :])
    normed_q = jnp.concatenate([normed[0]] + [shift_y(normed[d], d) for d in range(1, NY)])
    keep = jnp.where(first, normed_q[:, :slim], normed_q[:, slim:])
    give = jnp.where(first, normed_q[:, slim:], normed_q[:, :slim])
    took = swap_core(give)
    chip_rows = jnp.concatenate([jnp.where(first, keep, took), jnp.where(first, took, keep)])
    outgoing = jnp.dot(pick, chip_rows, preferred_element_type=F32).astype(BF)
    slots = NC * micro * capacity
    down_in, outgoing, *residual = lax.optimization_barrier((down_proj[0], outgoing, *residual))
    down = [lane_part(down_in, g, quarter)]
    down += [shift_y(lane_part(down_in, (g + d) % NY, quarter), d) for d in range(1, NY)]
    received = lax.all_to_all(
        outgoing.reshape(expert_count, slots, slim), ("z", "x"), 0, 0, tiled=True
    ).reshape(expert_count * slots, slim)
    residual = [residual[0]] + [shift_y(residual[d], d) for d in range(1, NY)]
    residual_q = absolute(residual, g).reshape(rows, quarter)
    received, residual_q, *down = lax.optimization_barrier((received, residual_q, *down))
    other = swap_core(received)
    own_sum = gate_up_dot(place, 0, received, gu)
    parts = gate_up_dot(place, 1, other, gu, own_sum)
    parts = [parts[0]] + [shift_y(parts[d], d) for d in range(1, NY)]
    total = sum(p.astype(F32) for p in parts)
    units = total.shape[1] // 2
    act = (jax.nn.silu(total[:, :units]) * total[:, units:]).astype(BF)
    acts = gather_y(act)
    give_r = down_dot(place, 1, acts, down, BF)
    keep_r = down_dot(place, 0, acts, down, F32)
    whole = (keep_r + swap_core(give_r).astype(F32)).astype(BF)
    returned = lax.all_to_all(
        whole.reshape(expert_count, slots, slim), ("z", "x"), 0, 0, tiled=True
    ).reshape(expert_count * slots, slim)
    high = weights.astype(BF)
    low = (weights - high.astype(F32)).astype(BF)
    both = lax.dot_general(
        jnp.concatenate([high, low], axis=1),
        returned,
        (((0,), (0,)), ((), ())),
        preferred_element_type=F32,
    )
    mix = both[: NC * rows] + both[NC * rows :]
    mix_keep = jnp.where(first, mix[:rows], mix[rows:])
    mix_give = jnp.where(first, mix[rows:], mix[:rows])
    mix_took = swap_core(mix_give)
    mix_q = jnp.concatenate(
        [jnp.where(first, mix_keep, mix_took), jnp.where(first, mix_took, mix_keep)], axis=1
    )
    out_q = (residual_q + mix_q).astype(BF)
    return join(place, gather_y(out_q), hidden_in.shape)


def solution(mesh):
    fine = Mesh(mesh.devices.reshape(NY, NZ, NX, NC), ("y", "z", "x", "c"))
    ep = ("z", "x", "c")
    return jax.shard_map(
        local,
        mesh=fine,
        in_specs=(
            P(None, ep, None),
            P(None, ep, "y", None),
            P(None, ep, None, None),
            P(None, ep),
            P(None, ep, None),
            P(None, ep, None),
            P(),
            P("y", None, None),
            P("y", ep),
            P(ep, "y", None, None),
            P(ep, "y", None),
        ),
        out_specs=P(None, ep, None),
        check_vma=False,
    )
```

```python
import functools
import math

import jax
import jax.numpy as jnp
from jax import lax
from jax.experimental import pallas as pl
from jax.experimental.pallas import tpu as pltpu
from jax.sharding import Mesh
from jax.sharding import PartitionSpec as P

ROPE = 64
NOPE = 128
NY, NZ, NX, NC = 4, 8, 4, 2
BF = jnp.bfloat16
F32 = jnp.float32
LANES = 128


def attend_kernel(rows, heads, latent, info_ref, q_ref, cache_ref, up_ref, *refs):
    outs, held = refs[:NY], refs[NY]
    step = pl.program_id(0)
    scale = 1.0 / math.sqrt(ROPE + NOPE)
    base = lax.rem(step + info_ref[0], NY) * rows
    for r in range(rows):
        cache = cache_ref[r]
        scores = jnp.dot(q_ref[r], cache, preferred_element_type=F32) * scale
        at = lax.broadcasted_iota(jnp.int32, scores.shape, 1)
        in_range = at < info_ref[1 + base + r]
        masked = jnp.where(in_range, scores, -1e30)
        peak = jnp.max(masked, axis=1, keepdims=True)
        exponent = jnp.where(in_range, jnp.exp(masked - peak), 0.0)
        weights = (exponent / jnp.sum(exponent, axis=1, keepdims=True)).astype(BF)
        held[step * rows + r] = lax.dot_general(
            weights, cache[:latent], (((1,), (1,)), ((), ())), preferred_element_type=F32
        )

    @pl.when(step == NY - 1)
    def _():
        for h in range(heads):
            value = jnp.dot(
                held[:, h, :].astype(BF), up_ref[h], preferred_element_type=F32
            ).astype(BF)
            for d in range(NY):
                outs[d][:, h * up_ref.shape[2] : (h + 1) * up_ref.shape[2]] = value[
                    d * rows : (d + 1) * rows
                ]


def attend(info, queries, cache_t, value_up):
    all_rows, heads, key = queries.shape
    rows = all_rows // NY
    latent, vdim = value_up.shape[1:]
    length = cache_t.shape[2]
    turn = lambda i, info: (lax.rem(i + info[0], NY), 0, 0)
    return pl.pallas_call(
        functools.partial(attend_kernel, rows, heads, latent),
        grid_spec=pltpu.PrefetchScalarGridSpec(
            num_scalar_prefetch=1,
            grid=(NY,),
            in_specs=[
                pl.BlockSpec((rows, heads, key), turn),
                pl.BlockSpec((rows, key, length), turn),
                pl.BlockSpec(value_up.shape, lambda i, info: (0, 0, 0)),
            ],
            out_specs=[pl.BlockSpec((rows, heads * vdim), lambda i, info: (0, 0))] * NY,
            scratch_shapes=[pltpu.VMEM((all_rows, heads, latent), F32)],
        ),
        out_shape=[jax.ShapeDtypeStruct((rows, heads * vdim), BF)] * NY,
        compiler_params=pltpu.CompilerParams(vmem_limit_bytes=60 << 20),
        name="attend",
    )(info, queries, cache_t, value_up)


def project_kernel(n_dim, place_ref, h_ref, *refs):
    own, other, out_ref, w_ref, acc_ref = refs[:NX], refs[NX : 2 * NX], *refs[2 * NX :]
    depth = own[0].shape[1]
    for d in range(NY):
        for core in range(NC):

            @pl.when(place_ref[1] == core)
            def _():
                for x in range(NX):

                    @pl.when(place_ref[0] == x)
                    def _():
                        rows = slice(d * n_dim, (d + 1) * n_dim)
                        for dx in range(NX):
                            at = NC * ((x - dx) % NX)
                            w_ref[at + core] = own[dx][rows, :]
                            w_ref[at + 1 - core] = other[dx][rows, :]

        term = lax.dot_general(
            h_ref[:, d * depth : (d + 1) * depth],
            w_ref[...].reshape(NX * NC * n_dim, depth),
            (((1,), (1,)), ((), ())),
            preferred_element_type=F32,
        )
        if d == 0:
            acc_ref[...] = term
        else:
            acc_ref[...] += term
    out_ref[...] = acc_ref[...].astype(BF)


def project(place, rows_in, own, other, n_dim):
    pieces = NX * NC
    count, depth = rows_in.shape[0], own[0].shape[1]
    vmem = pl.BlockSpec(memory_space=pltpu.VMEM)
    return pl.pallas_call(
        functools.partial(project_kernel, n_dim),
        in_specs=[pl.BlockSpec(memory_space=pltpu.SMEM)] + [vmem] * (1 + 2 * NX),
        out_specs=vmem,
        out_shape=jax.ShapeDtypeStruct((count, pieces * n_dim), BF),
        scratch_shapes=[
            pltpu.VMEM((pieces, n_dim, depth), BF),
            pltpu.VMEM((count, pieces * n_dim), F32),
        ],
        compiler_params=pltpu.CompilerParams(vmem_limit_bytes=32 << 20),
        name="project",
    )(place, rows_in, *own, *other)


def fan_out_kernel(depth, *refs):
    pieces, out_ref = refs[:NY], refs[NY]
    for x in range(NX):
        chunk = jnp.concatenate([p[:, x * depth : (x + 1) * depth] for p in pieces], axis=1)
        for z in range(NZ):
            out_ref[z * NX + x] = chunk


def fan_out(pieces):
    rows, k_dim = pieces[0].shape
    vmem = pl.BlockSpec(memory_space=pltpu.VMEM)
    return pl.pallas_call(
        functools.partial(fan_out_kernel, k_dim // NX),
        in_specs=[vmem] * NY,
        out_specs=vmem,
        out_shape=jax.ShapeDtypeStruct((NZ * NX, rows, NY * k_dim // NX), BF),
        name="fan_out",
    )(*pieces)


def norm_kernel(place_ref, back_ref, hidden_ref, *refs):
    outs, held_ref = refs[:NY], refs[NY]
    g = place_ref[0]
    rows, width = held_ref.shape
    segment = back_ref.shape[2]
    quarter = width // NY
    squares = jnp.zeros((rows, 1), F32)
    lower = lax.rem(g, 2) == 0
    for z in range(NZ):
        at = slice(z * segment, (z + 1) * segment)
        total = back_ref[z * NX].astype(F32)
        for x in range(1, NX):
            total += back_ref[z * NX + x].astype(F32)
        hidden = hidden_ref[lax.div(g, 2), :, at].astype(F32)
        total += jnp.where(lower, hidden[:rows], hidden[rows:])
        held_ref[:, at] = total
        squares += jnp.sum(total * total, axis=1, keepdims=True)
    scale = lax.rsqrt(squares / width + 1e-06)
    for d in range(NY):
        at = pl.ds(pl.multiple_of(lax.rem(g + d, NY) * quarter, quarter), quarter)
        outs[d][:, :quarter] = held_ref[:, at]
        outs[d][:, quarter:] = jnp.broadcast_to(scale, (rows, LANES))


def norm(place, back, hidden):
    micro, row_local, width = hidden.shape
    rows = micro * row_local // NY
    vmem = pl.BlockSpec(memory_space=pltpu.VMEM)
    return pl.pallas_call(
        norm_kernel,
        in_specs=[pl.BlockSpec(memory_space=pltpu.SMEM), vmem, vmem],
        out_specs=[vmem] * NY,
        out_shape=[jax.ShapeDtypeStruct((rows, width // NY + LANES), F32)] * NY,
        scratch_shapes=[pltpu.VMEM((rows, width), F32)],
        name="norm",
    )(place, back, hidden)


def scale_kernel(place_ref, gain_ref, *refs):
    pieces, outs = refs[:NY], refs[NY:]
    slim = outs[0].shape[1]
    quarter = NC * slim
    for k in range(NC):
        start = lax.rem(place_ref[1] + k, NC) * slim
        gain = gain_ref[:, pl.ds(pl.multiple_of(place_ref[0] * quarter + start, LANES), slim)]
        at = pl.ds(pl.multiple_of(start, LANES), slim)
        rows = [p[:, at] * p[:, quarter : quarter + 1] * gain for p in pieces]
        outs[k][...] = jnp.concatenate(rows).astype(BF)


def scale_rows(place, gain, pieces):
    rows = NY * pieces[0].shape[0]
    slim = gain.shape[1] // (NY * NC)
    vmem = pl.BlockSpec(memory_space=pltpu.VMEM)
    return pl.pallas_call(
        scale_kernel,
        in_specs=[pl.BlockSpec(memory_space=pltpu.SMEM)] + [vmem] * (1 + NY),
        out_specs=[vmem] * NC,
        out_shape=[jax.ShapeDtypeStruct((rows, slim), BF)] * NC,
        name="scale_rows",
    )(place, gain, *pieces)


def join_kernel(place_ref, *refs):
    pieces, out_ref = refs[:NY], refs[NY]
    quarter = pieces[0].shape[1]
    micro, rows = out_ref.shape[:2]
    for d in range(NY):
        at = lax.rem(place_ref[0] - d + NY, NY) * quarter
        for m in range(micro):
            out_ref[m, :, pl.ds(pl.multiple_of(at, quarter), quarter)] = pieces[d][
                m * rows : (m + 1) * rows, :
            ]


def join(place, pieces, shape):
    vmem = pl.BlockSpec(memory_space=pltpu.VMEM)
    return pl.pallas_call(
        join_kernel,
        in_specs=[pl.BlockSpec(memory_space=pltpu.SMEM)] + [vmem] * NY,
        out_specs=vmem,
        out_shape=jax.ShapeDtypeStruct(shape, BF),
        name="join",
    )(place, *pieces)


def gate_up_kernel(place_ref, x_ref, w_ref, *refs):
    del place_ref
    refs[-1][...] = jnp.dot(x_ref[...], w_ref[...], preferred_element_type=F32)


def gate_up_last_kernel(units, place_ref, x_ref, w_ref, sum_ref, *refs):
    outs, acc_ref = refs[:NY], refs[NY]
    acc_ref[...] = sum_ref[...] + jnp.dot(x_ref[...], w_ref[...], preferred_element_type=F32)
    for d in range(NY):
        to = lax.rem(place_ref[0] + d, NY)
        for k in range(2):
            start = pl.multiple_of((k * NY + to) * units, units)
            outs[d][:, k * units : (k + 1) * units] = acc_ref[:, pl.ds(start, units)].astype(BF)


def gate_up_dot(place, half, x, w, before=None):
    count, depth = x.shape
    width = w.shape[1]
    units = width // (2 * NY)
    in_specs = [
        pl.BlockSpec((count, depth), lambda i, p: (0, 0)),
        pl.BlockSpec((depth, width), lambda i, p: (lax.rem(p[1] + half, NC), 0)),
    ]
    if before is None:
        body, operands, scratch = gate_up_kernel, (x, w), []
        out_specs = pl.BlockSpec((count, width), lambda i, p: (0, 0))
        out_shape = jax.ShapeDtypeStruct((count, width), F32)
    else:
        body, operands = functools.partial(gate_up_last_kernel, units), (x, w, before)
        scratch = [pltpu.VMEM((count, width), F32)]
        in_specs.append(pl.BlockSpec((count, width), lambda i, p: (0, 0)))
        out_specs = [pl.BlockSpec((count, 2 * units), lambda i, p: (0, 0))] * NY
        out_shape = [jax.ShapeDtypeStruct((count, 2 * units), BF)] * NY
    return pl.pallas_call(
        body,
        grid_spec=pltpu.PrefetchScalarGridSpec(
            num_scalar_prefetch=1,
            grid=(1,),
            in_specs=in_specs,
            out_specs=out_specs,
            scratch_shapes=scratch,
        ),
        out_shape=out_shape,
        compiler_params=pltpu.CompilerParams(vmem_limit_bytes=60 << 20),
        cost_estimate=pl.CostEstimate(
            flops=2 * count * depth * width, bytes_accessed=6 << 20, transcendentals=0
        ),
        name="gate_up",
    )(place, *operands)


def down_kernel(place_ref, *refs):
    del place_ref
    acts, downs, out_ref = refs[:NY], refs[NY : 2 * NY], refs[2 * NY]
    act = jnp.concatenate([a[...] for a in acts], axis=1)
    down = jnp.concatenate([w[...] for w in downs], axis=0)
    out_ref[...] = jnp.dot(act, down, preferred_element_type=F32).astype(out_ref.dtype)


def down_dot(place, half, acts, downs, dtype):
    count, units = acts[0].shape
    width = downs[0].shape[1] // NC
    return pl.pallas_call(
        down_kernel,
        grid_spec=pltpu.PrefetchScalarGridSpec(
            num_scalar_prefetch=1,
            grid=(1,),
            in_specs=[pl.BlockSpec((count, units), lambda i, p: (0, 0))] * NY
            + [pl.BlockSpec((units, width), lambda i, p: (0, lax.rem(p[1] + half, NC)))] * NY,
            out_specs=pl.BlockSpec((count, width), lambda i, p: (0, 0)),
        ),
        out_shape=jax.ShapeDtypeStruct((count, width), dtype),
        compiler_params=pltpu.CompilerParams(vmem_limit_bytes=32 << 20),
        cost_estimate=pl.CostEstimate(
            flops=2 * count * units * NY * width, bytes_accessed=3 << 20, transcendentals=0
        ),
        name="down",
    )(place, *acts, *downs)


def swap_core(a):
    return lax.ppermute(a, "c", [(0, 1), (1, 0)])


def shift_y(a, d):
    return lax.ppermute(a, "y", [(i, (i + d) % NY) for i in range(NY)])


def shift_x(a, d):
    return lax.ppermute(a, "x", [(i, (i + d) % NX) for i in range(NX)])


def lane_part(a, index, size):
    return lax.dynamic_slice_in_dim(a, index * size, size, 1)


def gather_y(a):
    return [a] + [shift_y(a, d) for d in range(1, NY)]


def absolute(items, g):
    back = [items[(-j) % NY] for j in range(NY)]
    return lax.dynamic_slice_in_dim(jnp.stack(back + back[: NY - 1]), (NY - g) % NY, NY, 0)


def routing(ids, gates, expert_count, capacity, g):
    blocks, rows, top = ids.shape
    hot = ids[..., None] == jnp.arange(expert_count, dtype=jnp.int32)
    chosen = jnp.any(hot, axis=2)
    weight = jnp.sum(jnp.where(hot, gates[..., None], 0.0), axis=2)
    counts = chosen.astype(jnp.int32)
    place = jnp.cumsum(counts, axis=1) - counts
    block = jnp.broadcast_to(jnp.arange(blocks, dtype=jnp.int32)[:, None, None], place.shape)
    slot = jnp.where(chosen, block * capacity + place, -1).reshape(blocks * rows, expert_count)
    slots = jnp.arange(blocks * capacity, dtype=jnp.int32)[None, :, None]
    flat = (expert_count * blocks * capacity, blocks * rows)
    weight = weight.reshape(blocks * rows, expert_count).T[:, None, :]
    weights = jnp.where(slot.T[:, None, :] == slots, weight, 0.0).reshape(flat)
    turned = slot.reshape(NC, NY, -1)
    turned = jnp.stack(
        [lax.dynamic_index_in_dim(turned, (g - d) % NY, 1, keepdims=False) for d in range(NY)],
        axis=1,
    )
    turned = turned.reshape(blocks * rows, expert_count)
    pick = (turned.T[:, None, :] == slots).reshape(flat).astype(BF)
    return pick, weights


def local(
    hidden_in,
    queries,
    latent_cache,
    cache_lengths,
    expert_ids,
    gate_values,
    norm_gain,
    value_up,
    out_proj,
    gate_up,
    down_proj,
):
    g, c = lax.axis_index("y"), lax.axis_index("c")
    first = c == 0
    micro, row_local, width = hidden_in.shape
    rows = micro * row_local
    part = rows // NY
    quarter, slim = width // NY, width // (NY * NC)
    k_dim, n_dim = out_proj.shape
    k_slice = k_dim // NX
    expert_count = NZ * NX
    top = expert_ids.shape[2]
    capacity = min(row_local, 4)

    x = lax.axis_index("x")
    place = jnp.stack([g, c, x]).astype(jnp.int32)
    wy = gather_y(out_proj.T)
    info = jnp.concatenate([g.astype(jnp.int32)[None], cache_lengths.reshape(rows)])

    ids_o, gates_o = swap_core(expert_ids), swap_core(gate_values)
    ids = jnp.concatenate(
        [jnp.where(first, expert_ids, ids_o), jnp.where(first, ids_o, expert_ids)]
    )
    gates = jnp.concatenate(
        [jnp.where(first, gate_values, gates_o), jnp.where(first, gates_o, gate_values)]
    )
    pick, weights = routing(ids, gates, expert_count, capacity, g)

    head = attend(
        info,
        queries.reshape((rows,) + queries.shape[2:]),
        latent_cache.transpose(0, 1, 3, 2).reshape((rows,) + latent_cache.shape[:1:-1]),
        value_up,
    )
    *head, wy[1], wy[2], wy[3] = lax.optimization_barrier((*head, wy[1], wy[2], wy[3]))
    send = fan_out([head[0]] + [shift_y(head[d], d) for d in range(1, NY)])
    w_own = [jnp.concatenate([lane_part(w, (x + d) % NX, k_slice) for w in wy]) for d in range(NX)]
    w_own = [w_own[0]] + [shift_x(w_own[d], d) for d in range(1, NX)]
    w_other = [swap_core(w) for w in w_own]
    down = [None] * NY

    def send_down(d, source):
        return shift_y(lane_part(source, (g + d) % NY, quarter), d)

    down_in, gate_up, send = lax.optimization_barrier((down_proj[0], gate_up, send))
    down[1] = send_down(1, down_in)
    gu = gate_up[0].reshape(quarter, -1)
    got = lax.all_to_all(send, ("z", "x"), 0, 0, tiled=True)
    got, gu, down[1] = lax.optimization_barrier((got, gu, down[1]))
    spread = project(
        jnp.stack([x, c]).astype(jnp.int32),
        got.reshape(NZ * NX * part, NY * k_slice),
        w_own,
        w_other,
        n_dim,
    )
    down_in, spread = lax.optimization_barrier((down_proj[0], spread))
    down[3] = send_down(3, down_in)
    back = lax.all_to_all(
        spread.reshape(NZ * NX, part, NX * NC * n_dim), ("z", "x"), 0, 0, tiled=True
    )
    back, down[3] = lax.optimization_barrier((back, down[3]))
    pieces = norm(place, back, hidden_in)
    pieces = [pieces[0]] + [shift_y(pieces[d], d) for d in range(1, NY)]
    keep, give = scale_rows(place, norm_gain[None, :], pieces)
    took = swap_core(give)
    chip_rows = jnp.concatenate([jnp.where(first, keep, took), jnp.where(first, took, keep)])
    outgoing = jnp.dot(pick, chip_rows, preferred_element_type=F32).astype(BF)
    slots = NC * micro * capacity
    down_in, outgoing = lax.optimization_barrier((down_proj[0], outgoing))
    down[0] = lane_part(down_in, g, quarter)
    down[2] = send_down(2, down_in)
    received = lax.all_to_all(
        outgoing.reshape(expert_count, slots, slim), ("z", "x"), 0, 0, tiled=True
    ).reshape(expert_count * slots, slim)
    received, down[0], down[2] = lax.optimization_barrier((received, down[0], down[2]))
    other = swap_core(received)
    own_sum = gate_up_dot(place, 0, received, gu)
    parts = gate_up_dot(place, 1, other, gu, own_sum)
    parts = [parts[0]] + [shift_y(parts[d], d) for d in range(1, NY)]
    total = sum(p.astype(F32) for p in parts)
    units = total.shape[1] // 2
    act = (jax.nn.silu(total[:, :units]) * total[:, units:]).astype(BF)
    acts = gather_y(act)
    give_r = down_dot(place, 1, acts, down, BF)
    keep_r = down_dot(place, 0, acts, down, F32)
    whole = (keep_r + swap_core(give_r).astype(F32)).astype(BF)
    returned = lax.all_to_all(
        whole.reshape(expert_count, slots, slim), ("z", "x"), 0, 0, tiled=True
    ).reshape(expert_count * slots, slim)
    high = weights.astype(BF)
    low = (weights - high.astype(F32)).astype(BF)
    both = lax.dot_general(
        jnp.concatenate([high, low], axis=1),
        returned,
        (((0,), (0,)), ((), ())),
        preferred_element_type=F32,
    )
    mix = both[: NC * rows] + both[NC * rows :]
    mix_keep = jnp.where(first, mix[:rows], mix[rows:])
    mix_give = jnp.where(first, mix[rows:], mix[:rows])
    mix_took = swap_core(mix_give)
    mix_q = jnp.concatenate(
        [jnp.where(first, mix_keep, mix_took), jnp.where(first, mix_took, mix_keep)], axis=1
    )
    residual_q = absolute([p[:, :quarter] for p in pieces], g).reshape(rows, quarter)
    out_q = (residual_q + mix_q).astype(BF)
    return join(place, gather_y(out_q), hidden_in.shape)


def solution(mesh):
    fine = Mesh(mesh.devices.reshape(NY, NZ, NX, NC), ("y", "z", "x", "c"))
    ep = ("z", "x", "c")
    return jax.shard_map(
        local,
        mesh=fine,
        in_specs=(
            P(None, ep, None),
            P(None, ep, "y", None),
            P(None, ep, None, None),
            P(None, ep),
            P(None, ep, None),
            P(None, ep, None),
            P(),
            P("y", None, None),
            P("y", ep),
            P(ep, "y", None, None),
            P(ep, "y", None),
        ),
        out_specs=P(None, ep, None),
        check_vma=False,
    )
```

```python
import functools
import math

import jax
import jax.numpy as jnp
from jax import lax
from jax.experimental import pallas as pl
from jax.experimental.pallas import tpu as pltpu
from jax.sharding import Mesh
from jax.sharding import PartitionSpec as P

ROPE = 64
NOPE = 128
NY, NZ, NX, NC = 4, 8, 4, 2
BF = jnp.bfloat16
F32 = jnp.float32
LANES = 128


def attend_kernel(rows, heads, latent, info_ref, q_ref, cache_ref, up_ref, out_ref, held):
    step = pl.program_id(0)
    scale = 1.0 / math.sqrt(ROPE + NOPE)
    base = lax.rem(step + info_ref[0], NY) * rows
    for r in range(rows):
        cache = cache_ref[r]
        scores = jnp.dot(q_ref[r], cache, preferred_element_type=F32) * scale
        at = lax.broadcasted_iota(jnp.int32, scores.shape, 1)
        in_range = at < info_ref[1 + base + r]
        masked = jnp.where(in_range, scores, -1e30)
        peak = jnp.max(masked, axis=1, keepdims=True)
        exponent = jnp.where(in_range, jnp.exp(masked - peak), 0.0)
        weights = (exponent / jnp.sum(exponent, axis=1, keepdims=True)).astype(BF)
        held[step * rows + r] = lax.dot_general(
            weights, cache[:latent], (((1,), (1,)), ((), ())), preferred_element_type=F32
        )

    @pl.when(step == NY - 1)
    def _():
        group, vdim = heads // NX, up_ref.shape[2]
        for h in range(heads):
            value = jnp.dot(
                held[:, h, :].astype(BF), up_ref[h], preferred_element_type=F32
            ).astype(BF)
            lanes = slice(h % group * vdim, (h % group + 1) * vdim)
            for z in range(NZ):
                out_ref[z * NX + h // group, :, lanes] = value


def attend(info, queries, cache_t, value_up):
    all_rows, heads, key = queries.shape
    rows = all_rows // NY
    latent, vdim = value_up.shape[1:]
    length = cache_t.shape[2]
    shape = (NZ * NX, all_rows, heads * vdim // NX)
    turn = lambda i, info: (lax.rem(i + info[0], NY), 0, 0)
    return pl.pallas_call(
        functools.partial(attend_kernel, rows, heads, latent),
        grid_spec=pltpu.PrefetchScalarGridSpec(
            num_scalar_prefetch=1,
            grid=(NY,),
            in_specs=[
                pl.BlockSpec((rows, heads, key), turn),
                pl.BlockSpec((rows, key, length), turn),
                pl.BlockSpec(value_up.shape, lambda i, info: (0, 0, 0)),
            ],
            out_specs=pl.BlockSpec(shape, lambda i, info: (0, 0, 0)),
            scratch_shapes=[pltpu.VMEM((all_rows, heads, latent), F32)],
        ),
        out_shape=jax.ShapeDtypeStruct(shape, BF),
        compiler_params=pltpu.CompilerParams(vmem_limit_bytes=60 << 20),
        name="attend",
    )(info, queries, cache_t, value_up)


def project_kernel(place_ref, h_ref, *refs):
    own, other, outs, w_ref = refs[:NX], refs[NX : 2 * NX], refs[2 * NX : -1], refs[-1]
    sources, rows, depth = h_ref.shape
    for core in range(NC):

        @pl.when(place_ref[1] == core)
        def _():
            for x in range(NX):

                @pl.when(place_ref[0] == x)
                def _():
                    for dx in range(NX):
                        at = NC * ((x - dx) % NX)
                        w_ref[at + core] = own[dx][...]
                        w_ref[at + 1 - core] = other[dx][...]

    result = lax.dot_general(
        h_ref[...].reshape(sources * rows, depth),
        w_ref[...].reshape(-1, depth),
        (((1,), (1,)), ((), ())),
        preferred_element_type=F32,
    ).reshape(sources, rows, -1)
    part = rows // NY
    for d in range(NY):
        outs[d][...] = (
            result[:, d * part : (d + 1) * part, :].reshape(sources * part, -1).astype(BF)
        )


def project(place, values, own, other):
    sources, rows, depth = values.shape
    pieces = NX * NC
    n_dim = own[0].shape[0]
    vmem = pl.BlockSpec(memory_space=pltpu.VMEM)
    return pl.pallas_call(
        project_kernel,
        in_specs=[pl.BlockSpec(memory_space=pltpu.SMEM)] + [vmem] * (1 + 2 * NX),
        out_specs=[vmem] * NY,
        out_shape=[jax.ShapeDtypeStruct((sources * rows // NY, pieces * n_dim), BF)] * NY,
        scratch_shapes=[pltpu.VMEM((pieces, n_dim, depth), BF)],
        compiler_params=pltpu.CompilerParams(vmem_limit_bytes=32 << 20),
        name="project",
    )(place, values, *own, *other)


def norm_kernel(place_ref, back_ref, hidden_ref, *refs):
    outs, held_ref = refs[:NY], refs[NY]
    g = place_ref[0]
    rows, width = held_ref.shape
    segment = back_ref.shape[2]
    quarter = width // NY
    squares = jnp.zeros((rows, 1), F32)
    lower = lax.rem(g, 2) == 0
    for z in range(NZ):
        at = slice(z * segment, (z + 1) * segment)
        total = back_ref[z * NX].astype(F32)
        for x in range(1, NX):
            total += back_ref[z * NX + x].astype(F32)
        hidden = hidden_ref[lax.div(g, 2), :, at].astype(F32)
        total += jnp.where(lower, hidden[:rows], hidden[rows:])
        held_ref[:, at] = total
        squares += jnp.sum(total * total, axis=1, keepdims=True)
    scale = lax.rsqrt(squares / width + 1e-06)
    for d in range(NY):
        at = pl.ds(pl.multiple_of(lax.rem(g + d, NY) * quarter, quarter), quarter)
        outs[d][:, :quarter] = held_ref[:, at]
        outs[d][:, quarter:] = jnp.broadcast_to(scale, (rows, LANES))


def norm(place, back, hidden):
    micro, row_local, width = hidden.shape
    rows = micro * row_local // NY
    vmem = pl.BlockSpec(memory_space=pltpu.VMEM)
    return pl.pallas_call(
        norm_kernel,
        in_specs=[pl.BlockSpec(memory_space=pltpu.SMEM), vmem, vmem],
        out_specs=[vmem] * NY,
        out_shape=[jax.ShapeDtypeStruct((rows, width // NY + LANES), F32)] * NY,
        scratch_shapes=[pltpu.VMEM((rows, width), F32)],
        name="norm",
    )(place, back, hidden)


def scale_kernel(place_ref, gain_ref, *refs):
    pieces, outs = refs[:NY], refs[NY:]
    slim = outs[0].shape[1]
    quarter = NC * slim
    for k in range(NC):
        start = lax.rem(place_ref[1] + k, NC) * slim
        gain = gain_ref[:, pl.ds(pl.multiple_of(place_ref[0] * quarter + start, LANES), slim)]
        at = pl.ds(pl.multiple_of(start, LANES), slim)
        rows = [p[:, at] * p[:, quarter : quarter + 1] * gain for p in pieces]
        outs[k][...] = jnp.concatenate(rows).astype(BF)


def scale_rows(place, gain, pieces):
    rows = NY * pieces[0].shape[0]
    slim = gain.shape[1] // (NY * NC)
    vmem = pl.BlockSpec(memory_space=pltpu.VMEM)
    return pl.pallas_call(
        scale_kernel,
        in_specs=[pl.BlockSpec(memory_space=pltpu.SMEM)] + [vmem] * (1 + NY),
        out_specs=[vmem] * NC,
        out_shape=[jax.ShapeDtypeStruct((rows, slim), BF)] * NC,
        name="scale_rows",
    )(place, gain, *pieces)


def join_kernel(place_ref, *refs):
    pieces, out_ref = refs[:NY], refs[NY]
    quarter = pieces[0].shape[1]
    micro, rows = out_ref.shape[:2]
    for d in range(NY):
        at = lax.rem(place_ref[0] - d + NY, NY) * quarter
        for m in range(micro):
            out_ref[m, :, pl.ds(pl.multiple_of(at, quarter), quarter)] = pieces[d][
                m * rows : (m + 1) * rows, :
            ]


def join(place, pieces, shape):
    vmem = pl.BlockSpec(memory_space=pltpu.VMEM)
    return pl.pallas_call(
        join_kernel,
        in_specs=[pl.BlockSpec(memory_space=pltpu.SMEM)] + [vmem] * NY,
        out_specs=vmem,
        out_shape=jax.ShapeDtypeStruct(shape, BF),
        name="join",
    )(place, *pieces)


def gate_up_kernel(place_ref, x_ref, w_ref, *refs):
    del place_ref
    refs[-1][...] = jnp.dot(x_ref[...], w_ref[...], preferred_element_type=F32)


def gate_up_last_kernel(units, place_ref, x_ref, w_ref, sum_ref, *refs):
    outs, acc_ref = refs[:NY], refs[NY]
    acc_ref[...] = sum_ref[...] + jnp.dot(x_ref[...], w_ref[...], preferred_element_type=F32)
    for d in range(NY):
        to = lax.rem(place_ref[0] + d, NY)
        for k in range(2):
            start = pl.multiple_of((k * NY + to) * units, units)
            outs[d][:, k * units : (k + 1) * units] = acc_ref[:, pl.ds(start, units)].astype(BF)


def gate_up_dot(place, half, x, w, before=None):
    count, depth = x.shape
    width = w.shape[1]
    units = width // (2 * NY)
    in_specs = [
        pl.BlockSpec((count, depth), lambda i, p: (0, 0)),
        pl.BlockSpec((depth, width), lambda i, p: (lax.rem(p[1] + half, NC), 0)),
    ]
    if before is None:
        body, operands, scratch = gate_up_kernel, (x, w), []
        out_specs = pl.BlockSpec((count, width), lambda i, p: (0, 0))
        out_shape = jax.ShapeDtypeStruct((count, width), F32)
    else:
        body, operands = functools.partial(gate_up_last_kernel, units), (x, w, before)
        scratch = [pltpu.VMEM((count, width), F32)]
        in_specs.append(pl.BlockSpec((count, width), lambda i, p: (0, 0)))
        out_specs = [pl.BlockSpec((count, 2 * units), lambda i, p: (0, 0))] * NY
        out_shape = [jax.ShapeDtypeStruct((count, 2 * units), BF)] * NY
    return pl.pallas_call(
        body,
        grid_spec=pltpu.PrefetchScalarGridSpec(
            num_scalar_prefetch=1,
            grid=(1,),
            in_specs=in_specs,
            out_specs=out_specs,
            scratch_shapes=scratch,
        ),
        out_shape=out_shape,
        compiler_params=pltpu.CompilerParams(vmem_limit_bytes=32 << 20),
        cost_estimate=pl.CostEstimate(
            flops=2 * count * depth * width, bytes_accessed=6 << 20, transcendentals=0
        ),
        name="gate_up",
    )(place, *operands)


def down_kernel(place_ref, *refs):
    del place_ref
    acts, downs, out_ref = refs[:NY], refs[NY : 2 * NY], refs[2 * NY]
    act = jnp.concatenate([a[...] for a in acts], axis=1)
    down = jnp.concatenate([w[...] for w in downs], axis=0)
    out_ref[...] = jnp.dot(act, down, preferred_element_type=F32).astype(out_ref.dtype)


def down_dot(place, half, acts, downs, dtype):
    count, units = acts[0].shape
    width = downs[0].shape[1] // NC
    return pl.pallas_call(
        down_kernel,
        grid_spec=pltpu.PrefetchScalarGridSpec(
            num_scalar_prefetch=1,
            grid=(1,),
            in_specs=[pl.BlockSpec((count, units), lambda i, p: (0, 0))] * NY
            + [pl.BlockSpec((units, width), lambda i, p: (0, lax.rem(p[1] + half, NC)))] * NY,
            out_specs=pl.BlockSpec((count, width), lambda i, p: (0, 0)),
        ),
        out_shape=jax.ShapeDtypeStruct((count, width), dtype),
        compiler_params=pltpu.CompilerParams(vmem_limit_bytes=32 << 20),
        cost_estimate=pl.CostEstimate(
            flops=2 * count * units * NY * width, bytes_accessed=3 << 20, transcendentals=0
        ),
        name="down",
    )(place, *acts, *downs)


def swap_core(a):
    return lax.ppermute(a, "c", [(0, 1), (1, 0)])


def shift_y(a, d):
    return lax.ppermute(a, "y", [(i, (i + d) % NY) for i in range(NY)])


def shift_x(a, d):
    return lax.ppermute(a, "x", [(i, (i + d) % NX) for i in range(NX)])


def lane_part(a, index, size):
    return lax.dynamic_slice_in_dim(a, index * size, size, 1)


def gather_y(a):
    return [a] + [shift_y(a, d) for d in range(1, NY)]


def absolute(items, g):
    back = [items[(-j) % NY] for j in range(NY)]
    return lax.dynamic_slice_in_dim(jnp.stack(back + back[: NY - 1]), (NY - g) % NY, NY, 0)


def routing(ids, gates, expert_count, capacity, g):
    blocks, rows, top = ids.shape
    hot = ids[..., None] == jnp.arange(expert_count, dtype=jnp.int32)
    chosen = jnp.any(hot, axis=2)
    weight = jnp.sum(jnp.where(hot, gates[..., None], 0.0), axis=2)
    counts = chosen.astype(jnp.int32)
    place = jnp.cumsum(counts, axis=1) - counts
    block = jnp.broadcast_to(jnp.arange(blocks, dtype=jnp.int32)[:, None, None], place.shape)
    slot = jnp.where(chosen, block * capacity + place, -1).reshape(blocks * rows, expert_count)
    slots = jnp.arange(blocks * capacity, dtype=jnp.int32)[None, :, None]
    flat = (expert_count * blocks * capacity, blocks * rows)
    weight = weight.reshape(blocks * rows, expert_count).T[:, None, :]
    weights = jnp.where(slot.T[:, None, :] == slots, weight, 0.0).reshape(flat)
    turned = slot.reshape(NC, NY, -1)
    turned = jnp.stack(
        [lax.dynamic_index_in_dim(turned, (g - d) % NY, 1, keepdims=False) for d in range(NY)],
        axis=1,
    )
    turned = turned.reshape(blocks * rows, expert_count)
    pick = (turned.T[:, None, :] == slots).reshape(flat).astype(BF)
    return pick, weights


def local(
    hidden_in,
    queries,
    latent_cache,
    cache_lengths,
    expert_ids,
    gate_values,
    norm_gain,
    value_up,
    out_proj,
    gate_up,
    down_proj,
):
    g, c = lax.axis_index("y"), lax.axis_index("c")
    first = c == 0
    micro, row_local, width = hidden_in.shape
    rows = micro * row_local
    part = rows // NY
    quarter, slim = width // NY, width // (NY * NC)
    k_dim, n_dim = out_proj.shape
    k_slice = k_dim // NX
    expert_count = NZ * NX
    top = expert_ids.shape[2]
    capacity = min(row_local, 4)

    x = lax.axis_index("x")
    place = jnp.stack([g, c, x]).astype(jnp.int32)
    wt = out_proj.T
    w_own = [lane_part(wt, x, k_slice)]
    w_own += [shift_x(lane_part(wt, (x + d) % NX, k_slice), d) for d in range(1, NX)]
    w_other = [swap_core(w) for w in w_own]
    info = jnp.concatenate([g.astype(jnp.int32)[None], cache_lengths.reshape(rows)])

    ids_o, gates_o = swap_core(expert_ids), swap_core(gate_values)
    ids = jnp.concatenate(
        [jnp.where(first, expert_ids, ids_o), jnp.where(first, ids_o, expert_ids)]
    )
    gates = jnp.concatenate(
        [jnp.where(first, gate_values, gates_o), jnp.where(first, gates_o, gate_values)]
    )
    pick, weights = routing(ids, gates, expert_count, capacity, g)

    send = attend(
        info,
        queries.reshape((rows,) + queries.shape[2:]),
        latent_cache.transpose(0, 1, 3, 2).reshape((rows,) + latent_cache.shape[:1:-1]),
        value_up,
    )
    down = [None] * NY

    def send_down(d, source):
        return shift_y(lane_part(source, (g + d) % NY, quarter), d)

    down_in, gate_up, send = lax.optimization_barrier((down_proj[0], gate_up, send))
    down[1], down[3] = send_down(1, down_in), send_down(3, down_in)
    gu = gate_up[0].reshape(quarter, -1)
    got = lax.all_to_all(send, ("z", "x"), 0, 0, tiled=True)
    got, gu, down[1], down[3] = lax.optimization_barrier((got, gu, down[1], down[3]))
    parts = project(jnp.stack([x, c]).astype(jnp.int32), got, w_own, w_other)
    parts = [parts[0]] + [shift_y(parts[d], d) for d in range(1, NY)]
    spread = sum(p.astype(F32) for p in parts).astype(BF)
    back = lax.all_to_all(
        spread.reshape(NZ * NX, part, NX * NC * n_dim), ("z", "x"), 0, 0, tiled=True
    )
    pieces = norm(place, back, hidden_in)
    pieces = [pieces[0]] + [shift_y(pieces[d], d) for d in range(1, NY)]
    keep, give = scale_rows(place, norm_gain[None, :], pieces)
    took = swap_core(give)
    chip_rows = jnp.concatenate([jnp.where(first, keep, took), jnp.where(first, took, keep)])
    outgoing = jnp.dot(pick, chip_rows, preferred_element_type=F32).astype(BF)
    slots = NC * micro * capacity
    down_in, outgoing = lax.optimization_barrier((down_proj[0], outgoing))
    down[0] = lane_part(down_in, g, quarter)
    down[2] = send_down(2, down_in)
    received = lax.all_to_all(
        outgoing.reshape(expert_count, slots, slim), ("z", "x"), 0, 0, tiled=True
    ).reshape(expert_count * slots, slim)
    received, down[0], down[2] = lax.optimization_barrier((received, down[0], down[2]))
    other = swap_core(received)
    own_sum = gate_up_dot(place, 0, received, gu)
    parts = gate_up_dot(place, 1, other, gu, own_sum)
    parts = [parts[0]] + [shift_y(parts[d], d) for d in range(1, NY)]
    total = sum(p.astype(F32) for p in parts)
    units = total.shape[1] // 2
    act = (jax.nn.silu(total[:, :units]) * total[:, units:]).astype(BF)
    acts = gather_y(act)
    give_r = down_dot(place, 1, acts, down, BF)
    keep_r = down_dot(place, 0, acts, down, F32)
    whole = (keep_r + swap_core(give_r).astype(F32)).astype(BF)
    returned = lax.all_to_all(
        whole.reshape(expert_count, slots, slim), ("z", "x"), 0, 0, tiled=True
    ).reshape(expert_count * slots, slim)
    high = weights.astype(BF)
    low = (weights - high.astype(F32)).astype(BF)
    both = lax.dot_general(
        jnp.concatenate([high, low], axis=1),
        returned,
        (((0,), (0,)), ((), ())),
        preferred_element_type=F32,
    )
    mix = both[: NC * rows] + both[NC * rows :]
    mix_keep = jnp.where(first, mix[:rows], mix[rows:])
    mix_give = jnp.where(first, mix[rows:], mix[:rows])
    mix_took = swap_core(mix_give)
    mix_q = jnp.concatenate(
        [jnp.where(first, mix_keep, mix_took), jnp.where(first, mix_took, mix_keep)], axis=1
    )
    residual_q = absolute([p[:, :quarter] for p in pieces], g).reshape(rows, quarter)
    out_q = (residual_q + mix_q).astype(BF)
    return join(place, gather_y(out_q), hidden_in.shape)


def solution(mesh):
    fine = Mesh(mesh.devices.reshape(NY, NZ, NX, NC), ("y", "z", "x", "c"))
    ep = ("z", "x", "c")
    return jax.shard_map(
        local,
        mesh=fine,
        in_specs=(
            P(None, ep, None),
            P(None, ep, "y", None),
            P(None, ep, None, None),
            P(None, ep),
            P(None, ep, None),
            P(None, ep, None),
            P(),
            P("y", None, None),
            P("y", ep),
            P(ep, "y", None, None),
            P(ep, "y", None),
        ),
        out_specs=P(None, ep, None),
        check_vma=False,
    )
```

```python
import functools
import math

import jax
import jax.numpy as jnp
from jax import lax
from jax.experimental import pallas as pl
from jax.experimental.pallas import tpu as pltpu
from jax.sharding import Mesh
from jax.sharding import PartitionSpec as P

ROPE = 64
NOPE = 128
NY, NZ, NX, NC = 4, 8, 4, 2
BF = jnp.bfloat16
F32 = jnp.float32
LANES = 128


def attend_kernel(rows, heads, latent, info_ref, q_ref, cache_ref, up_ref, out_ref, held):
    step = pl.program_id(0)
    scale = 1.0 / math.sqrt(ROPE + NOPE)
    base = lax.rem(step + info_ref[0], NY) * rows
    for r in range(rows):
        cache = cache_ref[r]
        scores = jnp.dot(q_ref[r], cache, preferred_element_type=F32) * scale
        at = lax.broadcasted_iota(jnp.int32, scores.shape, 1)
        in_range = at < info_ref[1 + base + r]
        masked = jnp.where(in_range, scores, -1e30)
        peak = jnp.max(masked, axis=1, keepdims=True)
        exponent = jnp.where(in_range, jnp.exp(masked - peak), 0.0)
        weights = (exponent / jnp.sum(exponent, axis=1, keepdims=True)).astype(BF)
        held[step * rows + r] = lax.dot_general(
            weights, cache[:latent], (((1,), (1,)), ((), ())), preferred_element_type=F32
        )

    @pl.when(step == NY - 1)
    def _():
        group, vdim = heads // NX, up_ref.shape[2]
        for h in range(heads):
            value = jnp.dot(
                held[:, h, :].astype(BF), up_ref[h], preferred_element_type=F32
            ).astype(BF)
            lanes = slice(h % group * vdim, (h % group + 1) * vdim)
            for z in range(NZ):
                out_ref[z * NX + h // group, :, lanes] = value


def attend(info, queries, cache_t, value_up):
    all_rows, heads, key = queries.shape
    rows = all_rows // NY
    latent, vdim = value_up.shape[1:]
    length = cache_t.shape[2]
    shape = (NZ * NX, all_rows, heads * vdim // NX)
    turn = lambda i, info: (lax.rem(i + info[0], NY), 0, 0)
    return pl.pallas_call(
        functools.partial(attend_kernel, rows, heads, latent),
        grid_spec=pltpu.PrefetchScalarGridSpec(
            num_scalar_prefetch=1,
            grid=(NY,),
            in_specs=[
                pl.BlockSpec((rows, heads, key), turn),
                pl.BlockSpec((rows, key, length), turn),
                pl.BlockSpec(value_up.shape, lambda i, info: (0, 0, 0)),
            ],
            out_specs=pl.BlockSpec(shape, lambda i, info: (0, 0, 0)),
            scratch_shapes=[pltpu.VMEM((all_rows, heads, latent), F32)],
        ),
        out_shape=jax.ShapeDtypeStruct(shape, BF),
        compiler_params=pltpu.CompilerParams(vmem_limit_bytes=60 << 20),
        name="attend",
    )(info, queries, cache_t, value_up)


def project_kernel(place_ref, h_ref, *refs):
    own, other, outs, w_ref = refs[:NX], refs[NX : 2 * NX], refs[2 * NX : -1], refs[-1]
    sources, rows, depth = h_ref.shape
    for core in range(NC):

        @pl.when(place_ref[1] == core)
        def _():
            for x in range(NX):

                @pl.when(place_ref[0] == x)
                def _():
                    for dx in range(NX):
                        at = NC * ((x - dx) % NX)
                        w_ref[at + core] = own[dx][...]
                        w_ref[at + 1 - core] = other[dx][...]

    result = lax.dot_general(
        h_ref[...].reshape(sources * rows, depth),
        w_ref[...].reshape(-1, depth),
        (((1,), (1,)), ((), ())),
        preferred_element_type=F32,
    ).reshape(sources, rows, -1)
    part = rows // NY
    for d in range(NY):
        outs[d][...] = (
            result[:, d * part : (d + 1) * part, :].reshape(sources * part, -1).astype(BF)
        )


def project(place, values, own, other):
    sources, rows, depth = values.shape
    pieces = NX * NC
    n_dim = own[0].shape[0]
    vmem = pl.BlockSpec(memory_space=pltpu.VMEM)
    return pl.pallas_call(
        project_kernel,
        in_specs=[pl.BlockSpec(memory_space=pltpu.SMEM)] + [vmem] * (1 + 2 * NX),
        out_specs=[vmem] * NY,
        out_shape=[jax.ShapeDtypeStruct((sources * rows // NY, pieces * n_dim), BF)] * NY,
        scratch_shapes=[pltpu.VMEM((pieces, n_dim, depth), BF)],
        compiler_params=pltpu.CompilerParams(vmem_limit_bytes=32 << 20),
        name="project",
    )(place, values, *own, *other)


def norm_kernel(place_ref, back_ref, hidden_ref, *refs):
    outs, held_ref = refs[:NY], refs[NY]
    g = place_ref[0]
    rows, width = held_ref.shape
    segment = back_ref.shape[2]
    quarter = width // NY
    squares = jnp.zeros((rows, 1), F32)
    lower = lax.rem(g, 2) == 0
    for z in range(NZ):
        at = slice(z * segment, (z + 1) * segment)
        total = back_ref[z * NX].astype(F32)
        for x in range(1, NX):
            total += back_ref[z * NX + x].astype(F32)
        hidden = hidden_ref[lax.div(g, 2), :, at].astype(F32)
        total += jnp.where(lower, hidden[:rows], hidden[rows:])
        held_ref[:, at] = total
        squares += jnp.sum(total * total, axis=1, keepdims=True)
    scale = lax.rsqrt(squares / width + 1e-06)
    for d in range(NY):
        at = pl.ds(pl.multiple_of(lax.rem(g + d, NY) * quarter, quarter), quarter)
        outs[d][:, :quarter] = held_ref[:, at]
        outs[d][:, quarter:] = jnp.broadcast_to(scale, (rows, LANES))


def norm(place, back, hidden):
    micro, row_local, width = hidden.shape
    rows = micro * row_local // NY
    vmem = pl.BlockSpec(memory_space=pltpu.VMEM)
    return pl.pallas_call(
        norm_kernel,
        in_specs=[pl.BlockSpec(memory_space=pltpu.SMEM), vmem, vmem],
        out_specs=[vmem] * NY,
        out_shape=[jax.ShapeDtypeStruct((rows, width // NY + LANES), F32)] * NY,
        scratch_shapes=[pltpu.VMEM((rows, width), F32)],
        name="norm",
    )(place, back, hidden)


def scale_kernel(place_ref, gain_ref, *refs):
    pieces, outs = refs[:NY], refs[NY:]
    slim = outs[0].shape[1]
    quarter = NC * slim
    for k in range(NC):
        start = lax.rem(place_ref[1] + k, NC) * slim
        gain = gain_ref[:, pl.ds(pl.multiple_of(place_ref[0] * quarter + start, LANES), slim)]
        at = pl.ds(pl.multiple_of(start, LANES), slim)
        rows = [p[:, at] * p[:, quarter : quarter + 1] * gain for p in pieces]
        outs[k][...] = jnp.concatenate(rows).astype(BF)


def scale_rows(place, gain, pieces):
    rows = NY * pieces[0].shape[0]
    slim = gain.shape[1] // (NY * NC)
    vmem = pl.BlockSpec(memory_space=pltpu.VMEM)
    return pl.pallas_call(
        scale_kernel,
        in_specs=[pl.BlockSpec(memory_space=pltpu.SMEM)] + [vmem] * (1 + NY),
        out_specs=[vmem] * NC,
        out_shape=[jax.ShapeDtypeStruct((rows, slim), BF)] * NC,
        name="scale_rows",
    )(place, gain, *pieces)


def join_kernel(place_ref, *refs):
    pieces, out_ref = refs[:NY], refs[NY]
    quarter = pieces[0].shape[1]
    micro, rows = out_ref.shape[:2]
    for d in range(NY):
        at = lax.rem(place_ref[0] - d + NY, NY) * quarter
        for m in range(micro):
            out_ref[m, :, pl.ds(pl.multiple_of(at, quarter), quarter)] = pieces[d][
                m * rows : (m + 1) * rows, :
            ]


def join(place, pieces, shape):
    vmem = pl.BlockSpec(memory_space=pltpu.VMEM)
    return pl.pallas_call(
        join_kernel,
        in_specs=[pl.BlockSpec(memory_space=pltpu.SMEM)] + [vmem] * NY,
        out_specs=vmem,
        out_shape=jax.ShapeDtypeStruct(shape, BF),
        name="join",
    )(place, *pieces)


def gate_up_kernel(place_ref, x_ref, w_ref, *refs):
    del place_ref
    refs[-1][...] = jnp.dot(x_ref[...], w_ref[...], preferred_element_type=F32)


def gate_up_last_kernel(units, place_ref, x_ref, w_ref, sum_ref, *refs):
    outs, acc_ref = refs[:NY], refs[NY]
    acc_ref[...] = sum_ref[...] + jnp.dot(x_ref[...], w_ref[...], preferred_element_type=F32)
    for d in range(NY):
        to = lax.rem(place_ref[0] + d, NY)
        for k in range(2):
            start = pl.multiple_of((k * NY + to) * units, units)
            outs[d][:, k * units : (k + 1) * units] = acc_ref[:, pl.ds(start, units)].astype(BF)


def gate_up_dot(place, half, x, w, before=None):
    count, depth = x.shape
    width = w.shape[1]
    units = width // (2 * NY)
    in_specs = [
        pl.BlockSpec((count, depth), lambda i, p: (0, 0)),
        pl.BlockSpec((depth, width), lambda i, p: (lax.rem(p[1] + half, NC), 0)),
    ]
    if before is None:
        body, operands, scratch = gate_up_kernel, (x, w), []
        out_specs = pl.BlockSpec((count, width), lambda i, p: (0, 0))
        out_shape = jax.ShapeDtypeStruct((count, width), F32)
    else:
        body, operands = functools.partial(gate_up_last_kernel, units), (x, w, before)
        scratch = [pltpu.VMEM((count, width), F32)]
        in_specs.append(pl.BlockSpec((count, width), lambda i, p: (0, 0)))
        out_specs = [pl.BlockSpec((count, 2 * units), lambda i, p: (0, 0))] * NY
        out_shape = [jax.ShapeDtypeStruct((count, 2 * units), BF)] * NY
    return pl.pallas_call(
        body,
        grid_spec=pltpu.PrefetchScalarGridSpec(
            num_scalar_prefetch=1,
            grid=(1,),
            in_specs=in_specs,
            out_specs=out_specs,
            scratch_shapes=scratch,
        ),
        out_shape=out_shape,
        compiler_params=pltpu.CompilerParams(vmem_limit_bytes=32 << 20),
        cost_estimate=pl.CostEstimate(
            flops=2 * count * depth * width, bytes_accessed=6 << 20, transcendentals=0
        ),
        name="gate_up",
    )(place, *operands)


def down_kernel(place_ref, *refs):
    del place_ref
    acts, downs, out_ref = refs[:NY], refs[NY : 2 * NY], refs[2 * NY]
    act = jnp.concatenate([a[...] for a in acts], axis=1)
    down = jnp.concatenate([w[...] for w in downs], axis=0)
    out_ref[...] = jnp.dot(act, down, preferred_element_type=F32).astype(out_ref.dtype)


def down_dot(place, half, acts, downs, dtype):
    count, units = acts[0].shape
    width = downs[0].shape[1] // NC
    return pl.pallas_call(
        down_kernel,
        grid_spec=pltpu.PrefetchScalarGridSpec(
            num_scalar_prefetch=1,
            grid=(1,),
            in_specs=[pl.BlockSpec((count, units), lambda i, p: (0, 0))] * NY
            + [pl.BlockSpec((units, width), lambda i, p: (0, lax.rem(p[1] + half, NC)))] * NY,
            out_specs=pl.BlockSpec((count, width), lambda i, p: (0, 0)),
        ),
        out_shape=jax.ShapeDtypeStruct((count, width), dtype),
        compiler_params=pltpu.CompilerParams(vmem_limit_bytes=32 << 20),
        cost_estimate=pl.CostEstimate(
            flops=2 * count * units * NY * width, bytes_accessed=3 << 20, transcendentals=0
        ),
        name="down",
    )(place, *acts, *downs)


def swap_core(a):
    return lax.ppermute(a, "c", [(0, 1), (1, 0)])


def shift_y(a, d):
    return lax.ppermute(a, "y", [(i, (i + d) % NY) for i in range(NY)])


def shift_x(a, d):
    return lax.ppermute(a, "x", [(i, (i + d) % NX) for i in range(NX)])


def lane_part(a, index, size):
    return lax.dynamic_slice_in_dim(a, index * size, size, 1)


def gather_y(a):
    return [a] + [shift_y(a, d) for d in range(1, NY)]


def absolute(items, g):
    back = [items[(-j) % NY] for j in range(NY)]
    return lax.dynamic_slice_in_dim(jnp.stack(back + back[: NY - 1]), (NY - g) % NY, NY, 0)


def routing(ids, gates, expert_count, capacity, g):
    blocks, rows, top = ids.shape
    hot = ids[..., None] == jnp.arange(expert_count, dtype=jnp.int32)
    chosen = jnp.any(hot, axis=2)
    weight = jnp.sum(jnp.where(hot, gates[..., None], 0.0), axis=2)
    counts = chosen.astype(jnp.int32)
    place = jnp.cumsum(counts, axis=1) - counts
    block = jnp.broadcast_to(jnp.arange(blocks, dtype=jnp.int32)[:, None, None], place.shape)
    slot = jnp.where(chosen, block * capacity + place, -1).reshape(blocks * rows, expert_count)
    slots = jnp.arange(blocks * capacity, dtype=jnp.int32)[None, :, None]
    flat = (expert_count * blocks * capacity, blocks * rows)
    weight = weight.reshape(blocks * rows, expert_count).T[:, None, :]
    weights = jnp.where(slot.T[:, None, :] == slots, weight, 0.0).reshape(flat)
    turned = slot.reshape(NC, NY, -1)
    turned = jnp.stack(
        [lax.dynamic_index_in_dim(turned, (g - d) % NY, 1, keepdims=False) for d in range(NY)],
        axis=1,
    )
    turned = turned.reshape(blocks * rows, expert_count)
    pick = (turned.T[:, None, :] == slots).reshape(flat).astype(BF)
    return pick, weights


def local(
    hidden_in,
    queries,
    latent_cache,
    cache_lengths,
    expert_ids,
    gate_values,
    norm_gain,
    value_up,
    out_proj,
    gate_up,
    down_proj,
):
    g, c = lax.axis_index("y"), lax.axis_index("c")
    first = c == 0
    micro, row_local, width = hidden_in.shape
    rows = micro * row_local
    part = rows // NY
    quarter, slim = width // NY, width // (NY * NC)
    k_dim, n_dim = out_proj.shape
    k_slice = k_dim // NX
    expert_count = NZ * NX
    top = expert_ids.shape[2]
    capacity = min(row_local, 4)

    x = lax.axis_index("x")
    place = jnp.stack([g, c, x]).astype(jnp.int32)
    wt = out_proj.T
    w_own = [lane_part(wt, x, k_slice)]
    w_own += [shift_x(lane_part(wt, (x + d) % NX, k_slice), d) for d in range(1, NX)]
    info = jnp.concatenate([g.astype(jnp.int32)[None], cache_lengths.reshape(rows)])

    ids_o, gates_o = swap_core(expert_ids), swap_core(gate_values)
    ids = jnp.concatenate(
        [jnp.where(first, expert_ids, ids_o), jnp.where(first, ids_o, expert_ids)]
    )
    gates = jnp.concatenate(
        [jnp.where(first, gate_values, gates_o), jnp.where(first, gates_o, gate_values)]
    )
    pick, weights = routing(ids, gates, expert_count, capacity, g)

    send = attend(
        info,
        queries.reshape((rows,) + queries.shape[2:]),
        latent_cache.transpose(0, 1, 3, 2).reshape((rows,) + latent_cache.shape[:1:-1]),
        value_up,
    )
    send, *w_own = lax.optimization_barrier((send, *w_own))
    w_other = [swap_core(w) for w in w_own]
    got = lax.all_to_all(send, ("z", "x"), 0, 0, tiled=True)
    parts = project(jnp.stack([x, c]).astype(jnp.int32), got, w_own, w_other)
    parts = [parts[0]] + [shift_y(parts[d], d) for d in range(1, NY)]
    spread = sum(p.astype(F32) for p in parts).astype(BF)
    back = lax.all_to_all(
        spread.reshape(NZ * NX, part, NX * NC * n_dim), ("z", "x"), 0, 0, tiled=True
    )
    pieces = norm(place, back, hidden_in)
    pieces = [pieces[0]] + [shift_y(pieces[d], d) for d in range(1, NY)]
    keep, give = scale_rows(place, norm_gain[None, :], pieces)
    took = swap_core(give)
    chip_rows = jnp.concatenate([jnp.where(first, keep, took), jnp.where(first, took, keep)])
    outgoing = jnp.dot(pick, chip_rows, preferred_element_type=F32).astype(BF)
    slots = NC * micro * capacity
    down_in, gate_up, outgoing = lax.optimization_barrier((down_proj[0], gate_up, outgoing))
    gu = gate_up[0].reshape(quarter, -1)
    down = [lane_part(down_in, g, quarter)]
    down += [shift_y(lane_part(down_in, (g + d) % NY, quarter), d) for d in range(1, NY)]
    received = lax.all_to_all(
        outgoing.reshape(expert_count, slots, slim), ("z", "x"), 0, 0, tiled=True
    ).reshape(expert_count * slots, slim)
    received, gu, *down = lax.optimization_barrier((received, gu, *down))
    other = swap_core(received)
    own_sum = gate_up_dot(place, 0, received, gu)
    parts = gate_up_dot(place, 1, other, gu, own_sum)
    parts = [parts[0]] + [shift_y(parts[d], d) for d in range(1, NY)]
    total = sum(p.astype(F32) for p in parts)
    units = total.shape[1] // 2
    act = (jax.nn.silu(total[:, :units]) * total[:, units:]).astype(BF)
    acts = gather_y(act)
    give_r = down_dot(place, 1, acts, down, BF)
    keep_r = down_dot(place, 0, acts, down, F32)
    whole = (keep_r + swap_core(give_r).astype(F32)).astype(BF)
    returned = lax.all_to_all(
        whole.reshape(expert_count, slots, slim), ("z", "x"), 0, 0, tiled=True
    ).reshape(expert_count * slots, slim)
    high = weights.astype(BF)
    low = (weights - high.astype(F32)).astype(BF)
    both = lax.dot_general(
        jnp.concatenate([high, low], axis=1),
        returned,
        (((0,), (0,)), ((), ())),
        preferred_element_type=F32,
    )
    mix = both[: NC * rows] + both[NC * rows :]
    mix_keep = jnp.where(first, mix[:rows], mix[rows:])
    mix_give = jnp.where(first, mix[rows:], mix[:rows])
    mix_took = swap_core(mix_give)
    mix_q = jnp.concatenate(
        [jnp.where(first, mix_keep, mix_took), jnp.where(first, mix_took, mix_keep)], axis=1
    )
    residual_q = absolute([p[:, :quarter] for p in pieces], g).reshape(rows, quarter)
    out_q = (residual_q + mix_q).astype(BF)
    return join(place, gather_y(out_q), hidden_in.shape)


def solution(mesh):
    fine = Mesh(mesh.devices.reshape(NY, NZ, NX, NC), ("y", "z", "x", "c"))
    ep = ("z", "x", "c")
    return jax.shard_map(
        local,
        mesh=fine,
        in_specs=(
            P(None, ep, None),
            P(None, ep, "y", None),
            P(None, ep, None, None),
            P(None, ep),
            P(None, ep, None),
            P(None, ep, None),
            P(),
            P("y", None, None),
            P("y", ep),
            P(ep, "y", None, None),
            P(ep, "y", None),
        ),
        out_specs=P(None, ep, None),
        check_vma=False,
    )
```

```python
import functools
import math

import jax
import jax.numpy as jnp
from jax import lax
from jax.experimental import pallas as pl
from jax.experimental.pallas import tpu as pltpu
from jax.sharding import Mesh
from jax.sharding import PartitionSpec as P

ROPE = 64
NOPE = 128
NY, NZ, NX, NC = 4, 8, 4, 2
BF = jnp.bfloat16
F32 = jnp.float32
LANES = 128


def attend_kernel(rows, heads, latent, info_ref, q_ref, cache_ref, up_ref, out_ref, held):
    step = pl.program_id(0)
    scale = 1.0 / math.sqrt(ROPE + NOPE)
    base = lax.rem(step + info_ref[0], NY) * rows
    for r in range(rows):
        cache = cache_ref[r]
        scores = jnp.dot(q_ref[r], cache, preferred_element_type=F32) * scale
        at = lax.broadcasted_iota(jnp.int32, scores.shape, 1)
        in_range = at < info_ref[1 + base + r]
        masked = jnp.where(in_range, scores, -1e30)
        peak = jnp.max(masked, axis=1, keepdims=True)
        exponent = jnp.where(in_range, jnp.exp(masked - peak), 0.0)
        weights = (exponent / jnp.sum(exponent, axis=1, keepdims=True)).astype(BF)
        held[step * rows + r] = lax.dot_general(
            weights, cache[:latent], (((1,), (1,)), ((), ())), preferred_element_type=F32
        )

    @pl.when(step == NY - 1)
    def _():
        group, vdim = heads // NX, up_ref.shape[2]
        for h in range(heads):
            value = jnp.dot(
                held[:, h, :].astype(BF), up_ref[h], preferred_element_type=F32
            ).astype(BF)
            lanes = slice(h % group * vdim, (h % group + 1) * vdim)
            for z in range(NZ):
                out_ref[z * NX + h // group, :, lanes] = value


def attend(info, queries, cache_t, value_up):
    all_rows, heads, key = queries.shape
    rows = all_rows // NY
    latent, vdim = value_up.shape[1:]
    length = cache_t.shape[2]
    shape = (NZ * NX, all_rows, heads * vdim // NX)
    turn = lambda i, info: (lax.rem(i + info[0], NY), 0, 0)
    return pl.pallas_call(
        functools.partial(attend_kernel, rows, heads, latent),
        grid_spec=pltpu.PrefetchScalarGridSpec(
            num_scalar_prefetch=1,
            grid=(NY,),
            in_specs=[
                pl.BlockSpec((rows, heads, key), turn),
                pl.BlockSpec((rows, key, length), turn),
                pl.BlockSpec(value_up.shape, lambda i, info: (0, 0, 0)),
            ],
            out_specs=pl.BlockSpec(shape, lambda i, info: (0, 0, 0)),
            scratch_shapes=[pltpu.VMEM((all_rows, heads, latent), F32)],
        ),
        out_shape=jax.ShapeDtypeStruct(shape, BF),
        compiler_params=pltpu.CompilerParams(vmem_limit_bytes=60 << 20),
        name="attend",
    )(info, queries, cache_t, value_up)


def project_kernel(place_ref, h_ref, *refs):
    own, other, outs, w_ref = refs[:NX], refs[NX : 2 * NX], refs[2 * NX : -1], refs[-1]
    sources, rows, depth = h_ref.shape
    for core in range(NC):

        @pl.when(place_ref[1] == core)
        def _():
            for x in range(NX):

                @pl.when(place_ref[0] == x)
                def _():
                    for dx in range(NX):
                        at = NC * ((x - dx) % NX)
                        w_ref[at + core] = own[dx][...]
                        w_ref[at + 1 - core] = other[dx][...]

    result = lax.dot_general(
        h_ref[...].reshape(sources * rows, depth),
        w_ref[...].reshape(-1, depth),
        (((1,), (1,)), ((), ())),
        preferred_element_type=F32,
    ).reshape(sources, rows, -1)
    part = rows // NY
    for d in range(NY):
        outs[d][...] = (
            result[:, d * part : (d + 1) * part, :].reshape(sources * part, -1).astype(BF)
        )


def project(place, values, own, other):
    sources, rows, depth = values.shape
    pieces = NX * NC
    n_dim = own[0].shape[0]
    vmem = pl.BlockSpec(memory_space=pltpu.VMEM)
    return pl.pallas_call(
        project_kernel,
        in_specs=[pl.BlockSpec(memory_space=pltpu.SMEM)] + [vmem] * (1 + 2 * NX),
        out_specs=[vmem] * NY,
        out_shape=[jax.ShapeDtypeStruct((sources * rows // NY, pieces * n_dim), BF)] * NY,
        scratch_shapes=[pltpu.VMEM((pieces, n_dim, depth), BF)],
        compiler_params=pltpu.CompilerParams(vmem_limit_bytes=32 << 20),
        name="project",
    )(place, values, *own, *other)


def norm_kernel(place_ref, back_ref, hidden_ref, *refs):
    outs, held_ref = refs[:NY], refs[NY]
    g = place_ref[0]
    rows, width = held_ref.shape
    segment = back_ref.shape[2]
    quarter = width // NY
    squares = jnp.zeros((rows, 1), F32)
    lower = lax.rem(g, 2) == 0
    for z in range(NZ):
        at = slice(z * segment, (z + 1) * segment)
        total = back_ref[z * NX].astype(F32)
        for x in range(1, NX):
            total += back_ref[z * NX + x].astype(F32)
        hidden = hidden_ref[lax.div(g, 2), :, at].astype(F32)
        total += jnp.where(lower, hidden[:rows], hidden[rows:])
        held_ref[:, at] = total
        squares += jnp.sum(total * total, axis=1, keepdims=True)
    scale = lax.rsqrt(squares / width + 1e-06)
    for d in range(NY):
        at = pl.ds(pl.multiple_of(lax.rem(g + d, NY) * quarter, quarter), quarter)
        outs[d][:, :quarter] = held_ref[:, at]
        outs[d][:, quarter:] = jnp.broadcast_to(scale, (rows, LANES))


def norm(place, back, hidden):
    micro, row_local, width = hidden.shape
    rows = micro * row_local // NY
    vmem = pl.BlockSpec(memory_space=pltpu.VMEM)
    return pl.pallas_call(
        norm_kernel,
        in_specs=[pl.BlockSpec(memory_space=pltpu.SMEM), vmem, vmem],
        out_specs=[vmem] * NY,
        out_shape=[jax.ShapeDtypeStruct((rows, width // NY + LANES), F32)] * NY,
        scratch_shapes=[pltpu.VMEM((rows, width), F32)],
        name="norm",
    )(place, back, hidden)


def scale_kernel(place_ref, gain_ref, *refs):
    pieces, outs = refs[:NY], refs[NY:]
    slim = outs[0].shape[1]
    quarter = NC * slim
    for k in range(NC):
        start = lax.rem(place_ref[1] + k, NC) * slim
        gain = gain_ref[:, pl.ds(pl.multiple_of(place_ref[0] * quarter + start, LANES), slim)]
        at = pl.ds(pl.multiple_of(start, LANES), slim)
        rows = [p[:, at] * p[:, quarter : quarter + 1] * gain for p in pieces]
        outs[k][...] = jnp.concatenate(rows).astype(BF)


def scale_rows(place, gain, pieces):
    rows = NY * pieces[0].shape[0]
    slim = gain.shape[1] // (NY * NC)
    vmem = pl.BlockSpec(memory_space=pltpu.VMEM)
    return pl.pallas_call(
        scale_kernel,
        in_specs=[pl.BlockSpec(memory_space=pltpu.SMEM)] + [vmem] * (1 + NY),
        out_specs=[vmem] * NC,
        out_shape=[jax.ShapeDtypeStruct((rows, slim), BF)] * NC,
        name="scale_rows",
    )(place, gain, *pieces)


def join_kernel(place_ref, *refs):
    pieces, out_ref = refs[:NY], refs[NY]
    quarter = pieces[0].shape[1]
    micro, rows = out_ref.shape[:2]
    for d in range(NY):
        at = lax.rem(place_ref[0] - d + NY, NY) * quarter
        for m in range(micro):
            out_ref[m, :, pl.ds(pl.multiple_of(at, quarter), quarter)] = pieces[d][
                m * rows : (m + 1) * rows, :
            ]


def join(place, pieces, shape):
    vmem = pl.BlockSpec(memory_space=pltpu.VMEM)
    return pl.pallas_call(
        join_kernel,
        in_specs=[pl.BlockSpec(memory_space=pltpu.SMEM)] + [vmem] * NY,
        out_specs=vmem,
        out_shape=jax.ShapeDtypeStruct(shape, BF),
        name="join",
    )(place, *pieces)


def gate_up_kernel(place_ref, x_ref, w_ref, *refs):
    del place_ref
    refs[-1][...] = jnp.dot(x_ref[...], w_ref[...], preferred_element_type=F32)


def gate_up_last_kernel(units, place_ref, x_ref, w_ref, sum_ref, *refs):
    outs, acc_ref = refs[:NY], refs[NY]
    acc_ref[...] = sum_ref[...] + jnp.dot(x_ref[...], w_ref[...], preferred_element_type=F32)
    for d in range(NY):
        to = lax.rem(place_ref[0] + d, NY)
        for k in range(2):
            start = pl.multiple_of((k * NY + to) * units, units)
            outs[d][:, k * units : (k + 1) * units] = acc_ref[:, pl.ds(start, units)].astype(BF)


def gate_up_dot(place, half, x, w, before=None):
    count, depth = x.shape
    width = w.shape[1]
    units = width // (2 * NY)
    in_specs = [
        pl.BlockSpec((count, depth), lambda i, p: (0, 0)),
        pl.BlockSpec((depth, width), lambda i, p: (lax.rem(p[1] + half, NC), 0)),
    ]
    if before is None:
        body, operands, scratch = gate_up_kernel, (x, w), []
        out_specs = pl.BlockSpec((count, width), lambda i, p: (0, 0))
        out_shape = jax.ShapeDtypeStruct((count, width), F32)
    else:
        body, operands = functools.partial(gate_up_last_kernel, units), (x, w, before)
        scratch = [pltpu.VMEM((count, width), F32)]
        in_specs.append(pl.BlockSpec((count, width), lambda i, p: (0, 0)))
        out_specs = [pl.BlockSpec((count, 2 * units), lambda i, p: (0, 0))] * NY
        out_shape = [jax.ShapeDtypeStruct((count, 2 * units), BF)] * NY
    return pl.pallas_call(
        body,
        grid_spec=pltpu.PrefetchScalarGridSpec(
            num_scalar_prefetch=1,
            grid=(1,),
            in_specs=in_specs,
            out_specs=out_specs,
            scratch_shapes=scratch,
        ),
        out_shape=out_shape,
        compiler_params=pltpu.CompilerParams(vmem_limit_bytes=32 << 20),
        cost_estimate=pl.CostEstimate(
            flops=2 * count * depth * width, bytes_accessed=6 << 20, transcendentals=0
        ),
        name="gate_up",
    )(place, *operands)


def down_kernel(place_ref, *refs):
    del place_ref
    acts, downs, out_ref = refs[:NY], refs[NY : 2 * NY], refs[2 * NY]
    act = jnp.concatenate([a[...] for a in acts], axis=1)
    down = jnp.concatenate([w[...] for w in downs], axis=0)
    out_ref[...] = jnp.dot(act, down, preferred_element_type=F32).astype(out_ref.dtype)


def down_dot(place, half, acts, downs, dtype):
    count, units = acts[0].shape
    width = downs[0].shape[1] // NC
    return pl.pallas_call(
        down_kernel,
        grid_spec=pltpu.PrefetchScalarGridSpec(
            num_scalar_prefetch=1,
            grid=(1,),
            in_specs=[pl.BlockSpec((count, units), lambda i, p: (0, 0))] * NY
            + [pl.BlockSpec((units, width), lambda i, p: (0, lax.rem(p[1] + half, NC)))] * NY,
            out_specs=pl.BlockSpec((count, width), lambda i, p: (0, 0)),
        ),
        out_shape=jax.ShapeDtypeStruct((count, width), dtype),
        compiler_params=pltpu.CompilerParams(vmem_limit_bytes=32 << 20),
        cost_estimate=pl.CostEstimate(
            flops=2 * count * units * NY * width, bytes_accessed=3 << 20, transcendentals=0
        ),
        name="down",
    )(place, *acts, *downs)


def swap_core(a):
    return lax.ppermute(a, "c", [(0, 1), (1, 0)])


def shift_y(a, d):
    return lax.ppermute(a, "y", [(i, (i + d) % NY) for i in range(NY)])


def shift_x(a, d):
    return lax.ppermute(a, "x", [(i, (i + d) % NX) for i in range(NX)])


def lane_part(a, index, size):
    return lax.dynamic_slice_in_dim(a, index * size, size, 1)


def gather_y(a):
    return [a] + [shift_y(a, d) for d in range(1, NY)]


def absolute(items, g):
    back = [items[(-j) % NY] for j in range(NY)]
    return lax.dynamic_slice_in_dim(jnp.stack(back + back[: NY - 1]), (NY - g) % NY, NY, 0)


def routing(ids, gates, expert_count, capacity, g):
    blocks, rows, top = ids.shape
    hot = ids[..., None] == jnp.arange(expert_count, dtype=jnp.int32)
    chosen = jnp.any(hot, axis=2)
    weight = jnp.sum(jnp.where(hot, gates[..., None], 0.0), axis=2)
    counts = chosen.astype(jnp.int32)
    place = jnp.cumsum(counts, axis=1) - counts
    order = jnp.arange(blocks, dtype=jnp.int32)
    order = order % (blocks // NC) * NC + order // (blocks // NC)
    slot = jnp.where(chosen, order[:, None, None] * capacity + place, -1)
    slot = slot.reshape(blocks * rows, expert_count)
    turned = slot.reshape(NC, NY, -1)
    turned = jnp.stack(
        [lax.dynamic_index_in_dim(turned, (g - d) % NY, 1, keepdims=False) for d in range(NY)],
        axis=1,
    )
    turned = turned.reshape(blocks * rows, expert_count)
    weight = weight.reshape(blocks * rows, expert_count).T[:, None, :]
    count = NC * capacity
    flat = (expert_count * count, blocks * rows)
    picks, weights = [], []
    for micro in range(blocks // NC):
        slots = micro * count + jnp.arange(count, dtype=jnp.int32)[None, :, None]
        picks.append((turned.T[:, None, :] == slots).reshape(flat).astype(BF))
        weights.append(jnp.where(slot.T[:, None, :] == slots, weight, 0.0).reshape(flat))
    return picks, weights


def local(
    hidden_in,
    queries,
    latent_cache,
    cache_lengths,
    expert_ids,
    gate_values,
    norm_gain,
    value_up,
    out_proj,
    gate_up,
    down_proj,
):
    g, c = lax.axis_index("y"), lax.axis_index("c")
    first = c == 0
    micro, row_local, width = hidden_in.shape
    rows = micro * row_local
    part = rows // NY
    quarter, slim = width // NY, width // (NY * NC)
    k_dim, n_dim = out_proj.shape
    k_slice = k_dim // NX
    expert_count = NZ * NX
    top = expert_ids.shape[2]
    capacity = min(row_local, 4)

    x = lax.axis_index("x")
    place = jnp.stack([g, c, x]).astype(jnp.int32)
    wt = out_proj.T
    w_own = [lane_part(wt, x, k_slice)]
    w_own += [shift_x(lane_part(wt, (x + d) % NX, k_slice), d) for d in range(1, NX)]
    info = jnp.concatenate([g.astype(jnp.int32)[None], cache_lengths.reshape(rows)])

    ids_o, gates_o = swap_core(expert_ids), swap_core(gate_values)
    ids = jnp.concatenate(
        [jnp.where(first, expert_ids, ids_o), jnp.where(first, ids_o, expert_ids)]
    )
    gates = jnp.concatenate(
        [jnp.where(first, gate_values, gates_o), jnp.where(first, gates_o, gate_values)]
    )
    picks, weights = routing(ids, gates, expert_count, capacity, g)

    send = attend(
        info,
        queries.reshape((rows,) + queries.shape[2:]),
        latent_cache.transpose(0, 1, 3, 2).reshape((rows,) + latent_cache.shape[:1:-1]),
        value_up,
    )
    w_other = [swap_core(w) for w in w_own]
    down = [None] * NY

    def send_down(d, source):
        return shift_y(lane_part(source, (g + d) % NY, quarter), d)

    down_in, send = lax.optimization_barrier((down_proj[0], send))
    down[2] = send_down(2, down_in)
    got = lax.all_to_all(send, ("z", "x"), 0, 0, tiled=True)
    got, down[2] = lax.optimization_barrier((got, down[2]))
    parts = project(jnp.stack([x, c]).astype(jnp.int32), got, w_own, w_other)
    parts = [parts[0]] + [shift_y(parts[d], d) for d in range(1, NY)]
    spread = sum(p.astype(F32) for p in parts).astype(BF)
    back = lax.all_to_all(
        spread.reshape(NZ * NX, part, NX * NC * n_dim), ("z", "x"), 0, 0, tiled=True
    )
    pieces = norm(place, back, hidden_in)
    pieces = [pieces[0]] + [shift_y(pieces[d], d) for d in range(1, NY)]
    keep, give = scale_rows(place, norm_gain[None, :], pieces)
    took = swap_core(give)
    chip_rows = jnp.concatenate([jnp.where(first, keep, took), jnp.where(first, took, keep)])
    slots = NC * capacity
    outgoing = [jnp.dot(pick, chip_rows, preferred_element_type=F32).astype(BF) for pick in picks]
    down_in, gate_up, *outgoing = lax.optimization_barrier((down_proj[0], gate_up, *outgoing))
    gu = gate_up[0].reshape(quarter, -1)
    down[0] = lane_part(down_in, g, quarter)
    down[1], down[3] = send_down(1, down_in), send_down(3, down_in)

    def across(a):
        return lax.all_to_all(
            a.reshape(expert_count, slots, slim), ("z", "x"), 0, 0, tiled=True
        ).reshape(expert_count * slots, slim)

    received = [across(outgoing[0])]
    received[0], outgoing[1], gu, *down = lax.optimization_barrier(
        (received[0], outgoing[1], gu, *down)
    )
    received.append(across(outgoing[1]))
    mix = 0.0
    for m in range(micro):
        other = swap_core(received[m])
        own_sum = gate_up_dot(place, 0, received[m], gu)
        parts = gate_up_dot(place, 1, other, gu, own_sum)
        parts = [parts[0]] + [shift_y(parts[d], d) for d in range(1, NY)]
        total = sum(p.astype(F32) for p in parts)
        units = total.shape[1] // 2
        act = (jax.nn.silu(total[:, :units]) * total[:, units:]).astype(BF)
        acts = gather_y(act)
        give_r = down_dot(place, 1, acts, down, BF)
        keep_r = down_dot(place, 0, acts, down, F32)
        returned = across((keep_r + swap_core(give_r).astype(F32)).astype(BF))
        high = weights[m].astype(BF)
        low = (weights[m] - high.astype(F32)).astype(BF)
        both = lax.dot_general(
            jnp.concatenate([high, low], axis=1),
            returned,
            (((0,), (0,)), ((), ())),
            preferred_element_type=F32,
        )
        mix = mix + both[: NC * rows] + both[NC * rows :]
    mix_keep = jnp.where(first, mix[:rows], mix[rows:])
    mix_give = jnp.where(first, mix[rows:], mix[:rows])
    mix_took = swap_core(mix_give)
    mix_q = jnp.concatenate(
        [jnp.where(first, mix_keep, mix_took), jnp.where(first, mix_took, mix_keep)], axis=1
    )
    residual_q = absolute([p[:, :quarter] for p in pieces], g).reshape(rows, quarter)
    out_q = (residual_q + mix_q).astype(BF)
    return join(place, gather_y(out_q), hidden_in.shape)


def solution(mesh):
    fine = Mesh(mesh.devices.reshape(NY, NZ, NX, NC), ("y", "z", "x", "c"))
    ep = ("z", "x", "c")
    return jax.shard_map(
        local,
        mesh=fine,
        in_specs=(
            P(None, ep, None),
            P(None, ep, "y", None),
            P(None, ep, None, None),
            P(None, ep),
            P(None, ep, None),
            P(None, ep, None),
            P(),
            P("y", None, None),
            P("y", ep),
            P(ep, "y", None, None),
            P(ep, "y", None),
        ),
        out_specs=P(None, ep, None),
        check_vma=False,
    )
```

```python
import functools
import math

import jax
import jax.numpy as jnp
from jax import lax
from jax.experimental import pallas as pl
from jax.experimental.pallas import tpu as pltpu
from jax.sharding import Mesh
from jax.sharding import PartitionSpec as P

ROPE = 64
NOPE = 128
NY, NZ, NX, NC = 4, 8, 4, 2
BF = jnp.bfloat16
F32 = jnp.float32
LANES = 128


def attend_kernel(rows, heads, latent, info_ref, q_ref, cache_ref, up_ref, out_ref, held):
    step = pl.program_id(0)
    scale = 1.0 / math.sqrt(ROPE + NOPE)
    base = lax.rem(step + info_ref[0], NY) * rows
    for r in range(rows):
        cache = cache_ref[r]
        scores = jnp.dot(q_ref[r], cache, preferred_element_type=F32) * scale
        at = lax.broadcasted_iota(jnp.int32, scores.shape, 1)
        in_range = at < info_ref[1 + base + r]
        masked = jnp.where(in_range, scores, -1e30)
        peak = jnp.max(masked, axis=1, keepdims=True)
        exponent = jnp.where(in_range, jnp.exp(masked - peak), 0.0)
        weights = (exponent / jnp.sum(exponent, axis=1, keepdims=True)).astype(BF)
        held[step * rows + r] = lax.dot_general(
            weights, cache[:latent], (((1,), (1,)), ((), ())), preferred_element_type=F32
        )

    @pl.when(step == NY - 1)
    def _():
        group, vdim = heads // NX, up_ref.shape[2]
        for h in range(heads):
            value = jnp.dot(
                held[:, h, :].astype(BF), up_ref[h], preferred_element_type=F32
            ).astype(BF)
            lanes = slice(h % group * vdim, (h % group + 1) * vdim)
            for z in range(NZ):
                out_ref[z * NX + h // group, :, lanes] = value


def attend(info, queries, cache_t, value_up):
    all_rows, heads, key = queries.shape
    rows = all_rows // NY
    latent, vdim = value_up.shape[1:]
    length = cache_t.shape[2]
    shape = (NZ * NX, all_rows, heads * vdim // NX)
    turn = lambda i, info: (lax.rem(i + info[0], NY), 0, 0)
    return pl.pallas_call(
        functools.partial(attend_kernel, rows, heads, latent),
        grid_spec=pltpu.PrefetchScalarGridSpec(
            num_scalar_prefetch=1,
            grid=(NY,),
            in_specs=[
                pl.BlockSpec((rows, heads, key), turn),
                pl.BlockSpec((rows, key, length), turn),
                pl.BlockSpec(value_up.shape, lambda i, info: (0, 0, 0)),
            ],
            out_specs=pl.BlockSpec(shape, lambda i, info: (0, 0, 0)),
            scratch_shapes=[pltpu.VMEM((all_rows, heads, latent), F32)],
        ),
        out_shape=jax.ShapeDtypeStruct(shape, BF),
        compiler_params=pltpu.CompilerParams(vmem_limit_bytes=60 << 20),
        name="attend",
    )(info, queries, cache_t, value_up)


def project_kernel(place_ref, h_ref, *refs):
    own, other, outs, w_ref = refs[:NX], refs[NX : 2 * NX], refs[2 * NX : -1], refs[-1]
    sources, rows, depth = h_ref.shape
    for core in range(NC):

        @pl.when(place_ref[1] == core)
        def _():
            for x in range(NX):

                @pl.when(place_ref[0] == x)
                def _():
                    for dx in range(NX):
                        at = NC * ((x - dx) % NX)
                        w_ref[at + core] = own[dx][...]
                        w_ref[at + 1 - core] = other[dx][...]

    result = lax.dot_general(
        h_ref[...].reshape(sources * rows, depth),
        w_ref[...].reshape(-1, depth),
        (((1,), (1,)), ((), ())),
        preferred_element_type=F32,
    ).reshape(sources, rows, -1)
    part = rows // NY
    for d in range(NY):
        outs[d][...] = (
            result[:, d * part : (d + 1) * part, :].reshape(sources * part, -1).astype(BF)
        )


def project(place, values, own, other):
    sources, rows, depth = values.shape
    pieces = NX * NC
    n_dim = own[0].shape[0]
    vmem = pl.BlockSpec(memory_space=pltpu.VMEM)
    return pl.pallas_call(
        project_kernel,
        in_specs=[pl.BlockSpec(memory_space=pltpu.SMEM)] + [vmem] * (1 + 2 * NX),
        out_specs=[vmem] * NY,
        out_shape=[jax.ShapeDtypeStruct((sources * rows // NY, pieces * n_dim), BF)] * NY,
        scratch_shapes=[pltpu.VMEM((pieces, n_dim, depth), BF)],
        compiler_params=pltpu.CompilerParams(vmem_limit_bytes=32 << 20),
        name="project",
    )(place, values, *own, *other)


def norm_kernel(place_ref, back_ref, hidden_ref, *refs):
    outs, held_ref = refs[:NY], refs[NY]
    g = place_ref[0]
    rows, width = held_ref.shape
    segment = back_ref.shape[2]
    quarter = width // NY
    squares = jnp.zeros((rows, 1), F32)
    lower = lax.rem(g, 2) == 0
    for z in range(NZ):
        at = slice(z * segment, (z + 1) * segment)
        total = back_ref[z * NX].astype(F32)
        for x in range(1, NX):
            total += back_ref[z * NX + x].astype(F32)
        hidden = hidden_ref[lax.div(g, 2), :, at].astype(F32)
        total += jnp.where(lower, hidden[:rows], hidden[rows:])
        held_ref[:, at] = total
        squares += jnp.sum(total * total, axis=1, keepdims=True)
    scale = lax.rsqrt(squares / width + 1e-06)
    for d in range(NY):
        at = pl.ds(pl.multiple_of(lax.rem(g + d, NY) * quarter, quarter), quarter)
        outs[d][:, :quarter] = held_ref[:, at]
        outs[d][:, quarter:] = jnp.broadcast_to(scale, (rows, LANES))


def norm(place, back, hidden):
    micro, row_local, width = hidden.shape
    rows = micro * row_local // NY
    vmem = pl.BlockSpec(memory_space=pltpu.VMEM)
    return pl.pallas_call(
        norm_kernel,
        in_specs=[pl.BlockSpec(memory_space=pltpu.SMEM), vmem, vmem],
        out_specs=[vmem] * NY,
        out_shape=[jax.ShapeDtypeStruct((rows, width // NY + LANES), F32)] * NY,
        scratch_shapes=[pltpu.VMEM((rows, width), F32)],
        compiler_params=pltpu.CompilerParams(vmem_limit_bytes=8 << 20),
        name="norm",
    )(place, back, hidden)


def scale_kernel(place_ref, gain_ref, *refs):
    pieces, outs = refs[:NY], refs[NY:]
    slim = outs[0].shape[1]
    quarter = NC * slim
    for k in range(NC):
        start = lax.rem(place_ref[1] + k, NC) * slim
        gain = gain_ref[:, pl.ds(pl.multiple_of(place_ref[0] * quarter + start, LANES), slim)]
        at = pl.ds(pl.multiple_of(start, LANES), slim)
        rows = [p[:, at] * p[:, quarter : quarter + 1] * gain for p in pieces]
        outs[k][...] = jnp.concatenate(rows).astype(BF)


def scale_rows(place, gain, pieces):
    rows = NY * pieces[0].shape[0]
    slim = gain.shape[1] // (NY * NC)
    vmem = pl.BlockSpec(memory_space=pltpu.VMEM)
    return pl.pallas_call(
        scale_kernel,
        in_specs=[pl.BlockSpec(memory_space=pltpu.SMEM)] + [vmem] * (1 + NY),
        out_specs=[vmem] * NC,
        out_shape=[jax.ShapeDtypeStruct((rows, slim), BF)] * NC,
        compiler_params=pltpu.CompilerParams(vmem_limit_bytes=8 << 20),
        name="scale_rows",
    )(place, gain, *pieces)


def join_kernel(place_ref, *refs):
    pieces, out_ref = refs[:NY], refs[NY]
    quarter = pieces[0].shape[1]
    micro, rows = out_ref.shape[:2]
    for d in range(NY):
        at = lax.rem(place_ref[0] - d + NY, NY) * quarter
        for m in range(micro):
            out_ref[m, :, pl.ds(pl.multiple_of(at, quarter), quarter)] = pieces[d][
                m * rows : (m + 1) * rows, :
            ]


def join(place, pieces, shape):
    vmem = pl.BlockSpec(memory_space=pltpu.VMEM)
    return pl.pallas_call(
        join_kernel,
        in_specs=[pl.BlockSpec(memory_space=pltpu.SMEM)] + [vmem] * NY,
        out_specs=vmem,
        out_shape=jax.ShapeDtypeStruct(shape, BF),
        compiler_params=pltpu.CompilerParams(vmem_limit_bytes=8 << 20),
        name="join",
    )(place, *pieces)


def gate_up_kernel(place_ref, x_ref, w_ref, *refs):
    del place_ref
    refs[-1][...] = jnp.dot(x_ref[...], w_ref[...], preferred_element_type=F32)


def gate_up_last_kernel(units, place_ref, x_ref, w_ref, sum_ref, *refs):
    outs, acc_ref = refs[:NY], refs[NY]
    acc_ref[...] = sum_ref[...] + jnp.dot(x_ref[...], w_ref[...], preferred_element_type=F32)
    for d in range(NY):
        to = lax.rem(place_ref[0] + d, NY)
        for k in range(2):
            start = pl.multiple_of((k * NY + to) * units, units)
            outs[d][:, k * units : (k + 1) * units] = acc_ref[:, pl.ds(start, units)].astype(BF)


def gate_up_dot(place, half, x, w, before=None):
    count, depth = x.shape
    width = w.shape[1]
    units = width // (2 * NY)
    in_specs = [
        pl.BlockSpec((count, depth), lambda i, p: (0, 0)),
        pl.BlockSpec((depth, width), lambda i, p: (lax.rem(p[1] + half, NC), 0)),
    ]
    if before is None:
        body, operands, scratch = gate_up_kernel, (x, w), []
        out_specs = pl.BlockSpec((count, width), lambda i, p: (0, 0))
        out_shape = jax.ShapeDtypeStruct((count, width), F32)
    else:
        body, operands = functools.partial(gate_up_last_kernel, units), (x, w, before)
        scratch = [pltpu.VMEM((count, width), F32)]
        in_specs.append(pl.BlockSpec((count, width), lambda i, p: (0, 0)))
        out_specs = [pl.BlockSpec((count, 2 * units), lambda i, p: (0, 0))] * NY
        out_shape = [jax.ShapeDtypeStruct((count, 2 * units), BF)] * NY
    return pl.pallas_call(
        body,
        grid_spec=pltpu.PrefetchScalarGridSpec(
            num_scalar_prefetch=1,
            grid=(1,),
            in_specs=in_specs,
            out_specs=out_specs,
            scratch_shapes=scratch,
        ),
        out_shape=out_shape,
        compiler_params=pltpu.CompilerParams(vmem_limit_bytes=32 << 20),
        cost_estimate=pl.CostEstimate(
            flops=2 * count * depth * width, bytes_accessed=6 << 20, transcendentals=0
        ),
        name="gate_up",
    )(place, *operands)


def down_kernel(place_ref, *refs):
    del place_ref
    acts, downs, out_ref = refs[:NY], refs[NY : 2 * NY], refs[2 * NY]
    act = jnp.concatenate([a[...] for a in acts], axis=1)
    down = jnp.concatenate([w[...] for w in downs], axis=0)
    out_ref[...] = jnp.dot(act, down, preferred_element_type=F32).astype(out_ref.dtype)


def down_dot(place, half, acts, downs, dtype):
    count, units = acts[0].shape
    width = downs[0].shape[1] // NC
    return pl.pallas_call(
        down_kernel,
        grid_spec=pltpu.PrefetchScalarGridSpec(
            num_scalar_prefetch=1,
            grid=(1,),
            in_specs=[pl.BlockSpec((count, units), lambda i, p: (0, 0))] * NY
            + [pl.BlockSpec((units, width), lambda i, p: (0, lax.rem(p[1] + half, NC)))] * NY,
            out_specs=pl.BlockSpec((count, width), lambda i, p: (0, 0)),
        ),
        out_shape=jax.ShapeDtypeStruct((count, width), dtype),
        compiler_params=pltpu.CompilerParams(vmem_limit_bytes=32 << 20),
        cost_estimate=pl.CostEstimate(
            flops=2 * count * units * NY * width, bytes_accessed=3 << 20, transcendentals=0
        ),
        name="down",
    )(place, *acts, *downs)


def swap_core(a):
    return lax.ppermute(a, "c", [(0, 1), (1, 0)])


def shift_y(a, d):
    return lax.ppermute(a, "y", [(i, (i + d) % NY) for i in range(NY)])


def shift_x(a, d):
    return lax.ppermute(a, "x", [(i, (i + d) % NX) for i in range(NX)])


def lane_part(a, index, size):
    return lax.dynamic_slice_in_dim(a, index * size, size, 1)


def gather_y(a):
    return [a] + [shift_y(a, d) for d in range(1, NY)]


def absolute(items, g):
    back = [items[(-j) % NY] for j in range(NY)]
    return lax.dynamic_slice_in_dim(jnp.stack(back + back[: NY - 1]), (NY - g) % NY, NY, 0)


def routing(ids, gates, expert_count, capacity, g, first):
    blocks, rows, top = ids.shape
    hot = ids[..., None] == jnp.arange(expert_count, dtype=jnp.int32)
    chosen = jnp.any(hot, axis=2)
    weight = jnp.sum(jnp.where(hot, gates[..., None], 0.0), axis=2)
    counts = chosen.astype(jnp.int32)
    place = jnp.cumsum(counts, axis=1) - counts
    block = jnp.broadcast_to(jnp.arange(blocks, dtype=jnp.int32)[:, None, None], place.shape)
    slot = jnp.where(chosen, block * capacity + place, -1).reshape(blocks * rows, expert_count)
    slots = jnp.arange(blocks * capacity, dtype=jnp.int32)[None, :, None]
    flat = (expert_count * blocks * capacity, blocks * rows)
    weight = weight.reshape(blocks * rows, expert_count).T[:, None, :]
    weights = jnp.where(slot.T[:, None, :] == slots, weight, 0.0).reshape(flat)
    turned = slot.reshape(NC, NY, -1)
    turned = jnp.where(first, turned, turned[::-1])
    turned = jnp.stack(
        [lax.dynamic_index_in_dim(turned, (g - d) % NY, 1, keepdims=False) for d in range(NY)],
        axis=1,
    )
    turned = turned.reshape(blocks * rows, expert_count)
    pick = (turned.T[:, None, :] == slots).reshape(flat).astype(BF)
    return pick, weights


def local(
    hidden_in,
    queries,
    latent_cache,
    cache_lengths,
    expert_ids,
    gate_values,
    norm_gain,
    value_up,
    out_proj,
    gate_up,
    down_proj,
):
    g, c = lax.axis_index("y"), lax.axis_index("c")
    first = c == 0
    micro, row_local, width = hidden_in.shape
    rows = micro * row_local
    part = rows // NY
    quarter, slim = width // NY, width // (NY * NC)
    k_dim, n_dim = out_proj.shape
    k_slice = k_dim // NX
    expert_count = NZ * NX
    top = expert_ids.shape[2]
    capacity = min(row_local, 4)

    x = lax.axis_index("x")
    place = jnp.stack([g, c, x]).astype(jnp.int32)
    wt = out_proj.T
    w_own = [lane_part(wt, x, k_slice)]
    w_own += [shift_x(lane_part(wt, (x + d) % NX, k_slice), d) for d in range(1, NX)]
    info = jnp.concatenate([g.astype(jnp.int32)[None], cache_lengths.reshape(rows)])

    ids_o, gates_o = swap_core(expert_ids), swap_core(gate_values)
    ids = jnp.concatenate(
        [jnp.where(first, expert_ids, ids_o), jnp.where(first, ids_o, expert_ids)]
    )
    gates = jnp.concatenate(
        [jnp.where(first, gate_values, gates_o), jnp.where(first, gates_o, gate_values)]
    )
    pick, weights = routing(ids, gates, expert_count, capacity, g, first)

    send = attend(
        info,
        queries.reshape((rows,) + queries.shape[2:]),
        latent_cache.transpose(0, 1, 3, 2).reshape((rows,) + latent_cache.shape[:1:-1]),
        value_up,
    )
    w_other = [swap_core(w) for w in w_own]
    got = lax.all_to_all(send, ("z", "x"), 0, 0, tiled=True)
    parts = project(jnp.stack([x, c]).astype(jnp.int32), got, w_own, w_other)
    parts = [parts[0]] + [shift_y(parts[d], d) for d in range(1, NY)]
    spread = sum(p.astype(F32) for p in parts).astype(BF)
    back = lax.all_to_all(
        spread.reshape(NZ * NX, part, NX * NC * n_dim), ("z", "x"), 0, 0, tiled=True
    )
    pieces = norm(place, back, hidden_in)
    pieces = [pieces[0]] + [shift_y(pieces[d], d) for d in range(1, NY)]
    keep, give = scale_rows(place, norm_gain[None, :], pieces)
    took = swap_core(give)
    chip_rows = jnp.concatenate([keep, took])
    outgoing = jnp.dot(pick, chip_rows, preferred_element_type=F32).astype(BF)
    slots = NC * micro * capacity
    down_in, gate_up, outgoing = lax.optimization_barrier((down_proj[0], gate_up, outgoing))
    gu = gate_up[0].reshape(quarter, -1)
    down = [lane_part(down_in, g, quarter)]
    down += [shift_y(lane_part(down_in, (g + d) % NY, quarter), d) for d in range(1, NY)]
    received = lax.all_to_all(
        outgoing.reshape(expert_count, slots, slim), ("z", "x"), 0, 0, tiled=True
    ).reshape(expert_count * slots, slim)
    received, gu, weights, *down = lax.optimization_barrier((received, gu, weights, *down))
    other = swap_core(received)
    own_sum = gate_up_dot(place, 0, received, gu)
    parts = gate_up_dot(place, 1, other, gu, own_sum)
    parts = [parts[0]] + [shift_y(parts[d], d) for d in range(1, NY)]
    total = sum(p.astype(F32) for p in parts)
    units = total.shape[1] // 2
    act = (jax.nn.silu(total[:, :units]) * total[:, units:]).astype(BF)
    acts = gather_y(act)
    give_r = down_dot(place, 1, acts, down, BF)
    keep_r = down_dot(place, 0, acts, down, F32)
    whole = (keep_r + swap_core(give_r).astype(F32)).astype(BF)
    returned = lax.all_to_all(
        whole.reshape(expert_count, slots, slim), ("z", "x"), 0, 0, tiled=True
    ).reshape(expert_count * slots, slim)
    high = weights.astype(BF)
    low = (weights - high.astype(F32)).astype(BF)
    both = lax.dot_general(
        jnp.concatenate([high, low], axis=1),
        returned,
        (((0,), (0,)), ((), ())),
        preferred_element_type=F32,
    )
    mix = both[: NC * rows] + both[NC * rows :]
    mix_keep = jnp.where(first, mix[:rows], mix[rows:])
    mix_give = jnp.where(first, mix[rows:], mix[:rows])
    mix_took = swap_core(mix_give)
    mix_q = jnp.concatenate(
        [jnp.where(first, mix_keep, mix_took), jnp.where(first, mix_took, mix_keep)], axis=1
    )
    residual_q = absolute([p[:, :quarter] for p in pieces], g).reshape(rows, quarter)
    out_q = (residual_q + mix_q).astype(BF)
    return join(place, gather_y(out_q), hidden_in.shape)


def solution(mesh):
    fine = Mesh(mesh.devices.reshape(NY, NZ, NX, NC), ("y", "z", "x", "c"))
    ep = ("z", "x", "c")
    return jax.shard_map(
        local,
        mesh=fine,
        in_specs=(
            P(None, ep, None),
            P(None, ep, "y", None),
            P(None, ep, None, None),
            P(None, ep),
            P(None, ep, None),
            P(None, ep, None),
            P(),
            P("y", None, None),
            P("y", ep),
            P(ep, "y", None, None),
            P(ep, "y", None),
        ),
        out_specs=P(None, ep, None),
        check_vma=False,
    )
```

```python
import functools
import math

import jax
import jax.numpy as jnp
from jax import lax
from jax.experimental import pallas as pl
from jax.experimental.pallas import tpu as pltpu
from jax.sharding import Mesh
from jax.sharding import PartitionSpec as P

ROPE = 64
NOPE = 128
NY, NZ, NX, NC = 4, 8, 4, 2
BF = jnp.bfloat16
F32 = jnp.float32
LANES = 128


def attend_kernel(rows, heads, latent, info_ref, q_ref, cache_ref, up_ref, out_ref, held):
    step = pl.program_id(0)
    scale = 1.0 / math.sqrt(ROPE + NOPE)
    base = lax.rem(step + info_ref[0], NY) * rows
    for r in range(rows):
        cache = cache_ref[r]
        scores = jnp.dot(q_ref[r], cache, preferred_element_type=F32) * scale
        at = lax.broadcasted_iota(jnp.int32, scores.shape, 1)
        in_range = at < info_ref[1 + base + r]
        masked = jnp.where(in_range, scores, -1e30)
        peak = jnp.max(masked, axis=1, keepdims=True)
        exponent = jnp.where(in_range, jnp.exp(masked - peak), 0.0)
        weights = (exponent / jnp.sum(exponent, axis=1, keepdims=True)).astype(BF)
        held[step * rows + r] = lax.dot_general(
            weights, cache[:latent], (((1,), (1,)), ((), ())), preferred_element_type=F32
        )

    @pl.when(step == NY - 1)
    def _():
        group, vdim = heads // NX, up_ref.shape[2]
        for h in range(heads):
            value = jnp.dot(
                held[:, h, :].astype(BF), up_ref[h], preferred_element_type=F32
            ).astype(BF)
            lanes = slice(h % group * vdim, (h % group + 1) * vdim)
            for z in range(NZ):
                out_ref[z * NX + h // group, :, lanes] = value


def attend(info, queries, cache_t, value_up):
    all_rows, heads, key = queries.shape
    rows = all_rows // NY
    latent, vdim = value_up.shape[1:]
    length = cache_t.shape[2]
    shape = (NZ * NX, all_rows, heads * vdim // NX)
    turn = lambda i, info: (lax.rem(i + info[0], NY), 0, 0)
    return pl.pallas_call(
        functools.partial(attend_kernel, rows, heads, latent),
        grid_spec=pltpu.PrefetchScalarGridSpec(
            num_scalar_prefetch=1,
            grid=(NY,),
            in_specs=[
                pl.BlockSpec((rows, heads, key), turn),
                pl.BlockSpec((rows, key, length), turn),
                pl.BlockSpec(value_up.shape, lambda i, info: (0, 0, 0)),
            ],
            out_specs=pl.BlockSpec(shape, lambda i, info: (0, 0, 0)),
            scratch_shapes=[pltpu.VMEM((all_rows, heads, latent), F32)],
        ),
        out_shape=jax.ShapeDtypeStruct(shape, BF),
        compiler_params=pltpu.CompilerParams(vmem_limit_bytes=60 << 20),
        name="attend",
    )(info, queries, cache_t, value_up)


def project_kernel(place_ref, h_ref, *refs):
    own, other, outs, w_ref = refs[:NX], refs[NX : 2 * NX], refs[2 * NX : -1], refs[-1]
    sources, rows, depth = h_ref.shape
    for core in range(NC):

        @pl.when(place_ref[1] == core)
        def _():
            for x in range(NX):

                @pl.when(place_ref[0] == x)
                def _():
                    for dx in range(NX):
                        at = NC * ((x - dx) % NX)
                        w_ref[at + core] = own[dx][...]
                        w_ref[at + 1 - core] = other[dx][...]

    result = lax.dot_general(
        h_ref[...].reshape(sources * rows, depth),
        w_ref[...].reshape(-1, depth),
        (((1,), (1,)), ((), ())),
        preferred_element_type=F32,
    ).reshape(sources, rows, -1)
    part = rows // NY
    for d in range(NY):
        outs[d][...] = (
            result[:, d * part : (d + 1) * part, :].reshape(sources * part, -1).astype(BF)
        )


def project(place, values, own, other):
    sources, rows, depth = values.shape
    pieces = NX * NC
    n_dim = own[0].shape[0]
    vmem = pl.BlockSpec(memory_space=pltpu.VMEM)
    return pl.pallas_call(
        project_kernel,
        in_specs=[pl.BlockSpec(memory_space=pltpu.SMEM)] + [vmem] * (1 + 2 * NX),
        out_specs=[vmem] * NY,
        out_shape=[jax.ShapeDtypeStruct((sources * rows // NY, pieces * n_dim), BF)] * NY,
        scratch_shapes=[pltpu.VMEM((pieces, n_dim, depth), BF)],
        compiler_params=pltpu.CompilerParams(vmem_limit_bytes=32 << 20),
        name="project",
    )(place, values, *own, *other)


def norm_kernel(place_ref, back_ref, hidden_ref, *refs):
    outs, held_ref = refs[:NY], refs[NY]
    g = place_ref[0]
    rows, width = held_ref.shape
    segment = back_ref.shape[2]
    quarter = width // NY
    squares = jnp.zeros((rows, 1), F32)
    lower = lax.rem(g, 2) == 0
    for z in range(NZ):
        at = slice(z * segment, (z + 1) * segment)
        total = back_ref[z * NX].astype(F32)
        for x in range(1, NX):
            total += back_ref[z * NX + x].astype(F32)
        hidden = hidden_ref[lax.div(g, 2), :, at].astype(F32)
        total += jnp.where(lower, hidden[:rows], hidden[rows:])
        held_ref[:, at] = total
        squares += jnp.sum(total * total, axis=1, keepdims=True)
    scale = lax.rsqrt(squares / width + 1e-06)
    for d in range(NY):
        at = pl.ds(pl.multiple_of(lax.rem(g + d, NY) * quarter, quarter), quarter)
        outs[d][:, :quarter] = held_ref[:, at]
        outs[d][:, quarter:] = jnp.broadcast_to(scale, (rows, LANES))


def norm(place, back, hidden):
    micro, row_local, width = hidden.shape
    rows = micro * row_local // NY
    vmem = pl.BlockSpec(memory_space=pltpu.VMEM)
    return pl.pallas_call(
        norm_kernel,
        in_specs=[pl.BlockSpec(memory_space=pltpu.SMEM), vmem, vmem],
        out_specs=[vmem] * NY,
        out_shape=[jax.ShapeDtypeStruct((rows, width // NY + LANES), F32)] * NY,
        scratch_shapes=[pltpu.VMEM((rows, width), F32)],
        compiler_params=pltpu.CompilerParams(vmem_limit_bytes=8 << 20),
        name="norm",
    )(place, back, hidden)


def scale_kernel(place_ref, gain_ref, *refs):
    pieces, outs = refs[:NY], refs[NY:]
    slim = outs[0].shape[1]
    quarter = NC * slim
    for k in range(NC):
        start = lax.rem(place_ref[1] + k, NC) * slim
        gain = gain_ref[:, pl.ds(pl.multiple_of(place_ref[0] * quarter + start, LANES), slim)]
        at = pl.ds(pl.multiple_of(start, LANES), slim)
        rows = [p[:, at] * p[:, quarter : quarter + 1] * gain for p in pieces]
        outs[k][...] = jnp.concatenate(rows).astype(BF)


def scale_rows(place, gain, pieces):
    rows = NY * pieces[0].shape[0]
    slim = gain.shape[1] // (NY * NC)
    vmem = pl.BlockSpec(memory_space=pltpu.VMEM)
    return pl.pallas_call(
        scale_kernel,
        in_specs=[pl.BlockSpec(memory_space=pltpu.SMEM)] + [vmem] * (1 + NY),
        out_specs=[vmem] * NC,
        out_shape=[jax.ShapeDtypeStruct((rows, slim), BF)] * NC,
        compiler_params=pltpu.CompilerParams(vmem_limit_bytes=8 << 20),
        name="scale_rows",
    )(place, gain, *pieces)


def join_kernel(place_ref, *refs):
    pieces, out_ref = refs[:NY], refs[NY]
    quarter = pieces[0].shape[1]
    micro, rows = out_ref.shape[:2]
    for d in range(NY):
        at = lax.rem(place_ref[0] - d + NY, NY) * quarter
        for m in range(micro):
            out_ref[m, :, pl.ds(pl.multiple_of(at, quarter), quarter)] = pieces[d][
                m * rows : (m + 1) * rows, :
            ]


def join(place, pieces, shape):
    vmem = pl.BlockSpec(memory_space=pltpu.VMEM)
    return pl.pallas_call(
        join_kernel,
        in_specs=[pl.BlockSpec(memory_space=pltpu.SMEM)] + [vmem] * NY,
        out_specs=vmem,
        out_shape=jax.ShapeDtypeStruct(shape, BF),
        compiler_params=pltpu.CompilerParams(vmem_limit_bytes=8 << 20),
        name="join",
    )(place, *pieces)


def gate_up_kernel(place_ref, x_ref, w_ref, *refs):
    del place_ref
    refs[-1][...] = jnp.dot(x_ref[...], w_ref[...], preferred_element_type=F32)


def gate_up_last_kernel(units, place_ref, x_ref, w_ref, sum_ref, *refs):
    outs, acc_ref = refs[:NY], refs[NY]
    acc_ref[...] = sum_ref[...] + jnp.dot(x_ref[...], w_ref[...], preferred_element_type=F32)
    for d in range(NY):
        to = lax.rem(place_ref[0] + d, NY)
        for k in range(2):
            start = pl.multiple_of((k * NY + to) * units, units)
            outs[d][:, k * units : (k + 1) * units] = acc_ref[:, pl.ds(start, units)].astype(BF)


def gate_up_dot(place, x, w, before=None):
    count, depth = x.shape
    width = w.shape[1]
    units = width // (2 * NY)
    in_specs = [
        pl.BlockSpec((count, depth), lambda i, p: (0, 0)),
        pl.BlockSpec((depth, width), lambda i, p: (0, 0)),
    ]
    if before is None:
        body, operands, scratch = gate_up_kernel, (x, w), []
        out_specs = pl.BlockSpec((count, width), lambda i, p: (0, 0))
        out_shape = jax.ShapeDtypeStruct((count, width), F32)
    else:
        body, operands = functools.partial(gate_up_last_kernel, units), (x, w, before)
        scratch = [pltpu.VMEM((count, width), F32)]
        in_specs.append(pl.BlockSpec((count, width), lambda i, p: (0, 0)))
        out_specs = [pl.BlockSpec((count, 2 * units), lambda i, p: (0, 0))] * NY
        out_shape = [jax.ShapeDtypeStruct((count, 2 * units), BF)] * NY
    return pl.pallas_call(
        body,
        grid_spec=pltpu.PrefetchScalarGridSpec(
            num_scalar_prefetch=1,
            grid=(1,),
            in_specs=in_specs,
            out_specs=out_specs,
            scratch_shapes=scratch,
        ),
        out_shape=out_shape,
        compiler_params=pltpu.CompilerParams(vmem_limit_bytes=32 << 20),
        cost_estimate=pl.CostEstimate(
            flops=2 * count * depth * width, bytes_accessed=6 << 20, transcendentals=0
        ),
        name="gate_up",
    )(place, *operands)


def down_kernel(place_ref, *refs):
    del place_ref
    acts, downs, out_ref = refs[:NY], refs[NY : 2 * NY], refs[2 * NY]
    act = jnp.concatenate([a[...] for a in acts], axis=1)
    down = jnp.concatenate([w[...] for w in downs], axis=0)
    out_ref[...] = jnp.dot(act, down, preferred_element_type=F32).astype(out_ref.dtype)


def down_dot(place, half, acts, downs, dtype):
    count, units = acts[0].shape
    width = downs[0].shape[1] // NC
    return pl.pallas_call(
        down_kernel,
        grid_spec=pltpu.PrefetchScalarGridSpec(
            num_scalar_prefetch=1,
            grid=(1,),
            in_specs=[pl.BlockSpec((count, units), lambda i, p: (0, 0))] * NY
            + [pl.BlockSpec((units, width), lambda i, p: (0, lax.rem(p[1] + half, NC)))] * NY,
            out_specs=pl.BlockSpec((count, width), lambda i, p: (0, 0)),
        ),
        out_shape=jax.ShapeDtypeStruct((count, width), dtype),
        compiler_params=pltpu.CompilerParams(vmem_limit_bytes=32 << 20),
        cost_estimate=pl.CostEstimate(
            flops=2 * count * units * NY * width, bytes_accessed=3 << 20, transcendentals=0
        ),
        name="down",
    )(place, *acts, *downs)


def swap_core(a):
    return lax.ppermute(a, "c", [(0, 1), (1, 0)])


def shift_y(a, d):
    return lax.ppermute(a, "y", [(i, (i + d) % NY) for i in range(NY)])


def shift_x(a, d):
    return lax.ppermute(a, "x", [(i, (i + d) % NX) for i in range(NX)])


def lane_part(a, index, size):
    return lax.dynamic_slice_in_dim(a, index * size, size, 1)


def gather_y(a):
    return [a] + [shift_y(a, d) for d in range(1, NY)]


def absolute(items, g):
    back = [items[(-j) % NY] for j in range(NY)]
    return lax.dynamic_slice_in_dim(jnp.stack(back + back[: NY - 1]), (NY - g) % NY, NY, 0)


def routing(ids, gates, expert_count, capacity, g, first):
    blocks, rows, top = ids.shape
    hot = ids[..., None] == jnp.arange(expert_count, dtype=jnp.int32)
    chosen = jnp.any(hot, axis=2)
    weight = jnp.sum(jnp.where(hot, gates[..., None], 0.0), axis=2)
    counts = chosen.astype(jnp.int32)
    place = jnp.cumsum(counts, axis=1) - counts
    block = jnp.broadcast_to(jnp.arange(blocks, dtype=jnp.int32)[:, None, None], place.shape)
    slot = jnp.where(chosen, block * capacity + place, -1).reshape(blocks * rows, expert_count)
    slots = jnp.arange(blocks * capacity, dtype=jnp.int32)[None, :, None]
    flat = (expert_count * blocks * capacity, blocks * rows)
    weight = weight.reshape(blocks * rows, expert_count).T[:, None, :]
    weights = jnp.where(slot.T[:, None, :] == slots, weight, 0.0).reshape(flat)
    turned = slot.reshape(NC, NY, -1)
    turned = jnp.where(first, turned, turned[::-1])
    turned = jnp.stack(
        [lax.dynamic_index_in_dim(turned, (g - d) % NY, 1, keepdims=False) for d in range(NY)],
        axis=1,
    )
    turned = turned.reshape(blocks * rows, expert_count)
    pick = (turned.T[:, None, :] == slots).reshape(flat).astype(BF)
    return pick, weights


def local(
    hidden_in,
    queries,
    latent_cache,
    cache_lengths,
    expert_ids,
    gate_values,
    norm_gain,
    value_up,
    out_proj,
    gate_up,
    down_proj,
):
    g, c = lax.axis_index("y"), lax.axis_index("c")
    first = c == 0
    micro, row_local, width = hidden_in.shape
    rows = micro * row_local
    part = rows // NY
    quarter, slim = width // NY, width // (NY * NC)
    k_dim, n_dim = out_proj.shape
    k_slice = k_dim // NX
    expert_count = NZ * NX
    top = expert_ids.shape[2]
    capacity = min(row_local, 4)

    x = lax.axis_index("x")
    place = jnp.stack([g, c, x]).astype(jnp.int32)
    wt = out_proj.T
    w_own = [lane_part(wt, x, k_slice)]
    w_own += [shift_x(lane_part(wt, (x + d) % NX, k_slice), d) for d in range(1, NX)]
    info = jnp.concatenate([g.astype(jnp.int32)[None], cache_lengths.reshape(rows)])

    ids_o, gates_o = swap_core(expert_ids), swap_core(gate_values)
    ids = jnp.concatenate(
        [jnp.where(first, expert_ids, ids_o), jnp.where(first, ids_o, expert_ids)]
    )
    gates = jnp.concatenate(
        [jnp.where(first, gate_values, gates_o), jnp.where(first, gates_o, gate_values)]
    )
    pick, weights = routing(ids, gates, expert_count, capacity, g, first)

    send = attend(
        info,
        queries.reshape((rows,) + queries.shape[2:]),
        latent_cache.transpose(0, 1, 3, 2).reshape((rows,) + latent_cache.shape[:1:-1]),
        value_up,
    )
    w_other = [swap_core(w) for w in w_own]
    down = [None] * NY

    def send_down(d, source):
        return shift_y(lane_part(source, (g + d) % NY, quarter), d)

    down_in, send = lax.optimization_barrier((down_proj[0], send))
    down[2] = send_down(2, down_in)
    got = lax.all_to_all(send, ("z", "x"), 0, 0, tiled=True)
    got, down[2] = lax.optimization_barrier((got, down[2]))
    parts = project(jnp.stack([x, c]).astype(jnp.int32), got, w_own, w_other)
    parts = [parts[0]] + [shift_y(parts[d], d) for d in range(1, NY)]
    spread = sum(p.astype(F32) for p in parts).astype(BF)
    back = lax.all_to_all(
        spread.reshape(NZ * NX, part, NX * NC * n_dim), ("z", "x"), 0, 0, tiled=True
    )
    pieces = norm(place, back, hidden_in)
    pieces = [pieces[0]] + [shift_y(pieces[d], d) for d in range(1, NY)]
    keep, give = scale_rows(place, norm_gain[None, :], pieces)
    took = swap_core(give)
    chip_rows = jnp.concatenate([keep, took])
    outgoing = jnp.dot(pick, chip_rows, preferred_element_type=F32).astype(BF)
    slots = NC * micro * capacity
    down_in, gate_up, outgoing = lax.optimization_barrier((down_proj[0], gate_up, outgoing))
    gu = [
        lax.dynamic_slice_in_dim(gate_up[0], (c + k) % NC * slim, slim, 0).reshape(slim, -1)
        for k in range(NC)
    ]
    down[0] = lane_part(down_in, g, quarter)
    down[1], down[3] = send_down(1, down_in), send_down(3, down_in)
    received = lax.all_to_all(
        outgoing.reshape(expert_count, slots, slim), ("z", "x"), 0, 0, tiled=True
    ).reshape(expert_count * slots, slim)
    received, gu, weights, down = lax.optimization_barrier((received, gu, weights, down))
    other = swap_core(received)
    own_sum = gate_up_dot(place, received, gu[0])
    parts = gate_up_dot(place, other, gu[1], own_sum)
    parts = [parts[0]] + [shift_y(parts[d], d) for d in range(1, NY)]
    total = sum(p.astype(F32) for p in parts)
    units = total.shape[1] // 2
    act = (jax.nn.silu(total[:, :units]) * total[:, units:]).astype(BF)
    acts = gather_y(act)
    give_r = down_dot(place, 1, acts, down, BF)
    keep_r = down_dot(place, 0, acts, down, F32)
    whole = (keep_r + swap_core(give_r).astype(F32)).astype(BF)
    returned = lax.all_to_all(
        whole.reshape(expert_count, slots, slim), ("z", "x"), 0, 0, tiled=True
    ).reshape(expert_count * slots, slim)
    high = weights.astype(BF)
    low = (weights - high.astype(F32)).astype(BF)
    both = lax.dot_general(
        jnp.concatenate([high, low], axis=1),
        returned,
        (((0,), (0,)), ((), ())),
        preferred_element_type=F32,
    )
    mix = both[: NC * rows] + both[NC * rows :]
    mix_keep = jnp.where(first, mix[:rows], mix[rows:])
    mix_give = jnp.where(first, mix[rows:], mix[:rows])
    mix_took = swap_core(mix_give)
    mix_q = jnp.concatenate(
        [jnp.where(first, mix_keep, mix_took), jnp.where(first, mix_took, mix_keep)], axis=1
    )
    residual_q = absolute([p[:, :quarter] for p in pieces], g).reshape(rows, quarter)
    out_q = (residual_q + mix_q).astype(BF)
    return join(place, gather_y(out_q), hidden_in.shape)


def solution(mesh):
    fine = Mesh(mesh.devices.reshape(NY, NZ, NX, NC), ("y", "z", "x", "c"))
    ep = ("z", "x", "c")
    return jax.shard_map(
        local,
        mesh=fine,
        in_specs=(
            P(None, ep, None),
            P(None, ep, "y", None),
            P(None, ep, None, None),
            P(None, ep),
            P(None, ep, None),
            P(None, ep, None),
            P(),
            P("y", None, None),
            P("y", ep),
            P(ep, "y", None, None),
            P(ep, "y", None),
        ),
        out_specs=P(None, ep, None),
        check_vma=False,
    )
```

```python
import functools
import math

import jax
import jax.numpy as jnp
from jax import lax
from jax.experimental import pallas as pl
from jax.experimental.pallas import tpu as pltpu
from jax.sharding import Mesh
from jax.sharding import PartitionSpec as P

ROPE = 64
NOPE = 128
NY, NZ, NX, NC = 4, 8, 4, 2
BF = jnp.bfloat16
F32 = jnp.float32
LANES = 128


def attend_kernel(rows, heads, latent, place_ref, length_ref, q_ref, cache_ref, up_ref, out_ref, held):
    step = pl.program_id(0)
    scale = 1.0 / math.sqrt(ROPE + NOPE)
    base = lax.rem(step + place_ref[0], NY) * rows
    micro, base = lax.div(base, length_ref.shape[1]), lax.rem(base, length_ref.shape[1])
    for r in range(rows):
        cache = cache_ref[r]
        scores = jnp.dot(q_ref[r], cache, preferred_element_type=F32) * scale
        at = lax.broadcasted_iota(jnp.int32, scores.shape, 1)
        in_range = at < length_ref[micro, base + r]
        masked = jnp.where(in_range, scores, -1e30)
        peak = jnp.max(masked, axis=1, keepdims=True)
        exponent = jnp.where(in_range, jnp.exp(masked - peak), 0.0)
        weights = (exponent / jnp.sum(exponent, axis=1, keepdims=True)).astype(BF)
        held[step * rows + r] = lax.dot_general(
            weights, cache[:latent], (((1,), (1,)), ((), ())), preferred_element_type=F32
        )

    @pl.when(step == NY - 1)
    def _():
        group, vdim = heads // NX, up_ref.shape[2]
        for h in range(heads):
            value = jnp.dot(
                held[:, h, :].astype(BF), up_ref[h], preferred_element_type=F32
            ).astype(BF)
            lanes = slice(h % group * vdim, (h % group + 1) * vdim)
            for z in range(NZ):
                out_ref[z * NX + h // group, :, lanes] = value


def attend(place, lengths, queries, cache_t, value_up):
    all_rows, heads, key = queries.shape
    rows = all_rows // NY
    latent, vdim = value_up.shape[1:]
    length = cache_t.shape[2]
    shape = (NZ * NX, all_rows, heads * vdim // NX)
    turn = lambda i, place, lengths: (lax.rem(i + place[0], NY), 0, 0)
    return pl.pallas_call(
        functools.partial(attend_kernel, rows, heads, latent),
        grid_spec=pltpu.PrefetchScalarGridSpec(
            num_scalar_prefetch=2,
            grid=(NY,),
            in_specs=[
                pl.BlockSpec((rows, heads, key), turn),
                pl.BlockSpec((rows, key, length), turn),
                pl.BlockSpec(value_up.shape, lambda i, place, lengths: (0, 0, 0)),
            ],
            out_specs=pl.BlockSpec(shape, lambda i, place, lengths: (0, 0, 0)),
            scratch_shapes=[pltpu.VMEM((all_rows, heads, latent), F32)],
        ),
        out_shape=jax.ShapeDtypeStruct(shape, BF),
        compiler_params=pltpu.CompilerParams(vmem_limit_bytes=60 << 20),
        name="attend",
    )(place, lengths, queries, cache_t, value_up)


def project_kernel(place_ref, h_ref, *refs):
    own, other, outs, w_ref = refs[:NX], refs[NX : 2 * NX], refs[2 * NX : -1], refs[-1]
    sources, rows, depth = h_ref.shape
    for core in range(NC):

        @pl.when(place_ref[1] == core)
        def _():
            for x in range(NX):

                @pl.when(place_ref[0] == x)
                def _():
                    for dx in range(NX):
                        at = NC * ((x - dx) % NX)
                        w_ref[at + core] = own[dx][...]
                        w_ref[at + 1 - core] = other[dx][...]

    result = lax.dot_general(
        h_ref[...].reshape(sources * rows, depth),
        w_ref[...].reshape(-1, depth),
        (((1,), (1,)), ((), ())),
        preferred_element_type=F32,
    ).reshape(sources, rows, -1)
    part = rows // NY
    for d in range(NY):
        outs[d][...] = result[:, d * part : (d + 1) * part, :].astype(BF)


def project(place, values, own, other):
    sources, rows, depth = values.shape
    pieces = NX * NC
    n_dim = own[0].shape[0]
    vmem = pl.BlockSpec(memory_space=pltpu.VMEM)
    return pl.pallas_call(
        project_kernel,
        in_specs=[pl.BlockSpec(memory_space=pltpu.SMEM)] + [vmem] * (1 + 2 * NX),
        out_specs=[vmem] * NY,
        out_shape=[jax.ShapeDtypeStruct((sources, rows // NY, pieces * n_dim), BF)] * NY,
        scratch_shapes=[pltpu.VMEM((pieces, n_dim, depth), BF)],
        compiler_params=pltpu.CompilerParams(vmem_limit_bytes=32 << 20),
        name="project",
    )(place, values, *own, *other)


def norm_kernel(place_ref, back_ref, hidden_ref, *refs):
    outs, held_ref = refs[:NY], refs[NY]
    g = place_ref[0]
    rows, width = held_ref.shape
    segment = back_ref.shape[2]
    quarter = width // NY
    squares = jnp.zeros((rows, 1), F32)
    lower = lax.rem(g, 2) == 0
    for z in range(NZ):
        at = slice(z * segment, (z + 1) * segment)
        total = back_ref[z * NX].astype(F32)
        for x in range(1, NX):
            total += back_ref[z * NX + x].astype(F32)
        hidden = hidden_ref[lax.div(g, 2), :, at].astype(F32)
        total += jnp.where(lower, hidden[:rows], hidden[rows:])
        held_ref[:, at] = total
        squares += jnp.sum(total * total, axis=1, keepdims=True)
    scale = lax.rsqrt(squares / width + 1e-06)
    for d in range(NY):
        at = pl.ds(pl.multiple_of(lax.rem(g + d, NY) * quarter, quarter), quarter)
        outs[d][:, :quarter] = held_ref[:, at]
        outs[d][:, quarter:] = jnp.broadcast_to(scale, (rows, LANES))


def norm(place, back, hidden):
    micro, row_local, width = hidden.shape
    rows = micro * row_local // NY
    vmem = pl.BlockSpec(memory_space=pltpu.VMEM)
    return pl.pallas_call(
        norm_kernel,
        in_specs=[pl.BlockSpec(memory_space=pltpu.SMEM), vmem, vmem],
        out_specs=[vmem] * NY,
        out_shape=[jax.ShapeDtypeStruct((rows, width // NY + LANES), F32)] * NY,
        scratch_shapes=[pltpu.VMEM((rows, width), F32)],
        compiler_params=pltpu.CompilerParams(vmem_limit_bytes=8 << 20),
        name="norm",
    )(place, back, hidden)


def scale_kernel(place_ref, gain_ref, *refs):
    pieces, outs = refs[:NY], refs[NY:]
    slim = outs[0].shape[1]
    quarter = NC * slim
    for k in range(NC):
        start = lax.rem(place_ref[1] + k, NC) * slim
        gain = gain_ref[:, pl.ds(pl.multiple_of(place_ref[0] * quarter + start, LANES), slim)]
        at = pl.ds(pl.multiple_of(start, LANES), slim)
        rows = [p[:, at] * p[:, quarter : quarter + 1] * gain for p in pieces]
        outs[k][...] = jnp.concatenate(rows).astype(BF)


def scale_rows(place, gain, pieces):
    rows = NY * pieces[0].shape[0]
    slim = gain.shape[1] // (NY * NC)
    vmem = pl.BlockSpec(memory_space=pltpu.VMEM)
    return pl.pallas_call(
        scale_kernel,
        in_specs=[pl.BlockSpec(memory_space=pltpu.SMEM)] + [vmem] * (1 + NY),
        out_specs=[vmem] * NC,
        out_shape=[jax.ShapeDtypeStruct((rows, slim), BF)] * NC,
        compiler_params=pltpu.CompilerParams(vmem_limit_bytes=8 << 20),
        name="scale_rows",
    )(place, gain, *pieces)


def join_kernel(place_ref, *refs):
    pieces, out_ref = refs[:NY], refs[NY]
    quarter = pieces[0].shape[1]
    micro, rows = out_ref.shape[:2]
    for d in range(NY):
        at = lax.rem(place_ref[0] - d + NY, NY) * quarter
        for m in range(micro):
            out_ref[m, :, pl.ds(pl.multiple_of(at, quarter), quarter)] = pieces[d][
                m * rows : (m + 1) * rows, :
            ]


def join(place, pieces, shape):
    vmem = pl.BlockSpec(memory_space=pltpu.VMEM)
    return pl.pallas_call(
        join_kernel,
        in_specs=[pl.BlockSpec(memory_space=pltpu.SMEM)] + [vmem] * NY,
        out_specs=vmem,
        out_shape=jax.ShapeDtypeStruct(shape, BF),
        compiler_params=pltpu.CompilerParams(vmem_limit_bytes=8 << 20),
        name="join",
    )(place, *pieces)


def gate_up_kernel(place_ref, x_ref, w_ref, *refs):
    del place_ref
    refs[-1][...] = jnp.dot(x_ref[...], w_ref[...], preferred_element_type=F32)


def gate_up_last_kernel(units, place_ref, x_ref, w_ref, sum_ref, *refs):
    outs, acc_ref = refs[:NY], refs[NY]
    acc_ref[...] = sum_ref[...] + jnp.dot(x_ref[...], w_ref[...], preferred_element_type=F32)
    for d in range(NY):
        to = lax.rem(place_ref[0] + d, NY)
        for k in range(2):
            start = pl.multiple_of((k * NY + to) * units, units)
            outs[d][:, k * units : (k + 1) * units] = acc_ref[:, pl.ds(start, units)].astype(BF)


def gate_up_dot(place, x, w, before=None):
    count, depth = x.shape
    width = w.shape[1]
    units = width // (2 * NY)
    in_specs = [
        pl.BlockSpec((count, depth), lambda i, p: (0, 0)),
        pl.BlockSpec((depth, width), lambda i, p: (0, 0)),
    ]
    if before is None:
        body, operands, scratch = gate_up_kernel, (x, w), []
        out_specs = pl.BlockSpec((count, width), lambda i, p: (0, 0))
        out_shape = jax.ShapeDtypeStruct((count, width), F32)
    else:
        body, operands = functools.partial(gate_up_last_kernel, units), (x, w, before)
        scratch = [pltpu.VMEM((count, width), F32)]
        in_specs.append(pl.BlockSpec((count, width), lambda i, p: (0, 0)))
        out_specs = [pl.BlockSpec((count, 2 * units), lambda i, p: (0, 0))] * NY
        out_shape = [jax.ShapeDtypeStruct((count, 2 * units), BF)] * NY
    return pl.pallas_call(
        body,
        grid_spec=pltpu.PrefetchScalarGridSpec(
            num_scalar_prefetch=1,
            grid=(1,),
            in_specs=in_specs,
            out_specs=out_specs,
            scratch_shapes=scratch,
        ),
        out_shape=out_shape,
        compiler_params=pltpu.CompilerParams(vmem_limit_bytes=32 << 20),
        cost_estimate=pl.CostEstimate(
            flops=2 * count * depth * width, bytes_accessed=6 << 20, transcendentals=0
        ),
        name="gate_up",
    )(place, *operands)


def down_kernel(place_ref, *refs):
    del place_ref
    acts, downs, out_ref = refs[:NY], refs[NY : 2 * NY], refs[2 * NY]
    act = jnp.concatenate([a[...] for a in acts], axis=1)
    down = jnp.concatenate([w[...] for w in downs], axis=0)
    out_ref[...] = jnp.dot(act, down, preferred_element_type=F32).astype(out_ref.dtype)


def down_dot(place, half, acts, downs, dtype):
    count, units = acts[0].shape
    width = downs[0].shape[1] // NC
    return pl.pallas_call(
        down_kernel,
        grid_spec=pltpu.PrefetchScalarGridSpec(
            num_scalar_prefetch=1,
            grid=(1,),
            in_specs=[pl.BlockSpec((count, units), lambda i, p: (0, 0))] * NY
            + [pl.BlockSpec((units, width), lambda i, p: (0, lax.rem(p[1] + half, NC)))] * NY,
            out_specs=pl.BlockSpec((count, width), lambda i, p: (0, 0)),
        ),
        out_shape=jax.ShapeDtypeStruct((count, width), dtype),
        compiler_params=pltpu.CompilerParams(vmem_limit_bytes=32 << 20),
        cost_estimate=pl.CostEstimate(
            flops=2 * count * units * NY * width, bytes_accessed=3 << 20, transcendentals=0
        ),
        name="down",
    )(place, *acts, *downs)


def swap_core(a):
    return lax.ppermute(a, "c", [(0, 1), (1, 0)])


def shift_y(a, d):
    return lax.ppermute(a, "y", [(i, (i + d) % NY) for i in range(NY)])


def shift_x(a, d):
    return lax.ppermute(a, "x", [(i, (i + d) % NX) for i in range(NX)])


def lane_part(a, index, size):
    return lax.dynamic_slice_in_dim(a, index * size, size, 1)


def gather_y(a):
    return [a] + [shift_y(a, d) for d in range(1, NY)]


def absolute(items, g):
    back = [items[(-j) % NY] for j in range(NY)]
    return lax.dynamic_slice_in_dim(jnp.stack(back + back[: NY - 1]), (NY - g) % NY, NY, 0)


def routing(ids, gates, expert_count, capacity, g, first):
    blocks, rows, top = ids.shape
    hot = ids[..., None] == jnp.arange(expert_count, dtype=jnp.int32)
    chosen = jnp.any(hot, axis=2)
    weight = jnp.sum(jnp.where(hot, gates[..., None], 0.0), axis=2)
    counts = chosen.astype(jnp.int32)
    place = jnp.cumsum(counts, axis=1) - counts
    block = jnp.broadcast_to(jnp.arange(blocks, dtype=jnp.int32)[:, None, None], place.shape)
    slot = jnp.where(chosen, block * capacity + place, -1).reshape(blocks * rows, expert_count)
    slots = jnp.arange(blocks * capacity, dtype=jnp.int32)[None, :, None]
    flat = (expert_count * blocks * capacity, blocks * rows)
    weight = weight.reshape(blocks * rows, expert_count).T[:, None, :]
    weights = jnp.where(slot.T[:, None, :] == slots, weight, 0.0).reshape(flat)
    turned = slot.reshape(NC, NY, -1)
    turned = jnp.where(first, turned, turned[::-1])
    turned = jnp.stack(
        [lax.dynamic_index_in_dim(turned, (g - d) % NY, 1, keepdims=False) for d in range(NY)],
        axis=1,
    )
    turned = turned.reshape(blocks * rows, expert_count)
    pick = (turned.T[:, None, :] == slots).reshape(flat).astype(BF)
    return pick, weights


def local(
    hidden_in,
    queries,
    latent_cache,
    cache_lengths,
    expert_ids,
    gate_values,
    norm_gain,
    value_up,
    out_proj,
    gate_up,
    down_proj,
):
    g, c = lax.axis_index("y"), lax.axis_index("c")
    first = c == 0
    micro, row_local, width = hidden_in.shape
    rows = micro * row_local
    part = rows // NY
    quarter, slim = width // NY, width // (NY * NC)
    k_dim, n_dim = out_proj.shape
    k_slice = k_dim // NX
    expert_count = NZ * NX
    top = expert_ids.shape[2]
    capacity = min(row_local, 4)

    x = lax.axis_index("x")
    place = jnp.stack([g, c, x]).astype(jnp.int32)
    wt = out_proj.T
    w_own = [lane_part(wt, x, k_slice)]
    w_own += [shift_x(lane_part(wt, (x + d) % NX, k_slice), d) for d in range(1, NX)]

    ids_o, gates_o = swap_core(expert_ids), swap_core(gate_values)
    ids = jnp.concatenate(
        [jnp.where(first, expert_ids, ids_o), jnp.where(first, ids_o, expert_ids)]
    )
    gates = jnp.concatenate(
        [jnp.where(first, gate_values, gates_o), jnp.where(first, gates_o, gate_values)]
    )
    pick, weights = routing(ids, gates, expert_count, capacity, g, first)

    send = attend(
        place,
        cache_lengths,
        queries.reshape((rows,) + queries.shape[2:]),
        latent_cache.transpose(0, 1, 3, 2).reshape((rows,) + latent_cache.shape[:1:-1]),
        value_up,
    )
    w_other = [swap_core(w) for w in w_own]
    down = [None] * NY

    def send_down(d, source):
        return shift_y(lane_part(source, (g + d) % NY, quarter), d)

    down_in, send = lax.optimization_barrier((down_proj[0], send))
    down[2] = send_down(2, down_in)
    got = lax.all_to_all(send, ("z", "x"), 0, 0, tiled=True)
    parts = project(jnp.stack([x, c]).astype(jnp.int32), got, w_own, w_other)
    parts = [parts[0]] + [shift_y(parts[d], d) for d in range(1, NY)]
    spread = sum(p.astype(F32) for p in parts).astype(BF)
    back = lax.all_to_all(
        spread, ("z", "x"), 0, 0, tiled=True
    )
    back, down[2] = lax.optimization_barrier((back, down[2]))
    pieces = norm(place, back, hidden_in)
    pieces = [pieces[0]] + [shift_y(pieces[d], d) for d in range(1, NY)]
    keep, give = scale_rows(place, norm_gain[None, :], pieces)
    took = swap_core(give)
    chip_rows = jnp.concatenate([keep, took])
    outgoing = jnp.dot(pick, chip_rows, preferred_element_type=F32).astype(BF)
    slots = NC * micro * capacity
    down_in, gate_up, outgoing = lax.optimization_barrier((down_proj[0], gate_up, outgoing))
    gu = [
        lax.dynamic_slice_in_dim(gate_up[0], (c + k) % NC * slim, slim, 0).reshape(slim, -1)
        for k in range(NC)
    ]
    down[0] = lane_part(down_in, g, quarter)
    down[1], down[3] = send_down(1, down_in), send_down(3, down_in)
    received = lax.all_to_all(
        outgoing.reshape(expert_count, slots, slim), ("z", "x"), 0, 0, tiled=True
    ).reshape(expert_count * slots, slim)
    received, gu, weights, down = lax.optimization_barrier((received, gu, weights, down))
    other = swap_core(received)
    own_sum = gate_up_dot(place, received, gu[0])
    parts = gate_up_dot(place, other, gu[1], own_sum)
    parts = [parts[0]] + [shift_y(parts[d], d) for d in range(1, NY)]
    total = sum(p.astype(F32) for p in parts)
    units = total.shape[1] // 2
    act = (jax.nn.silu(total[:, :units]) * total[:, units:]).astype(BF)
    acts = gather_y(act)
    give_r = down_dot(place, 1, acts, down, BF)
    keep_r = down_dot(place, 0, acts, down, F32)
    whole = (keep_r + swap_core(give_r).astype(F32)).astype(BF)
    returned = lax.all_to_all(
        whole.reshape(expert_count, slots, slim), ("z", "x"), 0, 0, tiled=True
    ).reshape(expert_count * slots, slim)
    high = weights.astype(BF)
    low = (weights - high.astype(F32)).astype(BF)
    both = lax.dot_general(
        jnp.concatenate([high, low], axis=1),
        returned,
        (((0,), (0,)), ((), ())),
        preferred_element_type=F32,
    )
    mix = both[: NC * rows] + both[NC * rows :]
    mix_keep = jnp.where(first, mix[:rows], mix[rows:])
    mix_give = jnp.where(first, mix[rows:], mix[:rows])
    mix_took = swap_core(mix_give)
    mix_q = jnp.concatenate(
        [jnp.where(first, mix_keep, mix_took), jnp.where(first, mix_took, mix_keep)], axis=1
    )
    residual_q = absolute([p[:, :quarter] for p in pieces], g).reshape(rows, quarter)
    out_q = (residual_q + mix_q).astype(BF)
    return join(place, gather_y(out_q), hidden_in.shape)


def solution(mesh):
    fine = Mesh(mesh.devices.reshape(NY, NZ, NX, NC), ("y", "z", "x", "c"))
    ep = ("z", "x", "c")
    return jax.shard_map(
        local,
        mesh=fine,
        in_specs=(
            P(None, ep, None),
            P(None, ep, "y", None),
            P(None, ep, None, None),
            P(None, ep),
            P(None, ep, None),
            P(None, ep, None),
            P(),
            P("y", None, None),
            P("y", ep),
            P(ep, "y", None, None),
            P(ep, "y", None),
        ),
        out_specs=P(None, ep, None),
        check_vma=False,
    )
```

```python
import functools
import math

import jax
import jax.numpy as jnp
from jax import lax
from jax.experimental import pallas as pl
from jax.experimental.pallas import tpu as pltpu
from jax.sharding import Mesh
from jax.sharding import PartitionSpec as P

ROPE = 64
NOPE = 128
NY, NZ, NX, NC = 4, 8, 4, 2
BF = jnp.bfloat16
F32 = jnp.float32
LANES = 128


def attend_kernel(rows, heads, latent, place_ref, length_ref, q_ref, cache_ref, up_ref, out_ref, held):
    step = pl.program_id(0)
    scale = 1.0 / math.sqrt(ROPE + NOPE)
    base = lax.rem(step + place_ref[0], NY) * rows
    micro, base = lax.div(base, length_ref.shape[1]), lax.rem(base, length_ref.shape[1])
    for r in range(rows):
        cache = cache_ref[r]
        scores = jnp.dot(q_ref[r], cache, preferred_element_type=F32) * scale
        at = lax.broadcasted_iota(jnp.int32, scores.shape, 1)
        in_range = at < length_ref[micro, base + r]
        masked = jnp.where(in_range, scores, -1e30)
        peak = jnp.max(masked, axis=1, keepdims=True)
        exponent = jnp.where(in_range, jnp.exp(masked - peak), 0.0)
        weights = (exponent / jnp.sum(exponent, axis=1, keepdims=True)).astype(BF)
        held[step * rows + r] = lax.dot_general(
            weights, cache[:latent], (((1,), (1,)), ((), ())), preferred_element_type=F32
        )

    @pl.when(step == NY - 1)
    def _():
        group, vdim = heads // NX, up_ref.shape[2]
        for h in range(heads):
            value = jnp.dot(
                held[:, h, :].astype(BF), up_ref[h], preferred_element_type=F32
            ).astype(BF)
            lanes = slice(h % group * vdim, (h % group + 1) * vdim)
            for z in range(NZ):
                out_ref[z * NX + h // group, :, lanes] = value


def attend(place, lengths, queries, cache_t, value_up):
    all_rows, heads, key = queries.shape
    rows = all_rows // NY
    latent, vdim = value_up.shape[1:]
    length = cache_t.shape[2]
    shape = (NZ * NX, all_rows, heads * vdim // NX)
    turn = lambda i, place, lengths: (lax.rem(i + place[0], NY), 0, 0)
    return pl.pallas_call(
        functools.partial(attend_kernel, rows, heads, latent),
        grid_spec=pltpu.PrefetchScalarGridSpec(
            num_scalar_prefetch=2,
            grid=(NY,),
            in_specs=[
                pl.BlockSpec((rows, heads, key), turn),
                pl.BlockSpec((rows, key, length), turn),
                pl.BlockSpec(value_up.shape, lambda i, place, lengths: (0, 0, 0)),
            ],
            out_specs=pl.BlockSpec(shape, lambda i, place, lengths: (0, 0, 0)),
            scratch_shapes=[pltpu.VMEM((all_rows, heads, latent), F32)],
        ),
        out_shape=jax.ShapeDtypeStruct(shape, BF),
        compiler_params=pltpu.CompilerParams(vmem_limit_bytes=60 << 20),
        name="attend",
    )(place, lengths, queries, cache_t, value_up)


def project_kernel(place_ref, h_ref, *refs):
    own, other, outs, w_ref = refs[:NX], refs[NX : 2 * NX], refs[2 * NX : -1], refs[-1]
    sources, rows, depth = h_ref.shape
    for core in range(NC):

        @pl.when(place_ref[1] == core)
        def _():
            for x in range(NX):

                @pl.when(place_ref[0] == x)
                def _():
                    for dx in range(NX):
                        at = NC * ((x - dx) % NX)
                        w_ref[at + core] = own[dx][...]
                        w_ref[at + 1 - core] = other[dx][...]

    result = lax.dot_general(
        h_ref[...].reshape(sources * rows, depth),
        w_ref[...].reshape(-1, depth),
        (((1,), (1,)), ((), ())),
        preferred_element_type=F32,
    ).reshape(sources, rows, -1)
    part = rows // NY
    for d in range(NY):
        outs[d][...] = result[:, d * part : (d + 1) * part, :].astype(BF)


def project(place, values, own, other):
    sources, rows, depth = values.shape
    pieces = NX * NC
    n_dim = own[0].shape[0]
    vmem = pl.BlockSpec(memory_space=pltpu.VMEM)
    return pl.pallas_call(
        project_kernel,
        in_specs=[pl.BlockSpec(memory_space=pltpu.SMEM)] + [vmem] * (1 + 2 * NX),
        out_specs=[vmem] * NY,
        out_shape=[jax.ShapeDtypeStruct((sources, rows // NY, pieces * n_dim), BF)] * NY,
        scratch_shapes=[pltpu.VMEM((pieces, n_dim, depth), BF)],
        compiler_params=pltpu.CompilerParams(vmem_limit_bytes=32 << 20),
        name="project",
    )(place, values, *own, *other)


def norm_kernel(place_ref, back_ref, hidden_ref, *refs):
    outs, held_ref = refs[:NY], refs[NY]
    g = place_ref[0]
    rows, width = held_ref.shape
    segment = back_ref.shape[2]
    quarter = width // NY
    squares = jnp.zeros((rows, 1), F32)
    lower = lax.rem(g, 2) == 0
    for z in range(NZ):
        at = slice(z * segment, (z + 1) * segment)
        total = back_ref[z * NX].astype(F32)
        for x in range(1, NX):
            total += back_ref[z * NX + x].astype(F32)
        hidden = hidden_ref[lax.div(g, 2), :, at].astype(F32)
        total += jnp.where(lower, hidden[:rows], hidden[rows:])
        held_ref[:, at] = total
        squares += jnp.sum(total * total, axis=1, keepdims=True)
    scale = lax.rsqrt(squares / width + 1e-06)
    for d in range(NY):
        at = pl.ds(pl.multiple_of(lax.rem(g + d, NY) * quarter, quarter), quarter)
        outs[d][:, :quarter] = held_ref[:, at]
        outs[d][:, quarter:] = jnp.broadcast_to(scale, (rows, LANES))


def norm(place, back, hidden):
    micro, row_local, width = hidden.shape
    rows = micro * row_local // NY
    vmem = pl.BlockSpec(memory_space=pltpu.VMEM)
    return pl.pallas_call(
        norm_kernel,
        in_specs=[pl.BlockSpec(memory_space=pltpu.SMEM), vmem, vmem],
        out_specs=[vmem] * NY,
        out_shape=[jax.ShapeDtypeStruct((rows, width // NY + LANES), F32)] * NY,
        scratch_shapes=[pltpu.VMEM((rows, width), F32)],
        compiler_params=pltpu.CompilerParams(vmem_limit_bytes=8 << 20),
        name="norm",
    )(place, back, hidden)


def scale_kernel(place_ref, gain_ref, *refs):
    pieces, outs = refs[:NY], refs[NY:]
    slim = outs[0].shape[1]
    quarter = NC * slim
    for k in range(NC):
        start = lax.rem(place_ref[1] + k, NC) * slim
        gain = gain_ref[:, pl.ds(pl.multiple_of(place_ref[0] * quarter + start, LANES), slim)]
        at = pl.ds(pl.multiple_of(start, LANES), slim)
        rows = [p[:, at] * p[:, quarter : quarter + 1] * gain for p in pieces]
        outs[k][...] = jnp.concatenate(rows).astype(BF)


def scale_rows(place, gain, pieces):
    rows = NY * pieces[0].shape[0]
    slim = gain.shape[1] // (NY * NC)
    vmem = pl.BlockSpec(memory_space=pltpu.VMEM)
    return pl.pallas_call(
        scale_kernel,
        in_specs=[pl.BlockSpec(memory_space=pltpu.SMEM)] + [vmem] * (1 + NY),
        out_specs=[vmem] * NC,
        out_shape=[jax.ShapeDtypeStruct((rows, slim), BF)] * NC,
        compiler_params=pltpu.CompilerParams(vmem_limit_bytes=8 << 20),
        name="scale_rows",
    )(place, gain, *pieces)


def join_kernel(place_ref, *refs):
    pieces, out_ref = refs[:NY], refs[NY]
    quarter = pieces[0].shape[1]
    micro, rows = out_ref.shape[:2]
    for d in range(NY):
        at = lax.rem(place_ref[0] - d + NY, NY) * quarter
        for m in range(micro):
            out_ref[m, :, pl.ds(pl.multiple_of(at, quarter), quarter)] = pieces[d][
                m * rows : (m + 1) * rows, :
            ]


def join(place, pieces, shape):
    vmem = pl.BlockSpec(memory_space=pltpu.VMEM)
    return pl.pallas_call(
        join_kernel,
        in_specs=[pl.BlockSpec(memory_space=pltpu.SMEM)] + [vmem] * NY,
        out_specs=vmem,
        out_shape=jax.ShapeDtypeStruct(shape, BF),
        compiler_params=pltpu.CompilerParams(vmem_limit_bytes=8 << 20),
        name="join",
    )(place, *pieces)


def gate_up_kernel(place_ref, x_ref, w_ref, *refs):
    del place_ref
    refs[-1][...] = jnp.dot(x_ref[...], w_ref[...], preferred_element_type=F32)


def gate_up_last_kernel(units, place_ref, x_ref, w_ref, sum_ref, *refs):
    outs, acc_ref = refs[:NY], refs[NY]
    acc_ref[...] = sum_ref[...] + jnp.dot(x_ref[...], w_ref[...], preferred_element_type=F32)
    for d in range(NY):
        to = lax.rem(place_ref[0] + d, NY)
        for k in range(2):
            start = pl.multiple_of((k * NY + to) * units, units)
            outs[d][:, k * units : (k + 1) * units] = acc_ref[:, pl.ds(start, units)].astype(BF)


def gate_up_dot(place, x, w, before=None):
    count, depth = x.shape
    width = w.shape[1]
    units = width // (2 * NY)
    in_specs = [
        pl.BlockSpec((count, depth), lambda i, p: (0, 0)),
        pl.BlockSpec((depth, width), lambda i, p: (0, 0)),
    ]
    if before is None:
        body, operands, scratch = gate_up_kernel, (x, w), []
        out_specs = pl.BlockSpec((count, width), lambda i, p: (0, 0))
        out_shape = jax.ShapeDtypeStruct((count, width), F32)
    else:
        body, operands = functools.partial(gate_up_last_kernel, units), (x, w, before)
        scratch = [pltpu.VMEM((count, width), F32)]
        in_specs.append(pl.BlockSpec((count, width), lambda i, p: (0, 0)))
        out_specs = [pl.BlockSpec((count, 2 * units), lambda i, p: (0, 0))] * NY
        out_shape = [jax.ShapeDtypeStruct((count, 2 * units), BF)] * NY
    return pl.pallas_call(
        body,
        grid_spec=pltpu.PrefetchScalarGridSpec(
            num_scalar_prefetch=1,
            grid=(1,),
            in_specs=in_specs,
            out_specs=out_specs,
            scratch_shapes=scratch,
        ),
        out_shape=out_shape,
        compiler_params=pltpu.CompilerParams(vmem_limit_bytes=32 << 20),
        cost_estimate=pl.CostEstimate(
            flops=2 * count * depth * width, bytes_accessed=6 << 20, transcendentals=0
        ),
        name="gate_up",
    )(place, *operands)


def down_kernel(place_ref, *refs):
    del place_ref
    acts, downs, out_ref = refs[:NY], refs[NY : 2 * NY], refs[2 * NY]
    act = jnp.concatenate([a[...] for a in acts], axis=1)
    down = jnp.concatenate([w[...] for w in downs], axis=0)
    out_ref[...] = jnp.dot(act, down, preferred_element_type=F32).astype(out_ref.dtype)


def down_dot(place, half, acts, downs, dtype):
    count, units = acts[0].shape
    width = downs[0].shape[1] // NC
    return pl.pallas_call(
        down_kernel,
        grid_spec=pltpu.PrefetchScalarGridSpec(
            num_scalar_prefetch=1,
            grid=(1,),
            in_specs=[pl.BlockSpec((count, units), lambda i, p: (0, 0))] * NY
            + [pl.BlockSpec((units, width), lambda i, p: (0, lax.rem(p[1] + half, NC)))] * NY,
            out_specs=pl.BlockSpec((count, width), lambda i, p: (0, 0)),
        ),
        out_shape=jax.ShapeDtypeStruct((count, width), dtype),
        compiler_params=pltpu.CompilerParams(vmem_limit_bytes=32 << 20),
        cost_estimate=pl.CostEstimate(
            flops=2 * count * units * NY * width, bytes_accessed=3 << 20, transcendentals=0
        ),
        name="down",
    )(place, *acts, *downs)


def swap_core(a):
    return lax.ppermute(a, "c", [(0, 1), (1, 0)])


def shift_y(a, d):
    return lax.ppermute(a, "y", [(i, (i + d) % NY) for i in range(NY)])


def shift_x(a, d):
    return lax.ppermute(a, "x", [(i, (i + d) % NX) for i in range(NX)])


def lane_part(a, index, size):
    return lax.dynamic_slice_in_dim(a, index * size, size, 1)


def gather_y(a):
    return [a] + [shift_y(a, d) for d in range(1, NY)]


def absolute(items, g):
    back = [items[(-j) % NY] for j in range(NY)]
    return lax.dynamic_slice_in_dim(jnp.stack(back + back[: NY - 1]), (NY - g) % NY, NY, 0)


def routing(ids, gates, expert_count, capacity, g, first):
    blocks, rows, top = ids.shape
    hot = ids[..., None] == jnp.arange(expert_count, dtype=jnp.int32)
    chosen = jnp.any(hot, axis=2)
    weight = jnp.sum(jnp.where(hot, gates[..., None], 0.0), axis=2)
    counts = chosen.astype(jnp.int32)
    place = jnp.cumsum(counts, axis=1) - counts
    block = jnp.broadcast_to(jnp.arange(blocks, dtype=jnp.int32)[:, None, None], place.shape)
    slot = jnp.where(chosen, block * capacity + place, -1).reshape(blocks * rows, expert_count)
    slots = jnp.arange(blocks * capacity, dtype=jnp.int32)[None, :, None]
    flat = (expert_count * blocks * capacity, blocks * rows)
    weight = weight.reshape(blocks * rows, expert_count).T[:, None, :]
    weights = jnp.where(slot.T[:, None, :] == slots, weight, 0.0).reshape(flat)
    turned = slot.reshape(NC, NY, -1)
    turned = jnp.where(first, turned, turned[::-1])
    turned = jnp.stack(
        [lax.dynamic_index_in_dim(turned, (g - d) % NY, 1, keepdims=False) for d in range(NY)],
        axis=1,
    )
    turned = turned.reshape(blocks * rows, expert_count)
    pick = (turned.T[:, None, :] == slots).reshape(flat).astype(BF)
    return pick, weights


def local(
    hidden_in,
    queries,
    latent_cache,
    cache_lengths,
    expert_ids,
    gate_values,
    norm_gain,
    value_up,
    out_proj,
    gate_up,
    down_proj,
):
    g, c = lax.axis_index("y"), lax.axis_index("c")
    first = c == 0
    micro, row_local, width = hidden_in.shape
    rows = micro * row_local
    part = rows // NY
    quarter, slim = width // NY, width // (NY * NC)
    k_dim, n_dim = out_proj.shape
    k_slice = k_dim // NX
    expert_count = NZ * NX
    top = expert_ids.shape[2]
    capacity = min(row_local, 4)

    x = lax.axis_index("x")
    place = jnp.stack([g, c, x]).astype(jnp.int32)
    wt = out_proj.T
    w_own = [lane_part(wt, x, k_slice)]
    w_own += [shift_x(lane_part(wt, (x + d) % NX, k_slice), d) for d in range(1, NX)]

    ids_o, gates_o = swap_core(expert_ids), swap_core(gate_values)
    ids = jnp.concatenate(
        [jnp.where(first, expert_ids, ids_o), jnp.where(first, ids_o, expert_ids)]
    )
    gates = jnp.concatenate(
        [jnp.where(first, gate_values, gates_o), jnp.where(first, gates_o, gate_values)]
    )
    pick, weights = routing(ids, gates, expert_count, capacity, g, first)

    send = attend(
        place,
        cache_lengths,
        queries.reshape((rows,) + queries.shape[2:]),
        latent_cache.transpose(0, 1, 3, 2).reshape((rows,) + latent_cache.shape[:1:-1]),
        value_up,
    )
    w_other = [swap_core(w) for w in w_own]
    down = [None] * NY

    def send_down(d, source):
        return shift_y(lane_part(source, (g + d) % NY, quarter), d)

    down_in, send = lax.optimization_barrier((down_proj[0], send))
    down[1] = send_down(1, down_in)
    got = lax.all_to_all(send, ("z", "x"), 0, 0, tiled=True)
    parts = project(jnp.stack([x, c]).astype(jnp.int32), got, w_own, w_other)
    parts = [parts[0]] + [shift_y(parts[d], d) for d in range(1, NY)]
    spread = sum(p.astype(F32) for p in parts).astype(BF)
    back = lax.all_to_all(
        spread, ("z", "x"), 0, 0, tiled=True
    )
    back, down[1] = lax.optimization_barrier((back, down[1]))
    pieces = norm(place, back, hidden_in)
    pieces = [pieces[0]] + [shift_y(pieces[d], d) for d in range(1, NY)]
    keep, give = scale_rows(place, norm_gain[None, :], pieces)
    took = swap_core(give)
    chip_rows = jnp.concatenate([keep, took])
    outgoing = jnp.dot(pick, chip_rows, preferred_element_type=F32).astype(BF)
    slots = NC * micro * capacity
    down_in, gate_up, outgoing = lax.optimization_barrier((down_proj[0], gate_up, outgoing))
    gu = [
        lax.dynamic_slice_in_dim(gate_up[0], (c + k) % NC * slim, slim, 0).reshape(slim, -1)
        for k in range(NC)
    ]
    down[0] = lane_part(down_in, g, quarter)
    down[2], down[3] = send_down(2, down_in), send_down(3, down_in)
    received = lax.all_to_all(
        outgoing.reshape(expert_count, slots, slim), ("z", "x"), 0, 0, tiled=True
    ).reshape(expert_count * slots, slim)
    received, gu, weights, down = lax.optimization_barrier((received, gu, weights, down))
    other = swap_core(received)
    own_sum = gate_up_dot(place, received, gu[0])
    parts = gate_up_dot(place, other, gu[1], own_sum)
    parts = [parts[0]] + [shift_y(parts[d], d) for d in range(1, NY)]
    total = sum(p.astype(F32) for p in parts)
    units = total.shape[1] // 2
    act = (jax.nn.silu(total[:, :units]) * total[:, units:]).astype(BF)
    acts = gather_y(act)
    give_r = down_dot(place, 1, acts, down, BF)
    keep_r = down_dot(place, 0, acts, down, F32)
    whole = (keep_r + swap_core(give_r).astype(F32)).astype(BF)
    returned = lax.all_to_all(
        whole.reshape(expert_count, slots, slim), ("z", "x"), 0, 0, tiled=True
    ).reshape(expert_count * slots, slim)
    high = weights.astype(BF)
    low = (weights - high.astype(F32)).astype(BF)
    both = lax.dot_general(
        jnp.concatenate([high, low], axis=1),
        returned,
        (((0,), (0,)), ((), ())),
        preferred_element_type=F32,
    )
    mix = both[: NC * rows] + both[NC * rows :]
    mix_keep = jnp.where(first, mix[:rows], mix[rows:])
    mix_give = jnp.where(first, mix[rows:], mix[:rows])
    mix_took = swap_core(mix_give)
    mix_q = jnp.concatenate(
        [jnp.where(first, mix_keep, mix_took), jnp.where(first, mix_took, mix_keep)], axis=1
    )
    residual_q = absolute([p[:, :quarter] for p in pieces], g).reshape(rows, quarter)
    out_q = (residual_q + mix_q).astype(BF)
    return join(place, gather_y(out_q), hidden_in.shape)


def solution(mesh):
    fine = Mesh(mesh.devices.reshape(NY, NZ, NX, NC), ("y", "z", "x", "c"))
    ep = ("z", "x", "c")
    return jax.shard_map(
        local,
        mesh=fine,
        in_specs=(
            P(None, ep, None),
            P(None, ep, "y", None),
            P(None, ep, None, None),
            P(None, ep),
            P(None, ep, None),
            P(None, ep, None),
            P(),
            P("y", None, None),
            P("y", ep),
            P(ep, "y", None, None),
            P(ep, "y", None),
        ),
        out_specs=P(None, ep, None),
        check_vma=False,
    )
```
